32 devices in a mesh: dp: 8 (over z, x), section: 4 (over y, core).
Axes of the slice: x: 2, y: 2, z: 4, core: 2. Of those that a mesh axis runs over, the one named last changes fastest.
Arguments:
- stream: bfloat16 [24, 512, 768], P('dp'), may hold values from -6 to 6
- cotangent: bfloat16 [24, 512, 768], P('dp'), may hold values from -6 to 6
- segments: int32 [24, 512], P('dp'), may hold values from 0 to 3, never falling along the last dimension, each value on 1 to 256 neighbouring positions
- word_boxes: int32 [4, 24, 512], P(None, 'dp'), may hold values from 0 to 1023
- valid_mask: int32 [24, 512], P('dp'), may hold values 0 or 1
- w_qkv: bfloat16 [2, 768, 2304], replicated, may hold values from -0.21875 to 0.21875
- qv_bias: bfloat16 [2, 2, 768], replicated, may hold values from -3 to 3
- w_out: bfloat16 [2, 768, 768], replicated, may hold values from -1.75 to 1.75
- out_bias: bfloat16 [2, 768], replicated, may hold values from -2 to 2
- rel_proj: bfloat16 [2, 12, 64, 128], replicated, may hold values from -0.75 to 0.75
- ln_scale: bfloat16 [2, 2, 768], replicated, may hold values from 0.5 to 1.5
- ln_shift: bfloat16 [2, 2, 768], replicated, may hold values from -2 to 2
- ffn_in: bfloat16 [2, 768, 3072], replicated, may hold values from -0.21875 to 0.21875
- ffn_in_bias: bfloat16 [2, 3072], replicated, may hold values from -2 to 2
- ffn_out: bfloat16 [2, 3072, 768], replicated, may hold values from -0.109375 to 0.109375
- ffn_out_bias: bfloat16 [2, 768], replicated, may hold values from -2 to 2
Outputs:
- section_outputs: bfloat16 [4, 24, 512, 768], P('section', 'dp')
- section_input_grads: float32 [4, 24, 512, 768], P('section', 'dp')
- grad_w_qkv: float32 [2, 768, 2304], P(None, 'dp')
- grad_qv_bias: float32 [2, 2, 768], P(None, None, 'dp')
- grad_w_out: float32 [2, 768, 768], P(None, 'dp')
- grad_out_bias: float32 [2, 768], P(None, 'dp')
- grad_rel_proj: float32 [2, 12, 64, 128], P(None, None, None, 'dp')
- grad_ln_scale: float32 [2, 2, 768], P(None, None, 'dp')
- grad_ln_shift: float32 [2, 2, 768], P(None, None, 'dp')
- grad_ffn_in: float32 [2, 768, 3072], P(None, 'dp')
- grad_ffn_in_bias: float32 [2, 3072], P(None, 'dp')
- grad_ffn_out: float32 [2, 3072, 768], P(None, 'dp')
- grad_ffn_out_bias: float32 [2, 768], P(None, 'dp')
- root_mean_squares: float32 [4, 24, 2], P('section', 'dp')
The draws below stay inside these ranges and needn't reach their ends.
All inputs are finite; a program needn't handle non-finite values. No bound on the sum of `valid_mask` on one device may be relied on, other than what follows from the above.
Results may differ from the reference program's by a relative error of at most 0.035.
Values may be sent and summed in bfloat16 or wider, within the bound.
No kernel may reach another device: no remote copies, remote signals or barrier semaphores. Data moves between devices by JAX's collectives and lax.ppermute only.
A program may use at most 768 MiB of HBM per device.

```python
import math
import jax
import jax.numpy as jnp
import numpy as np
from jax import lax

D = 768
H = 12
HS = 64
FF = 3072
REL = 128
LEN = 512
PAGES = 4
LAYERS = 2
ROWS = 24
N_SECTION = 4


def with_ends(drawn, key, smallest, largest):
    shape = drawn.shape
    index_at = [jax.random.randint(jax.random.fold_in(key, axis), (), 0, shape[axis]) for axis in range(len(shape))]
    drawn = drawn.at[tuple(index_at)].set(smallest)
    longest = shape.index(max(shape))
    index_at[longest] = (index_at[longest] + 1) % shape[longest]
    return drawn.at[tuple(index_at)].set(largest)


def shard_levels(key, extent, cuts, least, top_value):
    gain = 1.0
    for axis_at, parts in cuts:
        steps = jax.random.uniform(jax.random.fold_in(jax.random.fold_in(key, 6), axis_at), (parts,), jnp.float32, least / len(cuts), top_value / len(cuts))
        gain = gain * jnp.repeat(jnp.exp(steps), extent[axis_at] // parts).reshape((-1,) + (1,) * (len(extent) - 1 - axis_at))
    return gain


def length_profile(number_of, total, limit, skew):
    weights = [(1 << 20) // math.isqrt(rank ** skew) + 1 for rank in range(2, number_of + 1)]
    surplus, holding = total - limit - (number_of - 1), [1] * (number_of - 1)
    while surplus > 0:
        candidates = [i for i in range(number_of - 1) if holding[i] < limit]
        whole, remaining = sum([weights[i] for i in candidates]), surplus
        for i in candidates:
            extra = min(limit - holding[i], max(1, remaining * weights[i] // whole), surplus)
            holding[i] = holding[i] + extra
            surplus = surplus - extra
    return np.array([limit] + holding)


def uneven_parts(stream_key, amount, total, reach, lean):
    if amount == 2:
        one = jax.random.randint(stream_key, (), max(1, total - reach), min(reach, total - 1) + 1)
        return jnp.stack([one, total - one])
    lengths = jnp.asarray(length_profile(amount, total, reach, lean), jnp.int32)
    twos = (amount - 1) // 2
    source_of, sink = lengths[1:1 + 2 * twos:2], lengths[2:2 + 2 * twos:2]
    margin = jnp.minimum(source_of - 1, reach - sink)
    moved = jax.random.randint(jax.random.fold_in(stream_key, 1), (twos,), 0, 1 << 20) % (margin + 1)
    lengths = lengths.at[1:1 + 2 * twos:2].set(source_of - moved).at[2:2 + 2 * twos:2].set(sink + moved)
    return lengths[jax.random.permutation(jax.random.fold_in(stream_key, 2), amount)]


def noise(rng, extent, spread, limit, split=(), held_as=jnp.bfloat16):
    entries = jax.random.normal(rng, extent, jnp.float32) * spread
    if len(split) > 0:
        entries = shard_levels(rng, extent, split, -0.22, 0.18) * entries
    return jnp.clip(entries, min=-limit, max=limit).astype(held_as)


def setup_inputs(seed: int = 0) -> dict:
    key_of = jax.random.split(jax.random.key(seed), 17)
    return {
        "stream": noise(key_of[0], (ROWS, LEN, D), 1.0, 6.0, ((0, 8),)),
        "cotangent": noise(key_of[1], (ROWS, LEN, D), 1.0, 6.0, ((0, 8),)),
        "segments": jax.vmap(lambda own: jnp.searchsorted(jnp.cumsum(uneven_parts(own, PAGES, LEN, LEN // 2, 2)), jnp.arange(LEN), side="right"))(jax.random.split(key_of[2], ROWS)).reshape((ROWS, LEN)).astype(jnp.int32),
        "word_boxes": with_ends(jax.random.randint(key_of[3], (4, ROWS, LEN), 0, 1024), jax.random.fold_in(key_of[3], 1), 0, 1023).astype(jnp.int32),
        "valid_mask": with_ends((jax.random.randint(key_of[4], (ROWS, LEN), 0, 8) < 7).astype(jnp.int32), jax.random.fold_in(key_of[4], 1), 0, 1),
        "w_qkv": noise(key_of[5], (LAYERS, D, 3 * D), D ** -0.5, 0.21875),
        "qv_bias": noise(key_of[6], (LAYERS, 2, D), 0.5, 3.0),
        "w_out": noise(key_of[7], (LAYERS, D, D), (D // 64) ** -0.5, 1.75),
        "out_bias": noise(key_of[8], (LAYERS, D), 0.3, 2.0),
        "rel_proj": noise(key_of[9], (LAYERS, H, HS, REL), HS ** -0.5, 0.75),
        "ln_scale": jnp.clip(1.0 + 0.1 * jax.random.normal(key_of[10], (LAYERS, 2, D), jnp.float32), 0.5, 1.5).astype(jnp.bfloat16),
        "ln_shift": noise(key_of[11], (LAYERS, 2, D), 0.3, 2.0),
        "ffn_in": noise(key_of[12], (LAYERS, D, FF), D ** -0.5, 0.21875),
        "ffn_in_bias": noise(key_of[13], (LAYERS, FF), 0.3, 2.0),
        "ffn_out": noise(key_of[14], (LAYERS, FF, D), FF ** -0.5, 0.109375),
        "ffn_out_bias": noise(key_of[15], (LAYERS, D), 0.3, 2.0),
    }


@jax.custom_vjp
def low(v):
    return lax.optimization_barrier(v.astype(jnp.bfloat16)).astype(jnp.float32)

@jax.custom_vjp
def low_back(v):
    return v

def low_keep(v):
    return (low(v), None)

def low_pass(kept, grad):
    return (grad,)

def back_keep(v):
    return (v, None)

def back_low(kept, grad):
    return (low(grad),)
low.defvjp(low_keep, low_pass)
low_back.defvjp(back_keep, back_low)
highest = lax.Precision.HIGHEST
ln_eps = 1e-05
masked_score = -1e+30
text_pairs = 32
box_pairs = 8

def angle_tables(word_boxes, length):
    row_count = word_boxes.shape[1]
    positions = jnp.arange(length, dtype=jnp.float32)
    text_rate = jnp.exp(-jnp.log(10000.0) * jnp.arange(text_pairs, dtype=jnp.float32) / text_pairs)
    text_angle = jnp.broadcast_to(positions[:, None] * text_rate[None, :], (row_count, length, text_pairs))
    box_rate = jnp.exp2(-jnp.arange(box_pairs, dtype=jnp.float32))
    coords = jnp.moveaxis(word_boxes.astype(jnp.float32), 0, -1)
    box_angle = (coords[..., None] * box_rate).reshape(row_count, length, 4 * box_pairs)
    angles = jnp.concatenate([text_angle, box_angle], -1)
    return (jnp.cos(angles), jnp.sin(angles))

def allowed_mask(segments, valid_mask):
    length = segments.shape[-1]
    same_page = segments[:, :, None] == segments[:, None, :]
    diagonal = jnp.arange(length)[:, None] == jnp.arange(length)[None, :]
    return same_page & (valid_mask[:, None, :] > 0) | diagonal[None]

def rotate(coefficients, cosines, sines):
    half = coefficients.shape[-1] // 2
    first = coefficients[..., :half]
    second = coefficients[..., half:]
    return jnp.concatenate([first * cosines + second * sines, first * sines - second * cosines], -1)

def layer_norm(residual, scale, shift):
    average = lax.optimization_barrier(jnp.mean(residual, -1, keepdims=True))
    centered = residual - average
    variance = lax.optimization_barrier(jnp.mean(centered * centered, -1, keepdims=True))
    return centered * lax.rsqrt(variance + ln_eps) * scale + shift

def attend_row(pieces):
    query_part, key_part, value_part, turned, key_features, allowed = pieces
    plain_scores = jnp.einsum('ihd,jhd->hij', query_part, key_part, precision=highest)
    plain_scores = plain_scores + jnp.einsum('ihf,jf->hij', turned, key_features, precision=highest)
    scores = jnp.where(allowed[None], low_back(plain_scores * HS ** (-0.5)), masked_score)
    row_max = lax.optimization_barrier(jnp.max(scores, -1, keepdims=True))
    exponent = jnp.exp(scores - row_max)
    shares = low(exponent / lax.optimization_barrier(jnp.sum(exponent, -1, keepdims=True)))
    return jnp.einsum('hij,jhd->ihd', shares, value_part, precision=highest)

def attention_part(stream_in, weights, cosines, sines, key_features, allowed):
    w_qkv, qv_bias, w_out, out_bias, rel_proj, ln_scale, ln_shift = weights[:7]
    row_count = stream_in.shape[0]
    joint_proj = jnp.einsum('rtd,de->rte', stream_in, w_qkv, precision=highest)
    query_part = low(low_back(joint_proj[..., :D] + qv_bias[0])).reshape(row_count, LEN, H, HS)
    key_part = low(low_back(joint_proj[..., D:2 * D])).reshape(row_count, LEN, H, HS)
    value_part = low(low_back(joint_proj[..., 2 * D:] + qv_bias[1])).reshape(row_count, LEN, H, HS)
    coefficients = low_back(jnp.einsum('rthd,hdf->rthf', query_part, rel_proj, precision=highest))
    turned = low(rotate(coefficients, cosines[:, :, None], sines[:, :, None]))
    context = lax.map(jax.checkpoint(attend_row), (query_part, key_part, value_part, turned, key_features, allowed))
    context = low(low_back(context.reshape(row_count, LEN, D)))
    attention_out = low_back(jnp.einsum('rtd,de->rte', context, w_out, precision=highest) + out_bias)
    mixed_rows = low(layer_norm(stream_in + attention_out, ln_scale[0], ln_shift[0]))
    return (mixed_rows, attention_out)

def feed_part(mixed_rows, weights):
    ln_scale, ln_shift, ffn_in, ffn_in_bias, ffn_out, ffn_out_bias = weights[5:]
    preact = low_back(jnp.einsum('rtd,df->rtf', mixed_rows, ffn_in, precision=highest) + ffn_in_bias)
    activated = low(jax.nn.gelu(preact, approximate=False))
    feed_out = low_back(jnp.einsum('rtf,fd->rtd', activated, ffn_out, precision=highest) + ffn_out_bias)
    return (layer_norm(mixed_rows + feed_out, ln_scale[1], ln_shift[1]), feed_out)

def reference(stream, cotangent, segments, word_boxes, valid_mask, w_qkv, qv_bias, w_out, out_bias, rel_proj, ln_scale, ln_shift, ffn_in, ffn_in_bias, ffn_out, ffn_out_bias):
    weights = tuple((w.astype(jnp.float32) for w in (w_qkv, qv_bias, w_out, out_bias, rel_proj, ln_scale, ln_shift, ffn_in, ffn_in_bias, ffn_out, ffn_out_bias)))
    group = 8
    group_count = ROWS // group

    def one_group(grads, group_index):
        start = (group_index * group).astype(jnp.int32)
        group_stream = lax.dynamic_slice_in_dim(stream, start, group, 0).astype(jnp.float32)
        group_cot = lax.dynamic_slice_in_dim(cotangent, start, group, 0).astype(jnp.float32)
        group_segments = lax.dynamic_slice_in_dim(segments, start, group, 0)
        group_boxes = lax.dynamic_slice_in_dim(word_boxes, start, group, 1)
        group_valid = lax.dynamic_slice_in_dim(valid_mask, start, group, 0)
        cosines, sines = angle_tables(group_boxes, LEN)
        key_features = low(jnp.concatenate([cosines, sines], -1))
        allowed = allowed_mask(group_segments, group_valid)
        weight = group_valid.astype(jnp.float32)[..., None]
        probes = jnp.zeros((N_SECTION, group, LEN, D), jnp.float32)

        def squares(branch, result):
            return jnp.stack([lax.optimization_barrier(jnp.sum(branch * branch * weight, (1, 2))), lax.optimization_barrier(jnp.sum(result * result * weight, (1, 2)))], -1)

        def chain(params, probe_in):
            outputs = []
            square_sums = []
            current = group_stream + probe_in[0]
            output = current
            for layer_number in range(LAYERS):
                layer_params = [p[layer_number] for p in params]
                mixed_rows, attention_out = attention_part(current, layer_params, cosines, sines, key_features, allowed)
                mixed_rows = mixed_rows + probe_in[2 * layer_number + 1]
                outputs.append(mixed_rows)
                square_sums.append(squares(attention_out, mixed_rows))
                output, feed_out = feed_part(mixed_rows, layer_params)
                outputs.append(output)
                square_sums.append(squares(feed_out, output))
                if layer_number + 1 < LAYERS:
                    current = low(low_back(output)) + probe_in[2 * layer_number + 2]
            return (output, (jnp.stack(outputs), jnp.stack(square_sums)))
        last, backward, (outputs, square_sums) = jax.vjp(chain, weights, probes, has_aux=True)
        grad_params, grad_probes = backward(group_cot)
        grads = jax.tree.map(jnp.add, grads, grad_params)
        section_grads = jnp.stack([grad_probes[s].astype(jnp.bfloat16).astype(jnp.float32) if s % 2 == 0 else grad_probes[s] for s in range(N_SECTION)])
        counted = lax.optimization_barrier(jnp.sum(group_valid.astype(jnp.float32), 1))
        row_rms = jnp.sqrt(square_sums / (D * jnp.maximum(counted, 1.0))[None, :, None])
        return (grads, (outputs.astype(jnp.bfloat16), section_grads, row_rms))
    initial = jax.tree.map(jnp.zeros_like, weights)
    grads, (outputs, grad_inputs, row_rms) = lax.scan(one_group, initial, jnp.arange(group_count, dtype=jnp.int32))
    section_outputs = jnp.transpose(outputs, (1, 0, 2, 3, 4)).reshape(N_SECTION, ROWS, LEN, D)
    section_input_grads = jnp.transpose(grad_inputs, (1, 0, 2, 3, 4)).reshape(N_SECTION, ROWS, LEN, D)
    root_mean_squares = jnp.transpose(row_rms, (1, 0, 2, 3)).reshape(N_SECTION, ROWS, 2)
    return (section_outputs, section_input_grads, grads[0], grads[1], grads[2], grads[3], grads[4], grads[5], grads[6], grads[7], grads[8], grads[9], grads[10], root_mean_squares)
```

```python
import jax
import jax.numpy as jnp
from jax import lax
from jax.experimental import pallas as pl
from jax.experimental.pallas import tpu as pltpu
from jax.sharding import PartitionSpec as P

ln_eps = 1e-05
masked_score = -1e30
text_pairs = 32
box_pairs = 8
bf16 = jnp.bfloat16
f32 = jnp.float32
MB = 1 << 20


def dot(a, b):
    return lax.dot_general(a, b, (((1,), (0,)), ((), ())), preferred_element_type=f32)


def dot_nt(a, b):
    return lax.dot_general(a, b, (((1,), (1,)), ((), ())), preferred_element_type=f32)


def dot_tn(a, b):
    return lax.dot_general(a, b, (((0,), (0,)), ((), ())), preferred_element_type=f32)


def angle_tables(boxes, positions):
    count = boxes.shape[1]
    text_rate = jnp.exp(-jnp.log(10000.0) * jnp.arange(text_pairs, dtype=f32) / text_pairs)
    text_angle = positions[None, :] * text_rate[:, None]
    box_rate = jnp.exp2(-jnp.arange(box_pairs, dtype=f32))
    box_angle = boxes.astype(f32)[:, None, :] * box_rate[None, :, None]
    angles = jnp.concatenate([text_angle, box_angle.reshape(4 * box_pairs, count)], 0)
    return (jnp.cos(angles), jnp.sin(angles))


def norm_parts(residual):
    average = jnp.mean(residual, -1, keepdims=True)
    centered = residual - average
    inverse = lax.rsqrt(jnp.mean(centered * centered, -1, keepdims=True) + ln_eps)
    return (centered * inverse, inverse)


def norm_back(gradient, scale, normed, inverse):
    dnormed = gradient * scale
    return inverse * (
        dnormed
        - jnp.mean(dnormed, -1, keepdims=True)
        - normed * jnp.mean(dnormed * normed, -1, keepdims=True)
    )


def lane_half(shape, half):
    lane = lax.broadcasted_iota(jnp.int32, shape, 1)
    return (lane < 64) if half == 0 else (lane >= 64)


def fill_bias(code_ref, segq_ref, bias_ref):
    shape = bias_ref.shape
    same = code_ref[...] == segq_ref[...]
    key_at = lax.broadcasted_iota(jnp.int32, shape, 0)
    query_at = lax.broadcasted_iota(jnp.int32, shape, 1)
    bias_ref[...] = jnp.where(same | (key_at == query_at), 0.0, masked_score)


def attention_fwd_kernel(
    code_ref, segq_ref, q_ref, k_ref, v_ref, rel_ref, ctab_ref, stab_ref, kf_ref,
    ctx_ref, lse_ref, turned_ref, bias_ref,
):
    @pl.when(pl.program_id(0) == 0)
    def _():
        fill_bias(code_ref, segq_ref, bias_ref)

    q_pair = q_ref[...]
    kside = jnp.concatenate([kf_ref[...], k_ref[...]], 1)
    v_t = v_ref[...].T
    rel = rel_ref[0]
    ctab, stab = ctab_ref[...], stab_ref[...]
    parts = []
    for half in range(2):
        q_mine = jnp.where(lane_half(q_pair.shape, half), q_pair, 0)
        coef = dot(q_mine, rel)
        turned = (coef * ctab + pltpu.roll(coef, 64, 1) * stab).astype(bf16)
        turned_ref[:, 128 * half : 128 * half + 128] = turned
        qside = jnp.concatenate([turned, q_mine], 1) * jnp.asarray(0.125, bf16)
        scores = dot_nt(kside, qside) + bias_ref[...]
        top = jnp.max(scores, 0, keepdims=True)
        expo = jnp.exp(scores - top)
        total = jnp.sum(expo, 0, keepdims=True)
        ctx = dot(v_t[64 * half : 64 * half + 64], expo.astype(bf16))
        parts.append(ctx * (1.0 / total))
        lse_ref[0, half : half + 1, :] = top + jnp.log(total)
    ctx_ref[...] = jnp.concatenate(parts, 0).T.astype(bf16)


def attention_fwd(q, k, v, rel, ctab, stab, kf, segq, code):
    nq, width = q.shape
    nk = k.shape[0]
    pairs = width // 128
    rel_pairs = rel.reshape(pairs, 128, 128)
    whole = lambda shape: pl.BlockSpec(shape, lambda p: (0, 0))
    cols = lambda rows, lanes: pl.BlockSpec((rows, lanes), lambda p: (0, p))
    return pl.pallas_call(
        attention_fwd_kernel,
        grid=(pairs,),
        in_specs=[
            whole((nk, 1)), whole((1, nq)), cols(nq, 128), cols(nk, 128), cols(nk, 128),
            pl.BlockSpec((1, 128, 128), lambda p: (p, 0, 0)),
            whole((nq, 128)), whole((nq, 128)), whole((nk, 128)),
        ],
        out_specs=[
            cols(nq, 128), pl.BlockSpec((1, 2, nq), lambda p: (p, 0, 0)), cols(nq, 256),
        ],
        out_shape=[
            jax.ShapeDtypeStruct((nq, width), bf16),
            jax.ShapeDtypeStruct((pairs, 2, nq), f32),
            jax.ShapeDtypeStruct((nq, 2 * width), bf16),
        ],
        scratch_shapes=[pltpu.VMEM((nk, nq), f32)],
        compiler_params=pltpu.CompilerParams(vmem_limit_bytes=40 * MB),
        name="attention_forward",
    )(code, segq, q, k, v, rel_pairs, ctab, stab, kf)


def attention_bwd_kernel(
    code_ref, segq_ref, q_ref, k_ref, v_ref, turned_ref, gc_ref, lse_ref, rel_ref, cos_ref, sin_ref,
    kf_ref, dq_ref, dk_ref, dv_ref, drel_ref, bias_ref, kft_ref,
):
    @pl.when(pl.program_id(0) == 0)
    def _():
        fill_bias(code_ref, segq_ref, bias_ref)
        kft_ref[...] = kf_ref[...].T

    q_pair, gc_pair = q_ref[...], gc_ref[...]
    kside = jnp.concatenate([kf_ref[...], k_ref[...]], 1)
    k_t = k_ref[...].T
    v_pair = v_ref[...]
    cosines, sines = cos_ref[...], sin_ref[...]
    scale = jnp.asarray(0.125, bf16)
    dk, dv, drel, dqs = 0.0, 0.0, 0.0, []
    for half in range(2):
        mine = lane_half(q_pair.shape, half)
        q_mine = jnp.where(mine, q_pair, 0)
        gc_mine = jnp.where(mine, gc_pair, 0)
        q_scaled = q_mine * scale
        qside = jnp.concatenate([turned_ref[:, 128 * half : 128 * half + 128] * scale, q_scaled], 1)
        scores = dot_nt(kside, qside) + bias_ref[...]
        shares = jnp.exp(scores - lse_ref[0, half : half + 1, :])
        gp = dot_nt(v_pair, gc_mine)
        dv = dv + dot(shares.astype(bf16), gc_mine)
        weighted = shares * gp
        delta = jnp.sum(weighted, 0, keepdims=True)
        gs = (weighted - shares * delta).astype(bf16)
        dk = dk + dot(gs, q_scaled)
        side_t = jnp.concatenate([kft_ref[...], k_t[64 * half : 64 * half + 64]], 0)
        dside = dot(side_t, gs) * 0.125
        g_cos, g_sin = dside[0:64], dside[64:128]
        gcoef = jnp.concatenate(
            [g_cos * cosines + g_sin * sines, g_cos * sines - g_sin * cosines], 0
        ).astype(bf16)
        dqs.append(dside[128:192] + dot(rel_ref[0, 64 * half : 64 * half + 64], gcoef))
        drel = drel + dot(gcoef, q_mine)
    dq_ref[...] = jnp.concatenate(dqs, 0).T.astype(bf16)
    dk_ref[...] = dk.astype(dk_ref.dtype)
    dv_ref[...] = dv.astype(dv_ref.dtype)
    drel_ref[...] = drel


def attention_bwd(q, k, v, turned, gc, lse, rel, cosines, sines, kf, segq, code, out_type):
    nq, width = q.shape
    nk = k.shape[0]
    pairs = width // 128
    rel_pairs = rel.reshape(pairs, 128, 128)
    whole = lambda shape: pl.BlockSpec(shape, lambda p: (0, 0))
    cols = lambda rows, lanes: pl.BlockSpec((rows, lanes), lambda p: (0, p))
    return pl.pallas_call(
        attention_bwd_kernel,
        grid=(pairs,),
        in_specs=[
            whole((nk, 1)), whole((1, nq)), cols(nq, 128), cols(nk, 128), cols(nk, 128),
            cols(nq, 256), cols(nq, 128), pl.BlockSpec((1, 2, nq), lambda p: (p, 0, 0)),
            pl.BlockSpec((1, 128, 128), lambda p: (p, 0, 0)),
            whole((64, nq)), whole((64, nq)), whole((nk, 128)),
        ],
        out_specs=[cols(nq, 128), cols(nk, 128), cols(nk, 128), cols(128, 128)],
        out_shape=[
            jax.ShapeDtypeStruct((nq, width), bf16),
            jax.ShapeDtypeStruct((nk, width), out_type),
            jax.ShapeDtypeStruct((nk, width), out_type),
            jax.ShapeDtypeStruct((128, width), f32),
        ],
        scratch_shapes=[pltpu.VMEM((nk, nq), f32), pltpu.VMEM((128, nk), bf16)],
        compiler_params=pltpu.CompilerParams(vmem_limit_bytes=40 * MB),
        name="attention_backward",
    )(code, segq, q, k, v, turned, gc, lse, rel_pairs, cosines, sines, kf)


def body(
    stream, cotangent, segments, word_boxes, valid_mask, w_qkv, qv_bias, w_out, out_bias, rel_proj,
    ln_scale, ln_shift, ffn_in, ffn_in_bias, ffn_out, ffn_out_bias,
):
    sections = lax.axis_size("section")
    dp = lax.axis_size("dp")
    section = lax.axis_index("section")
    dp_index = lax.axis_index("dp")
    core, layer_side = section % 2, section // 2
    rows, length, width = stream.shape
    layers = w_qkv.shape[0]
    ff_width = ffn_in.shape[2]
    assert rows == 3 and sections == 2 * layers and layers == 2
    half = length // 2
    tokens = length + half
    bits = dp.bit_length() - 1

    def flip(x, bit):
        return lax.ppermute(x, "section", [(i, i ^ bit) for i in range(sections)])

    def mine(x):
        own = lax.dynamic_index_in_dim(x, core, 0, keepdims=False)
        part = lax.dynamic_slice_in_dim(x[2], core * half, half, 0)
        return jnp.concatenate([own, part], 0)

    def whole_rows(own, other):
        first = jnp.where(core == 0, own, other)
        second = jnp.where(core == 0, other, own)
        return jnp.stack(
            [first[:length], second[:length], jnp.concatenate([first[length:], second[length:]], 0)]
        )

    def own_first(x):
        low = lax.dynamic_slice_in_dim(x, core * half, half, 0)
        high = lax.dynamic_slice_in_dim(x, (1 - core) * half, half, 0)
        return jnp.concatenate([low, high], 0)

    def both(x):
        own = lax.dynamic_index_in_dim(x, core, 0, keepdims=False)
        return jnp.concatenate([own, own_first(x[2])], 0)

    positions = jnp.arange(length, dtype=f32)
    positions = jnp.concatenate([positions, own_first(positions)])
    boxes = jnp.stack([both(word_boxes[i]) for i in range(4)])
    cos_t, sin_t = angle_tables(boxes, positions)
    kf = jnp.concatenate([cos_t, sin_t], 0).T.astype(bf16)
    ctab = jnp.concatenate([cos_t, -cos_t], 0)[:, :tokens].T
    stab = jnp.concatenate([sin_t, sin_t], 0)[:, :tokens].T
    seg_all, valid_all = both(segments), both(valid_mask)
    code_all = jnp.where(valid_all > 0, seg_all, -1)
    jobs = []
    for start, queries in ((0, length), (length, half)):
        q_at = slice(start, start + queries)
        k_at = slice(start, start + length)
        jobs.append(
            (q_at, ctab[q_at], stab[q_at], cos_t[:, q_at], sin_t[:, q_at], kf[k_at],
             seg_all[q_at][None, :], code_all[k_at][:, None])
        )

    h = mine(stream)
    valid = mine(valid_mask).astype(f32)[:, None]
    kept, square_parts = [], []

    def squares(values):
        per_token = jnp.sum(values * values, 1, keepdims=True) * valid
        return [jnp.sum(per_token[:length]), jnp.sum(per_token[length:])]

    for l in range(layers):
        gain, shift = ln_scale[l].astype(f32), ln_shift[l].astype(f32)
        joint = dot(h, w_qkv[l])
        q = (joint[:, :width] + qv_bias[l, 0]).astype(bf16)
        k = joint[:, width : 2 * width].astype(bf16)
        v = (joint[:, 2 * width :] + qv_bias[l, 1]).astype(bf16)
        other_k, other_v = flip(k[length:], 1), flip(v[length:], 1)
        keys = (k[:length], jnp.concatenate([k[length:], other_k], 0))
        values = (v[:length], jnp.concatenate([v[length:], other_v], 0))
        results = []
        for i, (q_at, ct, st, c_t, s_t, kfi, segq, code) in enumerate(jobs):
            results.append(
                attention_fwd(q[q_at], keys[i], values[i], rel_proj[l], ct, st, kfi, segq, code)
            )
        ctx = jnp.concatenate([results[0][0], results[1][0]], 0)
        attention_out = dot(ctx, w_out[l]) + out_bias[l]
        res_one = h.astype(f32) + attention_out
        normed_one, inverse_one = norm_parts(res_one)
        mixed = (normed_one * gain[0] + shift[0]).astype(bf16)
        preact = dot(mixed, ffn_in[l]) + ffn_in_bias[l]
        phi = 0.5 * (1.0 + lax.erf(preact * 0.7071067811865476))
        act = (preact * phi).astype(bf16)
        slope = (phi + preact * jnp.exp(-0.5 * preact * preact) * 0.3989422804014327).astype(bf16)
        feed_out = dot(act, ffn_out[l]) + ffn_out_bias[l]
        res_two = mixed.astype(f32) + feed_out
        normed_two, inverse_two = norm_parts(res_two)
        out = normed_two * gain[1] + shift[1]
        square_parts.append(
            [squares(attention_out), squares(mixed.astype(f32)), squares(feed_out), squares(out)]
        )
        out = out.astype(bf16)
        kept.append(
            (h, q, keys, values, results, ctx, res_one, mixed, act, slope, res_two, out)
        )
        h = out

    def flip_dp(x, bit):
        return lax.ppermute(x, "dp", [(i, i ^ bit) for i in range(dp)])

    def reduce_pieces(pieces):
        def halve(x, bit_value, axis, send):
            keep = lax.dynamic_index_in_dim(x, bit_value, axis, keepdims=False)
            away = lax.dynamic_index_in_dim(x, 1 - bit_value, axis, keepdims=False)
            return keep + send(away)

        reduced = []
        for x in pieces:
            slabs, double, cols = x.shape
            x = x.reshape(slabs, 2, double // 2, cols)
            x = halve(x, core, 1, lambda v: flip(v, 1))
            for bit in range(bits):
                x = x.reshape((x.shape[0] // 2, 2) + x.shape[1:])
                value = (dp_index >> bit) & 1
                x = halve(x, value, 1, lambda v: flip_dp(v, 1 << bit))
            reduced.append(x.reshape(x.shape[-2:]))
        return reduced

    def spread(x):
        far = flip(x, 2)
        x = jnp.where(layer_side == 0, jnp.concatenate([x, far], 1), jnp.concatenate([far, x], 1))
        near = flip(x, 1)
        return jnp.where(core == 0, jnp.concatenate([x, near], 0), jnp.concatenate([near, x], 0))

    def side(x):
        cols = x.shape[1] // 2
        return lax.dynamic_slice_in_dim(x, layer_side * cols, cols, 1)

    def product(left, right):
        result = dot_tn(left, side(right)).astype(bf16)
        return result.reshape(dp, result.shape[0] // dp, result.shape[1])

    grad = mine(cotangent).astype(f32)
    big, small, mixed_grads, input_grads = {}, {}, [None] * layers, [None] * layers
    for l in reversed(range(layers)):
        gain = ln_scale[l].astype(f32)
        h, q, keys, values, results, ctx, res_one, mixed, act, slope, res_two, out = kept[l]
        normed, inverse = norm_parts(res_two)
        scale_two, shift_two = jnp.sum(grad * normed, 0), jnp.sum(grad, 0)
        g_res_two = norm_back(grad, gain[1], normed, inverse)
        g_feed = g_res_two.astype(bf16)
        d_ffn_out = product(act, g_feed)
        g_pre = (dot_nt(g_feed, ffn_out[l]) * slope.astype(f32)).astype(bf16)
        d_ffn_in = product(mixed, g_pre)
        big[l, "ffn"] = reduce_pieces([d_ffn_out, d_ffn_in])
        g_mixed = dot_nt(g_pre, ffn_in[l]) + g_res_two
        mixed_grads[l] = g_mixed
        normed, inverse = norm_parts(res_one)
        scale_one, shift_one = jnp.sum(g_mixed * normed, 0), jnp.sum(g_mixed, 0)
        g_res_one = norm_back(g_mixed, gain[0], normed, inverse)
        g_attn = g_res_one.astype(bf16)
        d_out = product(ctx, g_attn)
        g_ctx = dot_nt(g_attn, w_out[l]).astype(bf16)
        grads = []
        for i, (q_at, ct, st, c_t, s_t, kfi, segq, code) in reversed(list(enumerate(jobs))):
            grads.append(
                attention_bwd(
                    q[q_at], keys[i], values[i], results[i][2], g_ctx[q_at], results[i][1],
                    rel_proj[l], c_t, s_t, kfi, segq, code, bf16 if i == 0 else f32,
                )
            )
        shared_grads, own_grads = grads
        dq = jnp.concatenate([own_grads[0], shared_grads[0]], 0)

        def joined(own, shared):
            arrived = flip(shared[half:].astype(bf16), 1)
            return jnp.concatenate([own, (shared[:half] + arrived).astype(bf16)], 0)

        dk, dv = joined(own_grads[1], shared_grads[1]), joined(own_grads[2], shared_grads[2])
        g_joint = jnp.concatenate([dq, dk, dv], 1)
        d_qkv = product(h, g_joint)
        g_h = (dot_nt(g_joint, w_qkv[l]) + g_res_one).astype(bf16)
        input_grads[l] = g_h
        grad = g_h.astype(f32)
        total = lambda x: jnp.sum(x.astype(f32), 0)
        vectors = [total(dq), total(dv), total(g_attn), scale_one, scale_two, shift_one, shift_two,
                   total(g_feed)]
        small_rows = jnp.concatenate(
            [x.reshape(dp, width // dp) for x in vectors]
            + [total(g_pre).reshape(dp, ff_width // dp)], 1,
        )
        d_rel = side(own_grads[3] + shared_grads[3])
        rel_rows = d_rel.shape[0] // dp
        d_rel = d_rel.reshape(dp, rel_rows, width // 2).astype(bf16)
        room = rel_rows * (width // 2)
        small_rows = jnp.pad(small_rows, ((0, 0), (0, room - small_rows.shape[1])))
        small_rows = small_rows.astype(bf16).reshape(dp, rel_rows, width // 2)
        misc = jnp.concatenate([d_rel, small_rows], 1)
        big[l, "attn"] = reduce_pieces([d_qkv, d_out, misc])

    def pick(pair):
        return jnp.where(layer_side == 0, pair[0], pair[1])

    mixed_side, out_side = pick([kept[0][7], kept[1][7]]), pick([kept[0][11], kept[1][11]])
    own_piece = jnp.where(core == 0, mixed_side, out_side)
    away_piece = jnp.where(core == 0, out_side, mixed_side)
    section_outs = whole_rows(own_piece, flip(away_piece, 1))[None]
    h_side, m_side = pick(input_grads), pick(mixed_grads)
    own_piece = jnp.where(core == 0, h_side.astype(f32), m_side)
    away_piece = jnp.where(core == 0, m_side.astype(bf16), h_side)
    in_grads = whole_rows(own_piece, flip(away_piece, 1).astype(f32))[None]

    squares_all = jnp.stack([jnp.stack([jnp.stack(pair) for pair in four]) for four in square_parts])
    squares_mine = pick(squares_all).reshape(2, 2, 2)
    squares_far = flip(squares_mine, 1)
    sub = lambda x: lax.dynamic_index_in_dim(x, core, 0, keepdims=False)
    near, far = sub(squares_mine), sub(squares_far)
    first = jnp.where(core == 0, near[:, 0], far[:, 0])
    second = jnp.where(core == 0, far[:, 0], near[:, 0])
    square_rows = jnp.stack([first, second, near[:, 1] + far[:, 1]])
    row_counts = jnp.sum(valid_mask.astype(f32), 1)
    root_mean_squares = jnp.sqrt(square_rows / (width * jnp.maximum(row_counts, 1.0))[:, None])[None]

    out = {}
    for l in range(layers):
        out[l, "ffn_out"], out[l, "ffn_in"] = [spread(x) for x in big[l, "ffn"]]
        qkv, w_o, misc = big[l, "attn"]
        out[l, "qkv"], out[l, "out"] = spread(qkv), spread(w_o)
        misc_rows = misc.shape[0]
        near = flip(misc, 1)
        rel_part = jnp.where(core == 0, misc, near)
        small_part = jnp.where(core == 0, near, misc)
        rel_far = flip(rel_part, 2)
        rel_all = jnp.where(
            layer_side == 0,
            jnp.concatenate([rel_part, rel_far], 1), jnp.concatenate([rel_far, rel_part], 1),
        )
        out[l, "rel"] = rel_all.astype(f32).T.reshape(width // 64, 64, misc_rows)
        flat = small_part.astype(f32).reshape(-1)
        n = width // dp
        pieces = [flat[i * n : (i + 1) * n] for i in range(8)] + [flat[8 * n : 8 * n + ff_width // dp]]
        out[l, "small"] = pieces

    both_layers = lambda name: jnp.stack([out[0, name].astype(f32), out[1, name].astype(f32)])
    small_at = lambda i: jnp.stack([out[l, "small"][i] for l in range(layers)])
    return (
        section_outs,
        in_grads,
        both_layers("qkv"),
        jnp.stack([small_at(0), small_at(1)], 1),
        both_layers("out"),
        small_at(2),
        both_layers("rel"),
        jnp.stack([small_at(3), small_at(4)], 1),
        jnp.stack([small_at(5), small_at(6)], 1),
        both_layers("ffn_in"),
        small_at(8),
        both_layers("ffn_out"),
        small_at(7),
        root_mean_squares,
    )


def solution(mesh):
    return jax.shard_map(
        body,
        mesh=mesh,
        in_specs=(
            P("dp", None, None),
            P("dp", None, None),
            P("dp", None),
            P(None, "dp", None),
            P("dp", None),
        )
        + (P(),) * 11,
        out_specs=(
            P("section", "dp", None, None),
            P("section", "dp", None, None),
            P(None, "dp", None),
            P(None, None, "dp"),
            P(None, "dp", None),
            P(None, "dp"),
            P(None, None, None, "dp"),
            P(None, None, "dp"),
            P(None, None, "dp"),
            P(None, "dp", None),
            P(None, "dp"),
            P(None, "dp", None),
            P(None, "dp"),
            P("section", "dp", None),
        ),
        check_vma=False,
    )
```

```python
import functools

import jax
import jax.numpy as jnp
from jax import lax
from jax.experimental import pallas as pl
from jax.experimental.pallas import tpu as pltpu
from jax.sharding import PartitionSpec as P

ln_eps = 1e-05
masked_score = -1e30
bf16 = jnp.bfloat16
f32 = jnp.float32
MB = 1 << 20
SUPER = 8
LANES = 384

ERF_COEFS = (
    0.7978849414899046, 0.0363330844086688, -3.259474462099993e-05, -5.5306316685416947e-05,
    3.964773125473232e-06, -1.322662757755248e-07, 1.7562773256476674e-09,
)


def dot(a, b):
    return lax.dot_general(a, b, (((1,), (0,)), ((), ())), preferred_element_type=f32)


def dot_nt(a, b):
    return lax.dot_general(a, b, (((1,), (1,)), ((), ())), preferred_element_type=f32)


def gelu_and_slope(x):
    square = x * x
    g = ERF_COEFS[-1]
    for c in ERF_COEFS[-2::-1]:
        g = g * square + c
    phi = 0.5 * jnp.tanh(x * g) + 0.5
    density = jnp.exp2(square * (-0.5 * 1.4426950408889634)) * 0.3989422804014327
    return x * phi, phi + x * density


def norm_parts(residual):
    average = jnp.mean(residual, -1, keepdims=True)
    centered = residual - average
    inverse = lax.rsqrt(jnp.mean(centered * centered, -1, keepdims=True) + ln_eps)
    return centered * inverse, inverse


def norm_back(gradient, gain, normed, inverse):
    dnormed = gradient * gain
    return inverse * (
        dnormed
        - jnp.mean(dnormed, -1, keepdims=True)
        - normed * jnp.mean(dnormed * normed, -1, keepdims=True)
    )


def col_sum(x):
    return jnp.sum(x, 0, keepdims=True)


def call(kernel, name, grid, ids, in_specs, inputs, out_specs, out_shape, scratch=()):
    return pl.pallas_call(
        kernel,
        grid_spec=pltpu.PrefetchScalarGridSpec(
            num_scalar_prefetch=1,
            grid=grid,
            in_specs=in_specs,
            out_specs=out_specs,
            scratch_shapes=list(scratch),
        ),
        out_shape=out_shape,
        compiler_params=pltpu.CompilerParams(vmem_limit_bytes=62 * MB),
        name=name,
    )(ids, *inputs)


def spec(shape, *index):
    def index_map(i, ids):
        return tuple(x(i, ids) if callable(x) else x for x in index)

    return pl.BlockSpec(shape, index_map)


def shape_of(shape, dtype):
    return jax.ShapeDtypeStruct(shape, dtype)


step = lambda i, ids: i


def row_tiles(half, width, gathered):
    if not gathered:
        return [spec((1, half, width), t, 0, 0) for t in range(3)]
    core = lambda ids: ids[0]
    return [
        spec((1, half, width), lambda i, ids: 2 * core(ids), 0, 0),
        spec((1, half, width), lambda i, ids: 2 * core(ids) + 1, 0, 0),
        spec((1, half, width), lambda i, ids: 4 + core(ids), 0, 0),
    ]


def tables_kernel(
    ids, boxes_ref, seg_ref, valid_ref,
    cos_ref, sin_ref, kf_ref, ctab_ref, stab_ref, code_ref, segrow_ref, valid_col_ref,
):
    core = ids[0]
    length = seg_ref.shape[1]
    half = length // 2

    def ordered(read):
        near = pl.multiple_of(core * half, half)
        far = pl.multiple_of((1 - core) * half, half)
        return jnp.concatenate(
            [read(pl.ds(core, 1), slice(None)), read(2, pl.ds(near, half)), read(2, pl.ds(far, half))], 1
        )

    def row_of(ref):
        def read(r, c):
            r = pl.ds(2, 1) if isinstance(r, int) else r
            return ref[r, c]
        return ordered(read)

    count = length * 2
    at = lax.broadcasted_iota(jnp.int32, (1, count), 1)
    shared = jnp.where(
        at < length + half, at - length + core * half, at - length - half + (1 - core) * half
    )
    position = jnp.where(at < length, at, shared).astype(f32)
    rate_at = lax.broadcasted_iota(jnp.int32, (32, 1), 0).astype(f32)
    text = position * jnp.exp(rate_at * (-9.210340371976184 / 32))
    box_rate = jnp.exp2(-lax.broadcasted_iota(jnp.int32, (8, 1), 0).astype(f32))
    angles = [text]
    for c in range(4):
        coords = row_of(boxes_ref.at[c]).astype(f32)
        angles.append(coords * box_rate)
    angles = jnp.concatenate(angles, 0)
    cosines, sines = jnp.cos(angles), jnp.sin(angles)
    cos_ref[...], sin_ref[...] = cosines, sines
    kf_ref[...] = jnp.concatenate([cosines, sines], 0).T.astype(bf16)
    ctab_ref[...] = jnp.concatenate([cosines, -cosines], 0).T
    stab_ref[...] = jnp.concatenate([sines, sines], 0).T
    seg = row_of(seg_ref).astype(f32)
    valid = row_of(valid_ref).astype(f32)
    segrow_ref[...] = jnp.broadcast_to(seg, segrow_ref.shape)
    code_ref[...] = jnp.broadcast_to(jnp.where(valid > 0, seg, -1.0), (128, count)).T
    valid_col_ref[...] = jnp.broadcast_to(valid, (128, count)).T


def make_tables(ids, word_boxes, segments, valid_mask):
    length = segments.shape[1]
    count = 2 * length
    full = lambda *shape: spec(shape, *([0] * len(shape)))
    outs = [
        ((64, count), f32), ((64, count), f32), ((count, 128), bf16), ((count, 128), f32),
        ((count, 128), f32), ((count, 128), f32), ((8, count), f32), ((count, 128), f32),
    ]
    return call(
        tables_kernel, "tables", (1,), ids,
        [full(*word_boxes.shape), full(*segments.shape), full(*valid_mask.shape)],
        [word_boxes, segments, valid_mask],
        [full(*s) for s, _ in outs], [shape_of(s, d) for s, d in outs],
    )


def qkv_kernel(
    ids, x0, x1, x2, w_ref, bias_ref, rel_ref, ctab_ref, stab_ref, joint_ref, turned_ref, kv_ref, x_ref,
    *, layer,
):
    j = pl.program_id(0)
    half = x0.shape[1]

    @pl.when(j == 0)
    def _():
        x_ref[0:half], x_ref[half : 2 * half], x_ref[2 * half :] = x0[0], x1[0], x2[0]

    flags = [(j == 0).astype(f32), (j == 2).astype(f32)]
    bias = bias_ref[layer, 0:1, :].astype(f32) * flags[0] + bias_ref[layer, 1:2, :].astype(f32) * flags[1]
    joint = (dot(x_ref[...], w_ref[0]) + bias).astype(bf16)
    joint_ref[...] = joint
    kv_ref[...] = joint[2 * half :]

    @pl.when(j == 0)
    def _():
        ctab, stab = ctab_ref[...], stab_ref[...]
        row = lax.broadcasted_iota(jnp.int32, (128, 128), 0)
        for p in range(rel_ref.shape[1]):
            rel = rel_ref[0, p]
            zero = jnp.zeros_like(rel)
            block = jnp.concatenate([jnp.where(row < 64, rel, zero), jnp.where(row < 64, zero, rel)], 1)
            coef = dot(joint[:, 128 * p : 128 * p + 128], block)
            for e in range(2):
                c = coef[:, 128 * e : 128 * e + 128]
                at = 256 * p + 128 * e
                turned_ref[:, at : at + 128] = (c * ctab + pltpu.roll(c, 64, 1) * stab).astype(bf16)


def project(ids, x, gathered, w_qkv, qv_bias, rel_pairs, ctab, stab, layer):
    half, width = x.shape[1], x.shape[2]
    tokens = 3 * half
    pairs = rel_pairs.shape[1]
    return call(
        functools.partial(qkv_kernel, layer=layer), "projections", (3,), ids,
        row_tiles(half, width, gathered)
        + [
            spec((1, width, width), layer, 0, step), spec(qv_bias.shape, 0, 0, 0),
            spec((1, pairs, 128, 128), layer, 0, 0, 0), spec((tokens, 128), 0, 0),
            spec((tokens, 128), 0, 0),
        ],
        [x, x, x, w_qkv, qv_bias, rel_pairs, ctab, stab],
        [
            spec((tokens, width), 0, step), spec((tokens, 2 * width), 0, 0),
            spec((half, width), 0, lambda i, ids: jnp.maximum(i - 1, 0)),
        ],
        [
            shape_of((tokens, 3 * width), bf16), shape_of((tokens, 2 * width), bf16),
            shape_of((half, 2 * width), bf16),
        ],
        [pltpu.VMEM((tokens, width), bf16)],
    )


def lane_half(shape, half):
    lane = lax.broadcasted_iota(jnp.int32, shape, 1)
    return (lane < 64) if half == 0 else (lane >= 64)


def only_half(x, half):
    return jnp.where(lane_half(x.shape, half), x, jnp.zeros_like(x))


def fill_bias(code_ref, seg_ref, bias_ref):
    shape = bias_ref.shape
    code = jnp.concatenate([code_ref[...]] * (shape[1] // 128), 1)
    same = code == seg_ref[0:1, :]
    key_at = lax.broadcasted_iota(jnp.int32, shape, 0)
    query_at = lax.broadcasted_iota(jnp.int32, shape, 1)
    bias_ref[...] = jnp.where(same | (key_at == query_at), 0.0, masked_score)


def attention_fwd_kernel(
    ids, code_ref, seg_ref, kf_ref, q_ref, turned_ref, k_ref, v_ref, *rest, per_step, shared,
):
    if shared:
        k_far, v_far, ctx_ref, lse_ref, bias_ref, k_all, v_all = rest
        half = k_ref.shape[0]
        k_all[0:half], k_all[half:] = k_ref[...], k_far[...]
        v_all[0:half], v_all[half:] = v_ref[...], v_far[...]
        k_ref, v_ref = k_all, v_all
    else:
        ctx_ref, lse_ref, bias_ref = rest

    @pl.when(pl.program_id(0) == 0)
    def _():
        fill_bias(code_ref, seg_ref, bias_ref)

    scale = jnp.asarray(0.125, bf16)
    units = [(pair, e) for pair in range(per_step) for e in range(2)]
    values_t = {}

    def scores_of(unit):
        pair, e = unit
        at = slice(128 * pair, 128 * pair + 128)
        turned = turned_ref[:, 256 * pair + 128 * e : 256 * pair + 128 * e + 128]
        qside = jnp.concatenate([turned, only_half(q_ref[:, at], e)], 1) * scale
        kside = jnp.concatenate([kf_ref[...], k_ref[:, at]], 1)
        return dot_nt(kside, qside) + bias_ref[...]

    def finish(unit, scores):
        pair, e = unit
        top = jnp.max(scores, 0, keepdims=True)
        expo = jnp.exp(scores - top)
        total = jnp.sum(expo, 0, keepdims=True)
        if pair not in values_t:
            values_t[pair] = v_ref[:, 128 * pair : 128 * pair + 128].T
        ctx = dot(values_t[pair][64 * e : 64 * e + 64], expo.astype(bf16))
        at = 128 * pair + 64 * e
        ctx_ref[at : at + 64, :] = (ctx * (1.0 / total)).astype(bf16)
        lse_ref[0, 2 * pair + e : 2 * pair + e + 1, :] = top + jnp.log(total)

    scores = scores_of(units[0])
    for i, unit in enumerate(units):
        upcoming = scores_of(units[i + 1]) if i + 1 < len(units) else None
        finish(unit, scores)
        scores = upcoming


def attention_fwd(ids, shared, tables, joint, turned, kv_far, per_step=2):
    cos_t, sin_t, kf, ctab, stab, code, seg, valid = tables
    tokens, width = joint.shape[0], joint.shape[1] // 3
    half = tokens // 3
    nk = 2 * half
    nq = half if shared else nk
    key_rows = half if shared else nk
    lanes = 128 * per_step
    steps = width // lanes
    q_row = 2 if shared else 0
    at = lambda off: (lambda i, ids: i + off)
    in_specs = [
        spec((nk, 128), int(shared), 0), spec((8, nq), 0, q_row), spec((nk, 128), int(shared), 0),
        spec((nq, lanes), q_row, step), spec((nq, 2 * lanes), q_row, step),
        spec((key_rows, lanes), q_row, at(steps)), spec((key_rows, lanes), q_row, at(2 * steps)),
    ]
    inputs = [code, seg, kf, joint, turned, joint, joint]
    scratch = [pltpu.VMEM((nk, nq), f32)]
    if shared:
        in_specs += [spec((half, lanes), 0, step), spec((half, lanes), 0, at(steps))]
        inputs += [kv_far, kv_far]
        scratch += [pltpu.VMEM((nk, lanes), bf16)] * 2
    return call(
        functools.partial(attention_fwd_kernel, per_step=per_step, shared=shared),
        "attention_forward", (steps,), ids, in_specs, inputs,
        [spec((lanes, nq), step, 0), spec((1, 2 * per_step, nq), step, 0, 0)],
        [shape_of((width, nq), bf16), shape_of((steps, 2 * per_step, nq), f32)],
        scratch,
    )


def attention_bwd_kernel(
    ids, code_ref, seg_ref, kf_ref, cos_ref, sin_ref, rel_ref, lse_ref, gc_ref, q_ref, turned_ref,
    k_ref, v_ref, *rest, per_step, shared,
):
    if shared:
        k_far, v_far, keep_ref, send_ref, drel_ref, bias_ref, kft_ref, k_all, v_all = rest
        half = k_ref.shape[0]
        k_all[0:half], k_all[half:] = k_ref[...], k_far[...]
        v_all[0:half], v_all[half:] = v_ref[...], v_far[...]
        k_ref, v_ref = k_all, v_all
    else:
        keep_ref, drel_ref, bias_ref, kft_ref = rest

    @pl.when(pl.program_id(0) == 0)
    def _():
        fill_bias(code_ref, seg_ref, bias_ref)
        kft_ref[...] = kf_ref[...].T

    scale = jnp.asarray(0.125, bf16)
    cosines, sines = cos_ref[...], sin_ref[...]
    units = [(pair, e) for pair in range(per_step) for e in range(2)]
    store = {}

    def scores_of(unit):
        pair, e = unit
        at = slice(128 * pair, 128 * pair + 128)
        q_mine = only_half(q_ref[:, at], e)
        gc_mine = only_half(gc_ref[:, at], e)
        q_scaled = q_mine * scale
        turned = turned_ref[:, 256 * pair + 128 * e : 256 * pair + 128 * e + 128]
        qside = jnp.concatenate([turned * scale, q_scaled], 1)
        kside = jnp.concatenate([kf_ref[...], k_ref[:, at]], 1)
        scores = dot_nt(kside, qside) + bias_ref[...]
        gp = dot_nt(v_ref[:, at], gc_mine)
        return scores, gp, q_mine, gc_mine, q_scaled

    def finish(unit, parts):
        pair, e = unit
        scores, gp, q_mine, gc_mine, q_scaled = parts
        at = slice(128 * pair, 128 * pair + 128)
        shares = jnp.exp(scores - lse_ref[0, 2 * pair + e : 2 * pair + e + 1, :])
        dv = dot(shares.astype(bf16), gc_mine)
        weighted = shares * gp
        delta = jnp.sum(weighted, 0, keepdims=True)
        gs = (weighted - shares * delta).astype(bf16)
        dk = dot(gs, q_scaled)
        if pair not in store:
            store[pair] = k_ref[:, at].T
        side_t = jnp.concatenate([kft_ref[...], store[pair][64 * e : 64 * e + 64]], 0)
        dside = dot(side_t, gs) * 0.125
        g_cos, g_sin = dside[0:64], dside[64:128]
        gcoef = jnp.concatenate(
            [g_cos * cosines + g_sin * sines, g_cos * sines - g_sin * cosines], 0
        ).astype(bf16)
        dq = dside[128:192] + dot(rel_ref[0, pair, 64 * e : 64 * e + 64], gcoef)
        drel = dot(gcoef, q_mine)
        if e == 0:
            store["even"] = (dq, dk, dv, drel)
            return
        dq0, dk0, dv0, drel0 = store["even"]
        dq = jnp.concatenate([dq0, dq], 0).T.astype(bf16)
        dk, dv = (dk0 + dk).astype(bf16), (dv0 + dv).astype(bf16)
        drel_ref[:, at] = drel0 + drel
        n = keep_ref.shape[1]
        keep_ref[0, :, at] = dq
        keep_ref[1, :, at], keep_ref[2, :, at] = dk[0:n], dv[0:n]
        if shared:
            send_ref[0, :, at], send_ref[1, :, at] = dk[n:], dv[n:]

    parts = scores_of(units[0])
    for i, unit in enumerate(units):
        upcoming = scores_of(units[i + 1]) if i + 1 < len(units) else None
        finish(unit, parts)
        parts = upcoming


def attention_bwd(ids, shared, tables, joint, turned, kv_far, lse, g_ctx, rel_pairs, layer, per_step=2):
    cos_t, sin_t, kf, ctab, stab, code, seg, valid = tables
    tokens, width = joint.shape[0], joint.shape[1] // 3
    half = tokens // 3
    nk = 2 * half
    nq = half if shared else nk
    key_rows = half if shared else nk
    lanes = 128 * per_step
    steps = width // lanes
    q_row = 2 if shared else 0
    at = lambda off: (lambda i, ids: i + off)
    in_specs = [
        spec((nk, 128), int(shared), 0), spec((8, nq), 0, q_row), spec((nk, 128), int(shared), 0),
        spec((64, nq), 0, q_row), spec((64, nq), 0, q_row),
        spec((1, per_step, 128, 128), layer, step, 0, 0),
        spec((1, 2 * per_step, nq), step, 0, 0), spec((nq, lanes), q_row, step),
        spec((nq, lanes), q_row, step), spec((nq, 2 * lanes), q_row, step),
        spec((key_rows, lanes), q_row, at(steps)), spec((key_rows, lanes), q_row, at(2 * steps)),
    ]
    inputs = [code, seg, kf, cos_t, sin_t, rel_pairs, lse, g_ctx, joint, turned, joint, joint]
    scratch = [pltpu.VMEM((nk, nq), f32), pltpu.VMEM((128, nk), bf16)]
    out_specs = [spec((3, key_rows, lanes), 0, 0, step)]
    out_shape = [shape_of((3, key_rows, width), bf16)]
    if shared:
        in_specs += [spec((half, lanes), 0, step), spec((half, lanes), 0, at(steps))]
        inputs += [kv_far, kv_far]
        scratch += [pltpu.VMEM((nk, lanes), bf16)] * 2
        out_specs.append(spec((2, half, lanes), 0, 0, step))
        out_shape.append(shape_of((2, half, width), bf16))
    out_specs.append(spec((128, lanes), 0, step))
    out_shape.append(shape_of((128, width), f32))
    return call(
        functools.partial(attention_bwd_kernel, per_step=per_step, shared=shared),
        "attention_backward", (steps,), ids, in_specs, inputs, out_specs, out_shape, scratch,
    )


def feed_fwd_kernel(
    ids, x0, x1, x2, own_ref, shared_ref, valid_ref, w_out_ref, out_bias_ref, scale_ref, shift_ref,
    in_ref, in_bias_ref, out_ref, ffn_bias_ref,
    n1_ref, r1_ref, n2_ref, r2_ref, mixed_ref, act_ref, slope_ref, h_ref, squares_ref,
    feed_ref,
    *, layer, parts,
):
    j = pl.program_id(0)
    half = x0.shape[1]
    long = 2 * half
    row = lambda ref, *at: ref[at[:-1] + (slice(at[-1], at[-1] + 1),)].astype(f32)

    def add_squares(values, k):
        weighted = values * values * valid_ref[:, 0:1]
        squares_ref[k : k + 1, :] = col_sum(weighted[0:long])
        squares_ref[k + 1 : k + 2, :] = col_sum(weighted[long:])

    @pl.when(j == 0)
    def _():
        ctx = jnp.concatenate([own_ref[...].T, shared_ref[...].T], 0)
        attention = dot(ctx, w_out_ref[0]) + row(out_bias_ref, layer)
        add_squares(attention, 0)
        x = jnp.concatenate([x0[0], x1[0], x2[0]], 0).astype(f32)
        normed, inverse = norm_parts(x + attention)
        mixed = (normed * row(scale_ref, layer, 0) + row(shift_ref, layer, 0)).astype(bf16)
        n1_ref[...] = normed.astype(bf16)
        r1_ref[...] = jnp.broadcast_to(inverse, r1_ref.shape)
        mixed_ref[...] = mixed
        add_squares(mixed.astype(f32), 2)

    cols = in_ref.shape[2] // parts
    at = lambda k: slice(cols * k, cols * k + cols)
    bias = in_bias_ref[layer : layer + 1, :].astype(f32)
    pre = dot(mixed_ref[...], in_ref[0, :, at(0)]) + bias[:, at(0)]
    feed = None
    for k in range(parts):
        coming = None
        if k + 1 < parts:
            coming = dot(mixed_ref[...], in_ref[0, :, at(k + 1)]) + bias[:, at(k + 1)]
        act, slope = gelu_and_slope(pre)
        act = act.astype(bf16)
        act_ref[:, at(k)] = act
        slope_ref[:, at(k)] = slope.astype(bf16)
        part = dot(act, out_ref[0, at(k)])
        feed = part if feed is None else feed + part
        pre = coming

    @pl.when(j == 0)
    def _():
        feed_ref[...] = feed

    @pl.when(j > 0)
    def _():
        feed_ref[...] += feed

    @pl.when(j == pl.num_programs(0) - 1)
    def _():
        total = feed_ref[...] + row(ffn_bias_ref, layer)
        add_squares(total, 4)
        normed, inverse = norm_parts(mixed_ref[...].astype(f32) + total)
        out = normed * row(scale_ref, layer, 1) + row(shift_ref, layer, 1)
        add_squares(out, 6)
        n2_ref[...] = normed.astype(bf16)
        r2_ref[...] = jnp.broadcast_to(inverse, r2_ref.shape)
        h_ref[...] = out.astype(bf16)


def feed_fwd(ids, x, gathered, ctx_own, ctx_shared, valid, weights, layer, chunk=768, parts=3):
    w_out, out_bias, ln_scale, ln_shift, ffn_in, ffn_in_bias, ffn_out, ffn_out_bias = weights
    half, width = x.shape[1], x.shape[2]
    tokens, ff = 3 * half, ffn_in.shape[2]
    full = lambda *shape: spec(shape, *([0] * len(shape)))
    dense = ((tokens, width), bf16)
    column = ((tokens, 128), f32)
    outs = [dense, column, dense, column, dense, ((tokens, ff), bf16), ((tokens, ff), bf16), dense,
            ((8, width), f32)]
    out_specs = [full(*s) for s, _ in outs]
    out_specs[5] = out_specs[6] = spec((tokens, chunk), 0, step)
    return call(
        functools.partial(feed_fwd_kernel, layer=layer, parts=parts), "feed_forward", (ff // chunk,), ids,
        row_tiles(half, width, gathered)
        + [
            full(*ctx_own.shape), full(*ctx_shared.shape), spec((tokens, 128), 0, 0),
            spec((1, width, width), layer, 0, 0), full(*out_bias.shape), full(*ln_scale.shape),
            full(*ln_shift.shape), spec((1, width, chunk), layer, 0, step),
            spec((ffn_in_bias.shape[0], chunk), 0, step), spec((1, chunk, width), layer, step, 0),
            full(*ffn_out_bias.shape),
        ],
        [x, x, x, ctx_own, ctx_shared, valid, w_out, out_bias, ln_scale, ln_shift, ffn_in, ffn_in_bias,
         ffn_out, ffn_out_bias],
        out_specs, [shape_of(s, d) for s, d in outs], [pltpu.VMEM((tokens, width), f32)],
    )


def feed_bwd_kernel(
    ids, g0, g1, g2, n2_ref, r2_ref, n1_ref, r1_ref, scale_ref, out_ref, slope_ref, in_ref, w_out_ref,
    feed_ref, pre_ref, mixed_ref, attn_ref, ctx_ref, sums_ref, pre_sum_ref,
    res_ref, acc_ref,
    *, layer, parts,
):
    j = pl.program_id(0)
    row = lambda k: scale_ref[layer, k : k + 1, :].astype(f32)

    @pl.when(j == 0)
    def _():
        grad = jnp.concatenate([g0[0], g1[0], g2[0]], 0).astype(f32)
        normed = n2_ref[...].astype(f32)
        sums_ref[1:2, :] = col_sum(grad * normed)
        sums_ref[3:4, :] = col_sum(grad)
        back = norm_back(grad, row(1), normed, r2_ref[:, 0:1])
        res_ref[...] = back
        feed = back.astype(bf16)
        feed_ref[...] = feed
        sums_ref[5:6, :] = col_sum(feed.astype(f32))
        sums_ref[6:8, :] = jnp.zeros((2, sums_ref.shape[1]), f32)

    cols = slope_ref.shape[1] // parts
    at = lambda k: slice(cols * k, cols * k + cols)
    g_act = dot_nt(feed_ref[...], out_ref[0, at(0)])
    total = None
    for k in range(parts):
        coming = dot_nt(feed_ref[...], out_ref[0, at(k + 1)]) if k + 1 < parts else None
        g_pre = (g_act * slope_ref[:, at(k)].astype(f32)).astype(bf16)
        pre_ref[:, at(k)] = g_pre
        pre_sum_ref[:, at(k)] = jnp.broadcast_to(col_sum(g_pre.astype(f32)), (8, cols))
        part = dot_nt(g_pre, in_ref[0, :, at(k)])
        total = part if total is None else total + part
        g_act = coming

    @pl.when(j == 0)
    def _():
        acc_ref[...] = total

    @pl.when(j > 0)
    def _():
        acc_ref[...] += total

    @pl.when(j == pl.num_programs(0) - 1)
    def _():
        g_mixed = acc_ref[...] + res_ref[...]
        mixed_ref[...] = g_mixed.astype(bf16)
        normed = n1_ref[...].astype(f32)
        sums_ref[0:1, :] = col_sum(g_mixed * normed)
        sums_ref[2:3, :] = col_sum(g_mixed)
        attn = norm_back(g_mixed, row(0), normed, r1_ref[:, 0:1]).astype(bf16)
        attn_ref[...] = attn
        sums_ref[4:5, :] = col_sum(attn.astype(f32))
        ctx_ref[...] = dot_nt(attn, w_out_ref[0]).astype(bf16)


def feed_bwd(ids, grad, gathered, kept, slope, weights, layer, chunk=768, parts=3):
    w_out, out_bias, ln_scale, ln_shift, ffn_in, ffn_in_bias, ffn_out, ffn_out_bias = weights
    n1, r1, n2, r2 = kept
    half, width = grad.shape[1], grad.shape[2]
    tokens, ff = 3 * half, ffn_in.shape[2]
    full = lambda *shape: spec(shape, *([0] * len(shape)))
    dense = ((tokens, width), bf16)
    outs = [dense, ((tokens, ff), bf16), dense, dense, dense, ((8, width), f32), ((8, ff), f32)]
    out_specs = [full(*s) for s, _ in outs]
    out_specs[1] = spec((tokens, chunk), 0, step)
    out_specs[6] = spec((8, chunk), 0, step)
    return call(
        functools.partial(feed_bwd_kernel, layer=layer, parts=parts), "feed_backward", (ff // chunk,), ids,
        row_tiles(half, width, gathered)
        + [
            full(tokens, width), full(tokens, 128), full(tokens, width), full(tokens, 128),
            full(*ln_scale.shape), spec((1, chunk, width), layer, step, 0), spec((tokens, chunk), 0, step),
            spec((1, width, chunk), layer, 0, step), spec((1, width, width), layer, 0, 0),
        ],
        [grad, grad, grad, n2, r2, n1, r1, ln_scale, ffn_out, slope, ffn_in, w_out],
        out_specs, [shape_of(s, d) for s, d in outs],
        [pltpu.VMEM((tokens, width), f32), pltpu.VMEM((tokens, width), f32)],
    )


def joint_bwd_kernel(
    ids, own_ref, shared_ref, arrived_ref, w_ref, attn_ref, joint_ref, h_ref, sums_ref, acc_ref,
):
    j = pl.program_id(0)
    far = arrived_ref[0].astype(f32) * (j > 0).astype(f32)
    near = (shared_ref[0].astype(f32) + far).astype(bf16)
    joint = jnp.concatenate([own_ref[0], near], 0)
    joint_ref[...] = joint
    part = dot_nt(joint, w_ref[0])
    sums_ref[...] = jnp.broadcast_to(col_sum(joint.astype(f32)), sums_ref.shape)

    @pl.when(j == 0)
    def _():
        acc_ref[...] = part + attn_ref[...].astype(f32)

    @pl.when(j > 0)
    def _():
        acc_ref[...] += part

    @pl.when(j == pl.num_programs(0) - 1)
    def _():
        h_ref[...] = acc_ref[...].astype(bf16)


def joint_bwd(ids, own, shared, arrived, w_qkv, g_attn, layer):
    _, length, width = own.shape
    half = shared.shape[1]
    tokens = length + half
    full = lambda *shape: spec(shape, *([0] * len(shape)))
    return call(
        joint_bwd_kernel, "projections_backward", (3,), ids,
        [
            spec((1, length, width), step, 0, 0), spec((1, half, width), step, 0, 0),
            spec((1, half, width), lambda i, ids: jnp.maximum(i - 1, 0), 0, 0),
            spec((1, width, width), layer, 0, step), full(tokens, width),
        ],
        [own, shared, arrived, w_qkv, g_attn],
        [spec((tokens, width), 0, step), full(tokens, width), spec((8, width), 0, step)],
        [
            shape_of((tokens, 3 * width), bf16), shape_of((tokens, width), bf16),
            shape_of((8, 3 * width), f32),
        ],
        [pltpu.VMEM((tokens, width), f32)],
    )


def slab_place(ids, slab):
    relative = jnp.bitwise_xor(ids[2], slab)
    return (
        jnp.bitwise_or(
            jnp.left_shift(jnp.bitwise_and(relative, 1), 2),
            jnp.bitwise_or(jnp.bitwise_and(relative, 2), jnp.right_shift(relative, 2)),
        )
    )


def store_piece(ids, keep_ref, send_ref, slab, core_rows, row, value):
    place = slab_place(ids, slab)
    core = ids[0]
    low, high = value[0:core_rows], value[core_rows:]
    at = slice(row, row + core_rows)

    @pl.when(core == 0)
    def _():
        keep_ref[place, at, :], send_ref[place, at, :] = low, high

    @pl.when(core != 0)
    def _():
        keep_ref[place, at, :], send_ref[place, at, :] = high, low


def feed_weights_kernel(ids, act_ref, feed_ref, mixed_ref, pre_ref, keep_ref, send_ref, feed_t, mixed_t):
    i = pl.program_id(0)

    @pl.when(i == 0)
    def _():
        feed_t[...] = feed_ref[...].T
        mixed_t[...] = mixed_ref[...].T

    slabs = act_ref.shape[1] // LANES
    out_steps = SUPER // slabs

    for s in range(out_steps):
        @pl.when(i == s)
        def _():
            result = dot(feed_t[...], act_ref[...]).astype(bf16)
            for k in range(slabs):
                store_piece(ids, keep_ref, send_ref, s * slabs + k, LANES // 2, 0,
                            result[:, LANES * k : LANES * k + LANES])

    groups = pre_ref.shape[1] // LANES
    rows = mixed_t.shape[0] // SUPER
    for s in range(4 // groups):
        @pl.when(i == out_steps + s)
        def _():
            result = dot(mixed_t[...], pre_ref[...]).astype(bf16)
            for slab in range(SUPER):
                for k in range(groups):
                    store_piece(
                        ids, keep_ref, send_ref, slab, rows // 2,
                        LANES // 2 + (s * groups + k) * (rows // 2),
                        result[rows * slab : rows * slab + rows, LANES * k : LANES * k + LANES],
                    )


def feed_weights(ids, act, g_feed, mixed, g_pre):
    tokens, width = mixed.shape
    block = 2 * LANES
    piece = (SUPER, LANES, LANES)
    full = lambda *shape: spec(shape, *([0] * len(shape)))
    return call(
        feed_weights_kernel, "feed_weights", (6,), ids,
        [
            spec((tokens, block), 0, lambda i, ids: jnp.minimum(i, 3)),
            spec((tokens, LANES), 0, lambda i, ids: ids[1]),
            full(tokens, width),
            spec((tokens, block), 0, lambda i, ids: 2 * ids[1] + jnp.maximum(i - 4, 0)),
        ],
        [act, g_feed, mixed, g_pre],
        [full(*piece), full(*piece)], [shape_of(piece, bf16), shape_of(piece, bf16)],
        [pltpu.VMEM((LANES, tokens), bf16), pltpu.VMEM((width, tokens), bf16)],
    )


def attention_weights_kernel(
    ids, x0, x1, x2, joint_ref, own_ref, shared_ref, attn_ref, rel0_ref, rel1_ref, small_ref,
    keep_ref, send_ref,
):
    x_t = jnp.concatenate([x0[0].T, x1[0].T, x2[0].T], 1)
    width = x_t.shape[0]
    rows = width // SUPER
    half = rows // 2
    groups = joint_ref.shape[1] // LANES
    for g in range(groups):
        result = dot(x_t, joint_ref[:, LANES * g : LANES * g + LANES]).astype(bf16)
        for slab in range(SUPER):
            store_piece(ids, keep_ref, send_ref, slab, half, g * half,
                        result[rows * slab : rows * slab + rows])
    long = own_ref.shape[1]
    result = dot(own_ref[...], attn_ref[0:long]) + dot(shared_ref[...], attn_ref[long:])
    result = result.astype(bf16)
    for slab in range(SUPER):
        store_piece(ids, keep_ref, send_ref, slab, half, groups * half,
                    result[rows * slab : rows * slab + rows])
    rel = (rel0_ref[...] + rel1_ref[...]).astype(bf16)
    count = rel.shape[0] // SUPER
    for slab in range(SUPER):
        both = jnp.concatenate([rel[count * slab : count * slab + count], small_ref[slab]], 0)
        store_piece(ids, keep_ref, send_ref, slab, count, (groups + 1) * half, both)


def attention_weights(ids, x, gathered, g_joint, ctx_own, ctx_shared, g_attn, rel0, rel1, small):
    half, width = x.shape[1], x.shape[2]
    tokens = 3 * half
    rows = (width // SUPER // 2) * 4 + rel0.shape[0] // SUPER
    piece = (SUPER, rows, LANES)
    side = lambda i, ids: ids[1]
    full = lambda *shape: spec(shape, *([0] * len(shape)))
    return call(
        attention_weights_kernel, "attention_weights", (1,), ids,
        row_tiles(half, width, gathered)
        + [
            spec((tokens, 3 * LANES), 0, side), full(*ctx_own.shape), full(*ctx_shared.shape),
            spec((tokens, LANES), 0, side), spec((rel0.shape[0], LANES), 0, side),
            spec((rel0.shape[0], LANES), 0, side), full(*small.shape),
        ],
        [x, x, x, g_joint, ctx_own, ctx_shared, g_attn, rel0, rel1, small],
        [full(*piece), full(*piece)], [shape_of(piece, bf16), shape_of(piece, bf16)],
    )


def place_rows_kernel(ids, own_ref, other_ref, out_ref):
    i = pl.program_id(0)
    core = ids[0]
    row = i // 2
    mine = jnp.where(row == 2, (i - 4) == core, row == core)

    @pl.when(mine)
    def _():
        out_ref[0] = own_ref[0].astype(out_ref.dtype)

    @pl.when(jnp.logical_not(mine))
    def _():
        out_ref[0] = other_ref[0].astype(out_ref.dtype)


def place_rows(ids, own, other, dtype):
    tokens, width = own.shape
    half = tokens // 3
    tile = lambda i, ids: jnp.where(i < 4, i % 2, 2)
    tiles = lambda x: x.reshape(3, half, width)
    return call(
        place_rows_kernel, "place_rows", (6,), ids,
        [spec((1, half, width), tile, 0, 0)] * 2, [tiles(own), tiles(other)],
        spec((1, half, width), step, 0, 0), shape_of((6, half, width), dtype),
    )


def body(
    stream, cotangent, segments, word_boxes, valid_mask, w_qkv, qv_bias, w_out, out_bias, rel_proj,
    ln_scale, ln_shift, ffn_in, ffn_in_bias, ffn_out, ffn_out_bias,
):
    sections = lax.axis_size("section")
    dp = lax.axis_size("dp")
    section = lax.axis_index("section")
    dp_index = lax.axis_index("dp")
    core, side = section % 2, section // 2
    rows, length, width = stream.shape
    layers = w_qkv.shape[0]
    ff = ffn_in.shape[2]
    half = length // 2
    assert rows == 3 and sections == 4 and layers == 2 and dp % SUPER == 0 and width == 2 * LANES
    fine = dp // SUPER
    ids = jnp.stack([core, side, dp_index // fine]).astype(jnp.int32)
    weights = (w_out, out_bias, ln_scale, ln_shift, ffn_in, ffn_in_bias, ffn_out, ffn_out_bias)
    rel_pairs = rel_proj.reshape(layers, width // 128, 128, 128)

    def flip(x, bit):
        return lax.ppermute(x, "section", [(i, i ^ bit) for i in range(sections)])

    def flip_dp(x, bit):
        return lax.ppermute(x, "dp", [(i, i ^ bit) for i in range(dp)])

    tables = make_tables(ids, word_boxes, segments, valid_mask)
    ctab, stab, valid_col = tables[3], tables[4], tables[7]

    halves = lambda x: x.reshape(-1, half, width)
    x, gathered = halves(stream), True
    kept = []
    for l in range(layers):
        joint, turned, kv = project(ids, x, gathered, w_qkv, qv_bias, rel_pairs, ctab, stab, l)
        kv_far = flip(kv, 1)
        ctx_own, lse_own = attention_fwd(ids, False, tables, joint, turned, None)
        ctx_shared, lse_shared = attention_fwd(ids, True, tables, joint, turned, kv_far)
        n1, r1, n2, r2, mixed, act, slope, out, squares = feed_fwd(
            ids, x, gathered, ctx_own, ctx_shared, valid_col, weights, l
        )
        kept.append(
            dict(x=x, gathered=gathered, joint=joint, turned=turned, kv_far=kv_far, ctx_own=ctx_own,
                 ctx_shared=ctx_shared, lse_own=lse_own, lse_shared=lse_shared, norms=(n1, r1, n2, r2),
                 mixed=mixed, act=act, slope=slope, out=out, squares=squares)
        )
        x, gathered = halves(out), False

    def reduce_start(keep, send):
        return keep + flip(send, 1)

    def reduce_rest(x):
        for bit in range(3):
            n = x.shape[0] // 2
            x = x[:n] + flip_dp(x[n:], fine << bit)
        x = x[0]
        bit = 1
        while bit < fine:
            x = x + flip_dp(x, bit)
            bit *= 2
        return x

    grad, gathered = halves(cotangent), True
    sums = {}
    for l in reversed(range(layers)):
        k = kept[l]
        g_feed, g_pre, g_mixed, g_attn, g_ctx, vec, pre_sum = feed_bwd(
            ids, grad, gathered, k["norms"], k["slope"], weights, l
        )
        keep, send = feed_weights(ids, k["act"], g_feed, k["mixed"], g_pre)
        sums[l, "feed"] = reduce_rest(reduce_start(keep, send))
        shared_keep, shared_send, rel_shared = attention_bwd(
            ids, True, tables, k["joint"], k["turned"], k["kv_far"], k["lse_shared"], g_ctx, rel_pairs, l
        )
        arrived = flip(shared_send, 1)
        own_grads, rel_own = attention_bwd(
            ids, False, tables, k["joint"], k["turned"], None, k["lse_own"], g_ctx, rel_pairs, l
        )
        g_joint, g_h, joint_sum = joint_bwd(ids, own_grads, shared_keep, arrived, w_qkv, g_attn, l)
        vectors = jnp.concatenate([vec, joint_sum[0:1, :width], joint_sum[0:1, 2 * width :]], 0)
        order = [8, 9, 4, 0, 1, 2, 3, 5]
        lines = jnp.stack([vectors[i] for i in order]).reshape(8, SUPER, width // SUPER)
        lines = jnp.pad(jnp.transpose(lines, (1, 0, 2)), ((0, 0), (0, 0), (0, LANES - width // SUPER)))
        lines = jnp.concatenate([lines, pre_sum[0].reshape(SUPER, 1, ff // SUPER)], 1)
        small = jnp.pad(lines, ((0, 0), (0, 16 - 9), (0, 0))).astype(bf16)
        keep, send = attention_weights(
            ids, k["x"], k["gathered"], g_joint, k["ctx_own"], k["ctx_shared"], g_attn, rel_own,
            rel_shared, small,
        )
        sums[l, "attention"] = reduce_rest(reduce_start(keep, send))
        k["g_mixed"], k["g_h"] = g_mixed, g_h
        grad, gathered = halves(g_h), False

    def of_layer(name):
        return jnp.where(side == 0, kept[0][name], kept[1][name])

    def to_section(first, second, dtype):
        a, b = of_layer(first), of_layer(second)
        own, away = jnp.where(core == 0, a, b), jnp.where(core == 0, b, a)
        return place_rows(ids, own, flip(away, 1), dtype).reshape(1, rows, length, width)

    section_outs = to_section("mixed", "out", bf16)
    in_grads = to_section("g_h", "g_mixed", f32)

    squares_mine = jnp.sum(of_layer("squares"), 1).reshape(2, 2, 2)
    squares_far = flip(squares_mine, 1)
    sub = lambda v: lax.dynamic_index_in_dim(v, core, 0, keepdims=False)
    near, far = sub(squares_mine), sub(squares_far)
    first = jnp.where(core == 0, near[:, 0], far[:, 0])
    second = jnp.where(core == 0, far[:, 0], near[:, 0])
    square_rows = jnp.stack([first, second, near[:, 1] + far[:, 1]])
    row_counts = jnp.sum(valid_mask.astype(f32), 1)
    root_mean_squares = jnp.sqrt(square_rows / (width * jnp.maximum(row_counts, 1.0))[:, None])[None]

    fine_at = dp_index % fine
    core_rows = width // SUPER // 2
    found = {}
    for l in range(layers):
        piece = jnp.concatenate([sums[l, "feed"], sums[l, "attention"]], 0)
        far = flip(piece, 2)
        sides = [jnp.where(side == 0, piece, far), jnp.where(side == 0, far, piece)]
        both = jnp.stack(sides)
        other = flip(both, 1)
        found[l] = jnp.where(core == 0, jnp.stack([both, other]), jnp.stack([other, both])).astype(f32)

    def fine_part(x, axis):
        n = x.shape[axis] // fine
        return x if fine == 1 else lax.dynamic_slice_in_dim(x, fine_at * n, n, axis)

    def gather(l):
        x = found[l]
        ffn_out_t = x[:, :, : LANES // 2]
        d_ffn_out = jnp.transpose(ffn_out_t, (3, 1, 0, 2)).reshape(LANES, width)
        at = LANES // 2

        def columns(at, groups):
            part = x[:, :, at : at + groups * core_rows].reshape(2, 2, groups, core_rows, LANES)
            part = jnp.transpose(part, (0, 3, 1, 2, 4))
            return part.reshape(2 * core_rows, 2 * groups * LANES)

        d_ffn_in = columns(at, 4)
        at += 4 * core_rows
        d_qkv = columns(at, 3)
        at += 3 * core_rows
        d_out = columns(at, 1)
        at += core_rows
        rel = jnp.concatenate([x[0, 0, at:], x[0, 1, at:]], 1)
        small = x[1, 0, at:]
        return (
            fine_part(d_qkv, 0), small, fine_part(d_out, 0),
            fine_part(rel.T, 1).reshape(width // 64, 64, -1), fine_part(d_ffn_in, 0),
            fine_part(d_ffn_out, 0),
        )

    parts = [gather(l) for l in range(layers)]
    stacked = [jnp.stack(pair) for pair in zip(*parts)]
    d_qkv, small, d_out, d_rel, d_ffn_in, d_ffn_out = stacked
    vector = lambda i: fine_part(small[:, i, : width // SUPER], 1)
    return (
        section_outs,
        in_grads,
        d_qkv,
        jnp.stack([vector(0), vector(1)], 1),
        d_out,
        vector(2),
        d_rel,
        jnp.stack([vector(3), vector(4)], 1),
        jnp.stack([vector(5), vector(6)], 1),
        d_ffn_in,
        fine_part(small[:, 8], 1),
        d_ffn_out,
        vector(7),
        root_mean_squares,
    )


def solution(mesh):
    return jax.shard_map(
        body,
        mesh=mesh,
        in_specs=(
            P("dp", None, None),
            P("dp", None, None),
            P("dp", None),
            P(None, "dp", None),
            P("dp", None),
        )
        + (P(),) * 11,
        out_specs=(
            P("section", "dp", None, None),
            P("section", "dp", None, None),
            P(None, "dp", None),
            P(None, None, "dp"),
            P(None, "dp", None),
            P(None, "dp"),
            P(None, None, None, "dp"),
            P(None, None, "dp"),
            P(None, None, "dp"),
            P(None, "dp", None),
            P(None, "dp"),
            P(None, "dp", None),
            P(None, "dp"),
            P("section", "dp", None),
        ),
        check_vma=False,
    )
```

```python
import functools

import jax
import jax.numpy as jnp
from jax import lax
from jax.experimental import pallas as pl
from jax.experimental.pallas import tpu as pltpu
from jax.sharding import PartitionSpec as P

ln_eps = 1e-05
masked_score = -1e30
bf16 = jnp.bfloat16
f32 = jnp.float32
MB = 1 << 20
SUPER = 8
LANES = 384
NORM_ROWS = 64

ERF_COEFS = (
    0.7978849414899046, 0.0363330844086688, -3.259474462099993e-05, -5.5306316685416947e-05,
    3.964773125473232e-06, -1.322662757755248e-07, 1.7562773256476674e-09,
)


def dot(a, b):
    return lax.dot_general(a, b, (((1,), (0,)), ((), ())), preferred_element_type=f32)


def dot_nt(a, b):
    return lax.dot_general(a, b, (((1,), (1,)), ((), ())), preferred_element_type=f32)


def gelu_and_slope(x):
    square = x * x
    g = ERF_COEFS[-1]
    for c in ERF_COEFS[-2::-1]:
        g = g * square + c
    phi = 0.5 * jnp.tanh(x * g) + 0.5
    density = jnp.exp2(square * (-0.5 * 1.4426950408889634)) * 0.3989422804014327
    return x * phi, phi + x * density


def norm_parts(residual):
    average = jnp.mean(residual, -1, keepdims=True)
    centered = residual - average
    inverse = lax.rsqrt(jnp.mean(centered * centered, -1, keepdims=True) + ln_eps)
    return centered * inverse, inverse


def norm_back(gradient, gain, normed, inverse):
    dnormed = gradient * gain
    return inverse * (
        dnormed
        - jnp.mean(dnormed, -1, keepdims=True)
        - normed * jnp.mean(dnormed * normed, -1, keepdims=True)
    )


def row_loop(count, chunk, sums):
    for i in range(count):
        sums = chunk(i, sums)
    return sums


def fold(x):
    return jnp.sum(x.reshape(-1, 8, x.shape[1]), 0)


def col_sum(x):
    return jnp.sum(x, 0, keepdims=True)


COST_US = dict(
    tables=4, projections=8, attention_forward=7, feed_forward=24, feed_backward=30, attention_backward=12,
    projections_backward=12, place_rows=4,
    unpack_feed=4, unpack_attention=3,
)


def call(kernel, name, grid, ids, in_specs, inputs, out_specs, out_shape, scratch=()):
    cost = pl.CostEstimate(flops=COST_US[name] * 1100000000, bytes_accessed=COST_US[name] * 1000000, transcendentals=0)
    return pl.pallas_call(
        kernel,
        grid_spec=pltpu.PrefetchScalarGridSpec(
            num_scalar_prefetch=1,
            grid=grid,
            in_specs=in_specs,
            out_specs=out_specs,
            scratch_shapes=list(scratch),
        ),
        out_shape=out_shape,
        compiler_params=pltpu.CompilerParams(vmem_limit_bytes=62 * MB),
        cost_estimate=cost,
        name=name,
    )(ids, *inputs)


def spec(shape, *index):
    def index_map(i, ids):
        return tuple(x(i, ids) if callable(x) else x for x in index)

    return pl.BlockSpec(shape, index_map)


def shape_of(shape, dtype):
    return jax.ShapeDtypeStruct(shape, dtype)


step = lambda i, ids: i


def row_tiles(half, width, gathered):
    if not gathered:
        return [spec((1, half, width), t, 0, 0) for t in range(3)]
    core = lambda ids: ids[0]
    return [
        spec((1, half, width), lambda i, ids: 2 * core(ids), 0, 0),
        spec((1, half, width), lambda i, ids: 2 * core(ids) + 1, 0, 0),
        spec((1, half, width), lambda i, ids: 4 + core(ids), 0, 0),
    ]


def tables_kernel(
    ids, boxes_ref, seg_ref, valid_ref,
    cos_ref, sin_ref, kf_ref, ctab_ref, stab_ref, code_ref, segrow_ref, valid_col_ref,
):
    core = ids[0]
    length = seg_ref.shape[1]
    half = length // 2

    def ordered(read):
        near = pl.multiple_of(core * half, half)
        far = pl.multiple_of((1 - core) * half, half)
        return jnp.concatenate(
            [read(pl.ds(core, 1), slice(None)), read(2, pl.ds(near, half)), read(2, pl.ds(far, half))], 1
        )

    def row_of(ref):
        def read(r, c):
            r = pl.ds(2, 1) if isinstance(r, int) else r
            return ref[r, c]
        return ordered(read)

    count = length * 2
    at = lax.broadcasted_iota(jnp.int32, (1, count), 1)
    shared = jnp.where(
        at < length + half, at - length + core * half, at - length - half + (1 - core) * half
    )
    position = jnp.where(at < length, at, shared).astype(f32)
    rate_at = lax.broadcasted_iota(jnp.int32, (32, 1), 0).astype(f32)
    text = position * jnp.exp(rate_at * (-9.210340371976184 / 32))
    box_rate = jnp.exp2(-lax.broadcasted_iota(jnp.int32, (8, 1), 0).astype(f32))
    angles = [text]
    for c in range(4):
        coords = row_of(boxes_ref.at[c]).astype(f32)
        angles.append(coords * box_rate)
    angles = jnp.concatenate(angles, 0)
    cosines, sines = jnp.cos(angles), jnp.sin(angles)
    cos_ref[...], sin_ref[...] = cosines, sines
    kf_ref[...] = jnp.concatenate([cosines, sines], 0).T.astype(bf16)
    ctab_ref[...] = jnp.concatenate([cosines, -cosines], 0).T
    stab_ref[...] = jnp.concatenate([sines, sines], 0).T
    seg = row_of(seg_ref).astype(f32)
    valid = row_of(valid_ref).astype(f32)
    segrow_ref[...] = jnp.broadcast_to(seg, segrow_ref.shape)
    code_ref[...] = jnp.broadcast_to(jnp.where(valid > 0, seg, -1.0), (128, count)).T
    valid_col_ref[...] = jnp.broadcast_to(valid, (128, count)).T


def make_tables(ids, word_boxes, segments, valid_mask):
    length = segments.shape[1]
    count = 2 * length
    full = lambda *shape: spec(shape, *([0] * len(shape)))
    outs = [
        ((64, count), f32), ((64, count), f32), ((count, 128), bf16), ((count, 128), f32),
        ((count, 128), f32), ((count, 128), f32), ((8, count), f32), ((count, 128), f32),
    ]
    return call(
        tables_kernel, "tables", (1,), ids,
        [full(*word_boxes.shape), full(*segments.shape), full(*valid_mask.shape)],
        [word_boxes, segments, valid_mask],
        [full(*s) for s, _ in outs], [shape_of(s, d) for s, d in outs],
    )


def qkv_kernel(
    ids, x0, x1, x2, w_ref, bias_ref, rel_ref, ctab_ref, stab_ref, joint_ref, turned_ref, kv_ref, x_ref,
    *, layer,
):
    j = pl.program_id(0)
    half = x0.shape[1]

    @pl.when(j == 0)
    def _():
        x_ref[0:half], x_ref[half : 2 * half], x_ref[2 * half :] = x0[0], x1[0], x2[0]

    flags = [(j == 0).astype(f32), (j == 2).astype(f32)]
    bias = bias_ref[layer, 0:1, :].astype(f32) * flags[0] + bias_ref[layer, 1:2, :].astype(f32) * flags[1]
    joint = (dot(x_ref[...], w_ref[0]) + bias).astype(bf16)
    joint_ref[...] = joint
    kv_ref[...] = joint[2 * half :]

    @pl.when(j == 0)
    def _():
        ctab, stab = ctab_ref[...], stab_ref[...]
        row = lax.broadcasted_iota(jnp.int32, (128, 128), 0)
        for p in range(rel_ref.shape[1]):
            rel = rel_ref[0, p]
            zero = jnp.zeros_like(rel)
            block = jnp.concatenate([jnp.where(row < 64, rel, zero), jnp.where(row < 64, zero, rel)], 1)
            coef = dot(joint[:, 128 * p : 128 * p + 128], block)
            for e in range(2):
                c = coef[:, 128 * e : 128 * e + 128]
                at = 256 * p + 128 * e
                turned_ref[:, at : at + 128] = (c * ctab + pltpu.roll(c, 64, 1) * stab).astype(bf16)


def project(ids, x, gathered, w_qkv, qv_bias, rel_pairs, ctab, stab, layer):
    half, width = x.shape[1], x.shape[2]
    tokens = 3 * half
    pairs = rel_pairs.shape[1]
    return call(
        functools.partial(qkv_kernel, layer=layer), "projections", (3,), ids,
        row_tiles(half, width, gathered)
        + [
            spec((1, width, width), layer, 0, step), spec(qv_bias.shape, 0, 0, 0),
            spec((1, pairs, 128, 128), layer, 0, 0, 0), spec((tokens, 128), 0, 0),
            spec((tokens, 128), 0, 0),
        ],
        [x, x, x, w_qkv, qv_bias, rel_pairs, ctab, stab],
        [
            spec((tokens, width), 0, step), spec((tokens, 2 * width), 0, 0),
            spec((half, width), 0, lambda i, ids: jnp.maximum(i - 1, 0)),
        ],
        [
            shape_of((tokens, 3 * width), bf16), shape_of((tokens, 2 * width), bf16),
            shape_of((half, 2 * width), bf16),
        ],
        [pltpu.VMEM((tokens, width), bf16)],
    )


def lane_half(shape, half):
    lane = lax.broadcasted_iota(jnp.int32, shape, 1)
    return (lane < 64) if half == 0 else (lane >= 64)


def only_half(x, half):
    return jnp.where(lane_half(x.shape, half), x, jnp.zeros_like(x))


def fill_bias(code_ref, seg_ref, bias_ref):
    shape = bias_ref.shape
    code = jnp.concatenate([code_ref[...]] * (shape[1] // 128), 1)
    same = code == seg_ref[0:1, :]
    key_at = lax.broadcasted_iota(jnp.int32, shape, 0)
    query_at = lax.broadcasted_iota(jnp.int32, shape, 1)
    bias_ref[...] = jnp.where(same | (key_at == query_at), 0.0, masked_score)


def attention_fwd_kernel(
    ids, code_ref, seg_ref, kf_ref, q_ref, turned_ref, k_ref, v_ref, *rest, per_step, shared,
):
    if shared:
        k_far, v_far, ctx_ref, lse_ref, bias_ref, k_all, v_all = rest
        half = k_ref.shape[0]
        k_all[0:half], k_all[half:] = k_ref[...], k_far[...]
        v_all[0:half], v_all[half:] = v_ref[...], v_far[...]
        k_ref, v_ref = k_all, v_all
    else:
        ctx_ref, lse_ref, bias_ref = rest

    @pl.when(pl.program_id(0) == 0)
    def _():
        fill_bias(code_ref, seg_ref, bias_ref)

    scale = jnp.asarray(0.125, bf16)
    units = [(pair, e) for pair in range(per_step) for e in range(2)]
    values_t = {}

    def scores_of(unit):
        pair, e = unit
        at = slice(128 * pair, 128 * pair + 128)
        turned = turned_ref[:, 256 * pair + 128 * e : 256 * pair + 128 * e + 128]
        qside = jnp.concatenate([turned, only_half(q_ref[:, at], e)], 1) * scale
        kside = jnp.concatenate([kf_ref[...], k_ref[:, at]], 1)
        return dot_nt(kside, qside) + bias_ref[...]

    def finish(unit, scores):
        pair, e = unit
        top = jnp.max(scores, 0, keepdims=True)
        expo = jnp.exp(scores - top)
        total = jnp.sum(expo, 0, keepdims=True)
        if pair not in values_t:
            values_t[pair] = v_ref[:, 128 * pair : 128 * pair + 128].T
        ctx = dot(values_t[pair][64 * e : 64 * e + 64], expo.astype(bf16))
        at = 128 * pair + 64 * e
        ctx_ref[at : at + 64, :] = (ctx * (1.0 / total)).astype(bf16)
        lse_ref[pair, e : e + 1, :] = top + jnp.log(total)

    scores = scores_of(units[0])
    for i, unit in enumerate(units):
        upcoming = scores_of(units[i + 1]) if i + 1 < len(units) else None
        finish(unit, scores)
        scores = upcoming


def attention_fwd(ids, shared, tables, joint, turned, kv_far, per_step=2):
    cos_t, sin_t, kf, ctab, stab, code, seg, valid = tables
    tokens, width = joint.shape[0], joint.shape[1] // 3
    half = tokens // 3
    nk = 2 * half
    nq = half if shared else nk
    key_rows = half if shared else nk
    lanes = 128 * per_step
    steps = width // lanes
    q_row = 2 if shared else 0
    at = lambda off: (lambda i, ids: i + off)
    in_specs = [
        spec((nk, 128), int(shared), 0), spec((8, nq), 0, q_row), spec((nk, 128), int(shared), 0),
        spec((nq, lanes), q_row, step), spec((nq, 2 * lanes), q_row, step),
        spec((key_rows, lanes), q_row, at(steps)), spec((key_rows, lanes), q_row, at(2 * steps)),
    ]
    inputs = [code, seg, kf, joint, turned, joint, joint]
    scratch = [pltpu.VMEM((nk, nq), f32)]
    if shared:
        in_specs += [spec((half, lanes), 0, step), spec((half, lanes), 0, at(steps))]
        inputs += [kv_far, kv_far]
        scratch += [pltpu.VMEM((nk, lanes), bf16)] * 2
    return call(
        functools.partial(attention_fwd_kernel, per_step=per_step, shared=shared),
        "attention_forward", (steps,), ids, in_specs, inputs,
        [spec((lanes, nq), step, 0), spec((per_step, 2, nq), step, 0, 0)],
        [shape_of((width, nq), bf16), shape_of((width // 128, 2, nq), f32)],
        scratch,
    )


def attention_bwd_kernel(
    ids, code_ref, seg_ref, kf_ref, cos_ref, sin_ref, rel_ref, lse_ref, gc_ref, q_ref, turned_ref,
    k_ref, v_ref, *rest, per_step, shared,
):
    if shared:
        k_far, v_far, keep_ref, send_ref, drel_ref, bias_ref, kft_ref, k_all, v_all = rest
        half = k_ref.shape[0]
        k_all[0:half], k_all[half:] = k_ref[...], k_far[...]
        v_all[0:half], v_all[half:] = v_ref[...], v_far[...]
        k_ref, v_ref = k_all, v_all
    else:
        keep_ref, drel_ref, bias_ref, kft_ref = rest

    @pl.when(pl.program_id(0) == 0)
    def _():
        fill_bias(code_ref, seg_ref, bias_ref)
        kft_ref[...] = kf_ref[...].T

    scale = jnp.asarray(0.125, bf16)
    cosines, sines = cos_ref[...], sin_ref[...]
    units = [(pair, e) for pair in range(per_step) for e in range(2)]
    store = {}

    def scores_of(unit):
        pair, e = unit
        at = slice(128 * pair, 128 * pair + 128)
        q_mine = only_half(q_ref[:, at], e)
        gc_mine = only_half(gc_ref[:, at], e)
        q_scaled = q_mine * scale
        turned = turned_ref[:, 256 * pair + 128 * e : 256 * pair + 128 * e + 128]
        qside = jnp.concatenate([turned * scale, q_scaled], 1)
        kside = jnp.concatenate([kf_ref[...], k_ref[:, at]], 1)
        scores = dot_nt(kside, qside) + bias_ref[...]
        gp = dot_nt(v_ref[:, at], gc_mine)
        return scores, gp, q_mine, gc_mine, q_scaled

    def finish(unit, parts):
        pair, e = unit
        scores, gp, q_mine, gc_mine, q_scaled = parts
        at = slice(128 * pair, 128 * pair + 128)
        shares = jnp.exp(scores - lse_ref[pair, e : e + 1, :])
        dv = dot(shares.astype(bf16), gc_mine)
        weighted = shares * gp
        delta = jnp.sum(weighted, 0, keepdims=True)
        gs = (weighted - shares * delta).astype(bf16)
        dk = dot(gs, q_scaled)
        if pair not in store:
            store[pair] = k_ref[:, at].T
        side_t = jnp.concatenate([kft_ref[...], store[pair][64 * e : 64 * e + 64]], 0)
        dside = dot(side_t, gs) * 0.125
        g_cos, g_sin = dside[0:64], dside[64:128]
        gcoef = jnp.concatenate(
            [g_cos * cosines + g_sin * sines, g_cos * sines - g_sin * cosines], 0
        ).astype(bf16)
        dq = dside[128:192] + dot(rel_ref[0, pair, 64 * e : 64 * e + 64], gcoef)
        drel = dot(gcoef, q_mine)
        if e == 0:
            store["even"] = (dq, dk, dv, drel)
            return
        dq0, dk0, dv0, drel0 = store["even"]
        dq = jnp.concatenate([dq0, dq], 0).T.astype(bf16)
        dk, dv = (dk0 + dk).astype(bf16), (dv0 + dv).astype(bf16)
        drel_ref[:, at] = drel0 + drel
        n = keep_ref.shape[1]
        keep_ref[0, :, at] = dq
        keep_ref[1, :, at], keep_ref[2, :, at] = dk[0:n], dv[0:n]
        if shared:
            send_ref[0, :, at], send_ref[1, :, at] = dk[n:], dv[n:]

    parts = scores_of(units[0])
    for i, unit in enumerate(units):
        upcoming = scores_of(units[i + 1]) if i + 1 < len(units) else None
        finish(unit, parts)
        parts = upcoming


def attention_bwd(ids, shared, tables, joint, turned, kv_far, lse, g_ctx, rel_pairs, layer, split, per_step=2):
    per_step = 1 if split else per_step
    cos_t, sin_t, kf, ctab, stab, code, seg, valid = tables
    tokens, width = joint.shape[0], joint.shape[1] // 3
    half = tokens // 3
    nk = 2 * half
    nq = half if shared else nk
    key_rows = half if shared else nk
    lanes = 128 * per_step
    all_steps = width // lanes
    steps = all_steps // 2 if split else all_steps
    out_width = lanes * steps
    first = lambda ids: ids[1] * steps if split else 0
    q_row = 2 if shared else 0
    at = lambda off: (lambda i, ids: first(ids) + i + off)
    here = at(0)
    in_specs = [
        spec((nk, 128), int(shared), 0), spec((8, nq), 0, q_row), spec((nk, 128), int(shared), 0),
        spec((64, nq), 0, q_row), spec((64, nq), 0, q_row),
        spec((1, per_step, 128, 128), layer, here, 0, 0),
        spec((per_step, 2, nq), here, 0, 0), spec((nq, lanes), q_row, here),
        spec((nq, lanes), q_row, here), spec((nq, 2 * lanes), q_row, here),
        spec((key_rows, lanes), q_row, at(all_steps)), spec((key_rows, lanes), q_row, at(2 * all_steps)),
    ]
    inputs = [code, seg, kf, cos_t, sin_t, rel_pairs, lse, g_ctx, joint, turned, joint, joint]
    scratch = [pltpu.VMEM((nk, nq), f32), pltpu.VMEM((128, nk), bf16)]
    out_specs = [spec((3, key_rows, lanes), 0, 0, step)]
    out_shape = [shape_of((3, key_rows, out_width), bf16)]
    if shared:
        in_specs += [spec((half, lanes), 0, here), spec((half, lanes), 0, at(all_steps))]
        inputs += [kv_far, kv_far]
        scratch += [pltpu.VMEM((nk, lanes), bf16)] * 2
        out_specs.append(spec((2, half, lanes), 0, 0, step))
        out_shape.append(shape_of((2, half, out_width), bf16))
    out_specs.append(spec((128, lanes), 0, step))
    out_shape.append(shape_of((128, out_width), f32))
    return call(
        functools.partial(attention_bwd_kernel, per_step=per_step, shared=shared),
        "attention_backward", (steps,), ids, in_specs, inputs, out_specs, out_shape, scratch,
    )


def feed_fwd_kernel(
    ids, x0, x1, x2, own_ref, shared_ref, valid_ref, w_out_ref, out_bias_ref, scale_ref, shift_ref,
    in_ref, in_bias_ref, out_ref, ffn_bias_ref,
    n1_ref, r1_ref, n2_ref, r2_ref, mixed_ref, act_ref, slope_ref, h_ref, squares_ref,
    feed_ref,
    *, layer, parts,
):
    j = pl.program_id(0)
    half = x0.shape[1]
    row = lambda ref, *at: ref[at[:-1] + (slice(at[-1], at[-1] + 1),)].astype(f32)

    rows = NORM_ROWS
    zero = jnp.zeros((8, x0.shape[2]), f32)

    def add_squares(sums, k, tile):
        for i, x in enumerate(sums):
            at = k + 2 * i + tile // 2
            squares_ref[at : at + 1, :] += col_sum(x)

    @pl.when(j == 0)
    def _():
        ctx = jnp.concatenate([own_ref[...].T, shared_ref[...].T], 0)
        feed_ref[...] = dot(ctx, w_out_ref[0])
        bias, gain, shift = row(out_bias_ref, layer), row(scale_ref, layer, 0), row(shift_ref, layer, 0)
        squares_ref[...] = jnp.zeros_like(squares_ref)
        for t, x_ref in enumerate((x0, x1, x2)):

            def chunk(i, sums):
                at = i * rows
                to = pl.ds(t * half + at, rows)
                valid = valid_ref[to, 0:1]
                attention = feed_ref[to, :] + bias
                normed, inverse = norm_parts(x_ref[0, pl.ds(at, rows), :].astype(f32) + attention)
                mixed = (normed * gain + shift).astype(bf16)
                n1_ref[to, :] = normed.astype(bf16)
                r1_ref[to, :] = jnp.broadcast_to(inverse, (rows, 128))
                mixed_ref[to, :] = mixed
                mixed = mixed.astype(f32)
                return (sums[0] + fold(attention * attention * valid), sums[1] + fold(mixed * mixed * valid))

            sums = row_loop(half // rows, chunk, (zero, zero))
            add_squares(sums, 0, t)

    cols = in_ref.shape[2] // parts
    at = lambda k: slice(cols * k, cols * k + cols)
    bias = in_bias_ref[layer : layer + 1, :].astype(f32)
    pre = dot(mixed_ref[...], in_ref[0, :, at(0)]) + bias[:, at(0)]
    feed = None
    for k in range(parts):
        coming = None
        if k + 1 < parts:
            coming = dot(mixed_ref[...], in_ref[0, :, at(k + 1)]) + bias[:, at(k + 1)]
        act, slope = gelu_and_slope(pre)
        act = act.astype(bf16)
        act_ref[:, at(k)] = act
        slope_ref[:, at(k)] = slope.astype(bf16)
        part = dot(act, out_ref[0, at(k)])
        feed = part if feed is None else feed + part
        pre = coming

    @pl.when(j == 0)
    def _():
        feed_ref[...] = feed

    @pl.when(j > 0)
    def _():
        feed_ref[...] += feed

    @pl.when(j == pl.num_programs(0) - 1)
    def _():
        bias, gain, shift = row(ffn_bias_ref, layer), row(scale_ref, layer, 1), row(shift_ref, layer, 1)
        for t in range(3):

            def chunk(i, sums):
                to = pl.ds(t * half + i * rows, rows)
                valid = valid_ref[to, 0:1]
                branch = feed_ref[to, :] + bias
                normed, inverse = norm_parts(mixed_ref[to, :].astype(f32) + branch)
                out = normed * gain + shift
                n2_ref[to, :] = normed.astype(bf16)
                r2_ref[to, :] = jnp.broadcast_to(inverse, (rows, 128))
                h_ref[to, :] = out.astype(bf16)
                return (sums[0] + fold(branch * branch * valid), sums[1] + fold(out * out * valid))

            sums = row_loop(half // rows, chunk, (zero, zero))
            add_squares(sums, 4, t)


def feed_fwd(ids, x, gathered, ctx_own, ctx_shared, valid, weights, layer, chunk=768, parts=3):
    w_out, out_bias, ln_scale, ln_shift, ffn_in, ffn_in_bias, ffn_out, ffn_out_bias = weights
    half, width = x.shape[1], x.shape[2]
    tokens, ff = 3 * half, ffn_in.shape[2]
    full = lambda *shape: spec(shape, *([0] * len(shape)))
    dense = ((tokens, width), bf16)
    column = ((tokens, 128), f32)
    outs = [dense, column, dense, column, dense, ((tokens, ff), bf16), ((tokens, ff), bf16), dense,
            ((8, width), f32)]
    out_specs = [full(*s) for s, _ in outs]
    out_specs[5] = out_specs[6] = spec((tokens, chunk), 0, step)
    return call(
        functools.partial(feed_fwd_kernel, layer=layer, parts=parts), "feed_forward", (ff // chunk,), ids,
        row_tiles(half, width, gathered)
        + [
            full(*ctx_own.shape), full(*ctx_shared.shape), spec((tokens, 128), 0, 0),
            spec((1, width, width), layer, 0, 0), full(*out_bias.shape), full(*ln_scale.shape),
            full(*ln_shift.shape), spec((1, width, chunk), layer, 0, step),
            spec((ffn_in_bias.shape[0], chunk), 0, step), spec((1, chunk, width), layer, step, 0),
            full(*ffn_out_bias.shape),
        ],
        [x, x, x, ctx_own, ctx_shared, valid, w_out, out_bias, ln_scale, ln_shift, ffn_in, ffn_in_bias,
         ffn_out, ffn_out_bias],
        out_specs, [shape_of(s, d) for s, d in outs], [pltpu.VMEM((tokens, width), f32)],
    )


def slab_place(ids, slab):
    relative = jnp.bitwise_xor(ids[2], slab)
    return (
        jnp.bitwise_or(
            jnp.left_shift(jnp.bitwise_and(relative, 1), 2),
            jnp.bitwise_or(jnp.bitwise_and(relative, 2), jnp.right_shift(relative, 2)),
        )
    )


def store_piece(ids, keep_ref, send_ref, slab, core_rows, row, value):
    place = slab_place(ids, slab)
    core = ids[0]
    low, high = value[0:core_rows], value[core_rows:]
    at = slice(row, row + core_rows)

    @pl.when(core == 0)
    def _():
        keep_ref[place, at, :], send_ref[place, at, :] = low, high

    @pl.when(core != 0)
    def _():
        keep_ref[place, at, :], send_ref[place, at, :] = high, low


def feed_bwd_kernel(
    ids, g0, g1, g2, n2_ref, r2_ref, n1_ref, r1_ref, scale_ref, out_ref, slope_ref, in_ref, w_out_ref,
    act_ref, mixed_in_ref, own_ref, shared_ref,
    mixed_ref, attn_ref, ctx_ref, sums_ref, pre_sum_ref, keep_ref, send_ref,
    res_ref, acc_ref, feed_ref, pre_ref, feed_t, mixed_t,
    *, layer, parts,
):
    j = pl.program_id(0)
    tokens = n2_ref.shape[0]
    gain = lambda k: scale_ref[layer, k : k + 1, :].astype(f32)
    rows = NORM_ROWS

    @pl.when(j == 0)
    def _():
        sums_ref[...] = jnp.zeros_like(sums_ref)
        for t, g_ref in enumerate((g0, g1, g2)):
            count = g_ref.shape[1]

            def chunk(i, sums):
                at = i * rows
                to = pl.ds(t * count + at, rows)
                grad = g_ref[0, pl.ds(at, rows), :].astype(f32)
                normed = n2_ref[to, :].astype(f32)
                back = norm_back(grad, gain(1), normed, r2_ref[to, 0:1])
                res_ref[to, :] = back
                feed = back.astype(bf16)
                feed_ref[to, :] = feed
                return (sums[0] + fold(grad * normed), sums[1] + fold(grad), sums[2] + fold(feed.astype(f32)))

            zero = jnp.zeros((8, n2_ref.shape[1]), f32)
            sums = row_loop(count // rows, chunk, (zero, zero, zero))
            for k, x in zip((1, 3, 5), sums):
                sums_ref[k : k + 1, :] += col_sum(x)
        for side in range(2):

            @pl.when(ids[1] == side)
            def _():
                feed_t[...] = feed_ref[:, LANES * side : LANES * side + LANES].T

        mixed_t[...] = mixed_in_ref[...].T

    cols = slope_ref.shape[1] // parts
    at = lambda k: slice(cols * k, cols * k + cols)
    g_act = dot_nt(feed_ref[...], out_ref[0, at(0)])
    for k in range(parts):
        coming = dot_nt(feed_ref[...], out_ref[0, at(k + 1)]) if k + 1 < parts else None
        g_pre = (g_act * slope_ref[:, at(k)].astype(f32)).astype(bf16)
        pre_ref[:, at(k)] = g_pre
        pre_sum_ref[:, at(k)] = jnp.broadcast_to(col_sum(g_pre.astype(f32)), (8, cols))
        g_act = coming
    total = dot_nt(pre_ref[...], in_ref[0])

    @pl.when(j == 0)
    def _():
        acc_ref[...] = total

    @pl.when(j > 0)
    def _():
        acc_ref[...] += total

    high = LANES // 2
    slabs = act_ref.shape[1] // LANES
    result = dot(feed_t[...], act_ref[...]).astype(bf16)
    for k in range(slabs):
        store_piece(ids, keep_ref, send_ref, j * slabs + k, high, 0, result[:, LANES * k : LANES * k + LANES])
    width = mixed_t.shape[0]
    slab_rows = width // SUPER
    half = slab_rows // 2
    steps = 4 // slabs
    for s in range(2 * steps):

        @pl.when((j == s) & (ids[1] == s // steps))
        def _():
            result = dot(mixed_t[...], pre_ref[...]).astype(bf16)
            for slab in range(SUPER):
                for k in range(slabs):
                    store_piece(
                        ids, keep_ref, send_ref, slab, half, high + ((s % steps) * slabs + k) * half,
                        result[slab_rows * slab : slab_rows * slab + slab_rows, LANES * k : LANES * k + LANES],
                    )

    @pl.when(j == pl.num_programs(0) - 1)
    def _():
        def chunk(i, sums):
            to = pl.ds(i * rows, rows)
            g_mixed = acc_ref[to, :] + res_ref[to, :]
            mixed_ref[to, :] = g_mixed.astype(bf16)
            normed = n1_ref[to, :].astype(f32)
            attn = norm_back(g_mixed, gain(0), normed, r1_ref[to, 0:1]).astype(bf16)
            attn_ref[to, :] = attn
            return (sums[0] + fold(g_mixed * normed), sums[1] + fold(g_mixed), sums[2] + fold(attn.astype(f32)))

        zero = jnp.zeros((8, width), f32)
        sums = row_loop(tokens // rows, chunk, (zero, zero, zero))
        for k, x in zip((0, 2, 4), sums):
            sums_ref[k : k + 1, :] = col_sum(x)
        ctx_ref[...] = dot_nt(attn_ref[...], w_out_ref[0]).astype(bf16)
        long = own_ref.shape[1]
        for side in range(2):

            @pl.when(ids[1] == side)
            def _():
                lanes = slice(LANES * side, LANES * side + LANES)
                result = dot(own_ref[...], attn_ref[0:long, lanes]) + dot(shared_ref[...], attn_ref[long:, lanes])
                result = result.astype(bf16)
                for slab in range(SUPER):
                    store_piece(ids, keep_ref, send_ref, slab, half, high + 4 * half,
                                result[slab_rows * slab : slab_rows * slab + slab_rows])


def feed_bwd(ids, grad, gathered, kept, slope, act, mixed, ctx_own, ctx_shared, weights, layer, chunk=768, parts=3):
    w_out, out_bias, ln_scale, ln_shift, ffn_in, ffn_in_bias, ffn_out, ffn_out_bias = weights
    n1, r1, n2, r2 = kept
    half, width = grad.shape[1], grad.shape[2]
    tokens, ff = 3 * half, ffn_in.shape[2]
    once = lambda *shape: pl.BlockSpec(shape, lambda i, ids: (0,) * len(shape), pipeline_mode=pl.Buffered(1))
    full = lambda *shape: spec(shape, *([0] * len(shape)))
    dense = ((tokens, width), bf16)
    piece = ((SUPER, LANES + width // SUPER // 2, LANES), bf16)
    outs = [dense, dense, dense, ((8, width), f32), ((8, ff), f32), piece, piece]
    out_specs = [full(*s) for s, _ in outs]
    out_specs[4] = spec((8, chunk), 0, step)
    return call(
        functools.partial(feed_bwd_kernel, layer=layer, parts=parts), "feed_backward", (ff // chunk,), ids,
        row_tiles(half, width, gathered)
        + [
            once(tokens, width), once(tokens, 128), once(tokens, width), once(tokens, 128),
            full(*ln_scale.shape), spec((1, chunk, width), layer, step, 0), spec((tokens, chunk), 0, step),
            spec((1, width, chunk), layer, 0, step), spec((1, width, width), layer, 0, 0),
            spec((tokens, chunk), 0, step), once(tokens, width), once(*ctx_own.shape), once(*ctx_shared.shape),
        ],
        [grad, grad, grad, n2, r2, n1, r1, ln_scale, ffn_out, slope, ffn_in, w_out, act, mixed, ctx_own,
         ctx_shared],
        out_specs, [shape_of(s, d) for s, d in outs],
        [
            pltpu.VMEM((tokens, width), f32), pltpu.VMEM((tokens, width), f32),
            pltpu.VMEM((tokens, width), bf16), pltpu.VMEM((tokens, chunk), bf16),
            pltpu.VMEM((LANES, tokens), bf16), pltpu.VMEM((width, tokens), bf16),
        ],
    )


def joint_bwd_kernel(
    ids, x0, x1, x2, own_ref, shared_ref, arrived_ref, w_ref, attn_ref, rel0_ref, rel1_ref, vec_ref, pre_sum_ref,
    h_ref, keep_ref, send_ref, acc_ref, x_t, sums_ref, mine_ref,
    *, split,
):
    j = pl.program_id(0)
    width = x_t.shape[0]
    rows = width // SUPER
    half = rows // 2

    @pl.when(j == 0)
    def _():
        x_t[...] = jnp.concatenate([x0[0].T, x1[0].T, x2[0].T], 1)
        sums_ref[...] = jnp.zeros_like(sums_ref)

    far = arrived_ref[0].astype(f32) * (j > 0).astype(f32)
    near = (shared_ref[0].astype(f32) + far).astype(bf16)
    joint = jnp.concatenate([own_ref[0], near], 0)
    part = dot_nt(joint, w_ref[0])
    if split:
        mine_ref[...] = joint

    @pl.when(j == 0)
    def _():
        flag = (ids[1] == 0).astype(f32) if split else 1.0
        acc_ref[...] = part + attn_ref[...].astype(f32) * flag

    @pl.when(j > 0)
    def _():
        acc_ref[...] += part

    for side in range(2):
        lanes = slice(LANES * side, LANES * side + LANES)

        @pl.when(ids[1] == side)
        def _():
            if not split:
                mine_ref[...] = joint[:, lanes]
            sums_ref[j, :, lanes] = jnp.broadcast_to(col_sum(mine_ref[...].astype(f32)), (8, LANES))

    result = dot(x_t[...], mine_ref[...]).astype(bf16)
    for group in range(3):

        @pl.when(j == group)
        def _():
            for slab in range(SUPER):
                store_piece(ids, keep_ref, send_ref, slab, half, group * half,
                            result[rows * slab : rows * slab + rows])

    @pl.when(j == pl.num_programs(0) - 1)
    def _():
        h_ref[...] = acc_ref[...].astype(bf16)
        rel = (rel0_ref[...] + rel1_ref[...]).astype(bf16)
        count = rel.shape[0] // SUPER
        lines = jnp.concatenate([vec_ref[0:6, :], sums_ref[0, 0:1], sums_ref[2, 0:1]], 0)
        blank = jnp.zeros((8, LANES - rows), f32)
        for slab in range(SUPER):
            narrow = jnp.concatenate([lines[:, rows * slab : rows * slab + rows], blank], 1)
            wide = pre_sum_ref[0:1, LANES * slab : LANES * slab + LANES]
            small = jnp.concatenate([narrow, wide, jnp.zeros((count - 9, LANES), f32)], 0).astype(bf16)
            both = jnp.concatenate([rel[count * slab : count * slab + count], small], 0)
            store_piece(ids, keep_ref, send_ref, slab, count, 3 * half, both)


def joint_bwd(ids, x, gathered, own, shared, arrived, w_qkv, g_attn, rel0, rel1, vec, pre_sum, layer, split):
    _, length, cols = own.shape
    width = g_attn.shape[1]
    half = shared.shape[1]
    tokens = length + half
    full = lambda *shape: spec(shape, *([0] * len(shape)))
    side = lambda i, ids: 0 if split else ids[1]
    piece = (SUPER, (width // SUPER // 2) * 3 + rel0.shape[0] // SUPER, LANES)
    return call(
        functools.partial(joint_bwd_kernel, split=split), "projections_backward", (3,), ids,
        row_tiles(half, width, gathered)
        + [
            spec((1, length, cols), step, 0, 0), spec((1, half, cols), step, 0, 0),
            spec((1, half, cols), lambda i, ids: jnp.maximum(i - 1, 0), 0, 0),
            spec((1, width, cols), layer, 0, lambda i, ids: 2 * i + ids[1] if split else i),
            full(tokens, width), spec((rel0.shape[0], LANES), 0, side), spec((rel0.shape[0], LANES), 0, side),
            full(*vec.shape), full(*pre_sum.shape),
        ],
        [x, x, x, own, shared, arrived, w_qkv, g_attn, rel0, rel1, vec, pre_sum],
        [full(tokens, width), full(*piece), full(*piece)],
        [shape_of((tokens, width), bf16), shape_of(piece, bf16), shape_of(piece, bf16)],
        [
            pltpu.VMEM((tokens, width), f32), pltpu.VMEM((width, tokens), bf16),
            pltpu.VMEM((3, 8, width), f32), pltpu.VMEM((tokens, LANES), bf16),
        ],
    )


def place_rows_kernel(ids, own_ref, other_ref, out_ref):
    i = pl.program_id(0)
    core = ids[0]
    row = i // 2
    mine = jnp.where(row == 2, (i - 4) == core, row == core)

    @pl.when(mine)
    def _():
        out_ref[0] = own_ref[0].astype(out_ref.dtype)

    @pl.when(jnp.logical_not(mine))
    def _():
        out_ref[0] = other_ref[0].astype(out_ref.dtype)


def place_rows(ids, own, other, dtype):
    tokens, width = own.shape
    half = tokens // 3
    tile = lambda i, ids: jnp.where(i < 4, i % 2, 2)
    tiles = lambda x: x.reshape(3, half, width)
    return call(
        place_rows_kernel, "place_rows", (6,), ids,
        [spec((1, half, width), tile, 0, 0)] * 2, [tiles(own), tiles(other)],
        spec((1, half, width), step, 0, 0), shape_of((6, half, width), dtype),
    )


def collect(ids, refs, scratch):
    for core in range(2):
        for side in range(2):

            @pl.when((ids[0] == core) & (ids[1] == side))
            def _():
                scratch[core, side] = refs[0][...]
                scratch[core, 1 - side] = refs[1][...]
                scratch[1 - core, side] = refs[2][...]
                scratch[1 - core, 1 - side] = refs[3][...]


def spread_columns(scratch, out_ref, layer, at, groups, rows, inner=False):
    for core in range(2):
        for side in range(2):
            for g in range(groups):
                piece = scratch[core, side, at + g * rows : at + g * rows + rows, :]
                lane = ((g * 2 + side) if inner else (side * groups + g)) * LANES
                out_ref[layer, core * rows : core * rows + rows, lane : lane + LANES] = piece.astype(f32)


def unpack_feed_kernel(ids, *refs):
    inputs, (in_ref, out_ref, w_out_ref, scratch) = refs[:8], refs[8:]
    high = LANES // 2
    for layer in range(2):
        collect(ids, inputs[4 * layer : 4 * layer + 4], scratch)
        columns = [scratch[core, side, 0:high, :] for side in range(2) for core in range(2)]
        out_ref[layer] = jnp.concatenate(columns, 0).astype(f32).T
        rows = in_ref.shape[1] // 2
        spread_columns(scratch, in_ref, layer, high, 4, rows)
        spread_columns(scratch, w_out_ref, layer, high + 4 * rows, 1, rows)


def unpack_attention_kernel(ids, *refs):
    inputs = refs[:8]
    qkv_ref, rel_ref, qv_ref, out_bias_ref, scale_ref, shift_ref, in_bias_ref, ffn_bias_ref = refs[8:16]
    scratch = refs[16]
    rows = qkv_ref.shape[1] // 2
    wide = 2 * rows
    for layer in range(2):
        collect(ids, inputs[4 * layer : 4 * layer + 4], scratch)
        spread_columns(scratch, qkv_ref, layer, 0, 3, rows, True)
        at = 3 * rows
        count = rel_ref.shape[2]
        rel = jnp.concatenate([scratch[0, side, at : at + count, :] for side in range(2)], 1).astype(f32)
        rel = jnp.concatenate([rel, jnp.zeros((128 - count, rel.shape[1]), f32)], 0)
        rel_ref[layer] = rel.T[:, 0:count]
        small = scratch[1, 0, at : at + count, :].astype(f32)
        scale_ref[layer] = small[0:2, 0:wide]
        shift_ref[layer] = small[2:4, 0:wide]
        out_bias_ref[layer : layer + 1] = small[4:5, 0:wide]
        ffn_bias_ref[layer : layer + 1] = small[5:6, 0:wide]
        other = scratch[1, 1, at : at + count, :].astype(f32)
        qv_ref[layer] = small[6:8, 0:wide] + other[6:8, 0:wide]
        in_bias_ref[layer : layer + 1] = small[8:9]


def unpack(kernel, name, ids, pieces, shapes):
    full = lambda *shape: spec(shape, *([0] * len(shape)))
    return call(
        kernel, name, (1,), ids, [full(*p.shape) for p in pieces], pieces,
        [full(*s) for s in shapes], [shape_of(s, f32) for s in shapes],
        [pltpu.VMEM((2, 2) + pieces[0].shape, bf16)],
    )


def body(
    stream, cotangent, segments, word_boxes, valid_mask, w_qkv, qv_bias, w_out, out_bias, rel_proj,
    ln_scale, ln_shift, ffn_in, ffn_in_bias, ffn_out, ffn_out_bias,
):
    sections = lax.axis_size("section")
    dp = lax.axis_size("dp")
    section = lax.axis_index("section")
    dp_index = lax.axis_index("dp")
    core, side = section % 2, section // 2
    rows, length, width = stream.shape
    layers = w_qkv.shape[0]
    ff = ffn_in.shape[2]
    half = length // 2
    assert rows == 3 and sections == 4 and layers == 2 and dp % SUPER == 0 and width == 2 * LANES
    fine = dp // SUPER
    ids = jnp.stack([core, side, dp_index // fine]).astype(jnp.int32)
    weights = (w_out, out_bias, ln_scale, ln_shift, ffn_in, ffn_in_bias, ffn_out, ffn_out_bias)
    rel_pairs = rel_proj.reshape(layers, width // 128, 128, 128)

    def flip(x, bit):
        return lax.ppermute(x, "section", [(i, i ^ bit) for i in range(sections)])

    def flip_dp(x, bit):
        return lax.ppermute(x, "dp", [(i, i ^ bit) for i in range(dp)])

    tables = make_tables(ids, word_boxes, segments, valid_mask)
    ctab, stab, valid_col = tables[3], tables[4], tables[7]

    halves = lambda x: x.reshape(-1, half, width)
    x, gathered = halves(stream), True
    kept = []
    for l in range(layers):
        joint, turned, kv = project(ids, x, gathered, w_qkv, qv_bias, rel_pairs, ctab, stab, l)
        kv_far = flip(kv, 1)
        ctx_own, lse_own = attention_fwd(ids, False, tables, joint, turned, None)
        ctx_shared, lse_shared = attention_fwd(ids, True, tables, joint, turned, kv_far)
        n1, r1, n2, r2, mixed, act, slope, out, squares = feed_fwd(
            ids, x, gathered, ctx_own, ctx_shared, valid_col, weights, l
        )
        kept.append(
            dict(x=x, gathered=gathered, joint=joint, turned=turned, kv_far=kv_far, ctx_own=ctx_own,
                 ctx_shared=ctx_shared, lse_own=lse_own, lse_shared=lse_shared, norms=(n1, r1, n2, r2),
                 mixed=mixed, act=act, slope=slope, out=out, squares=squares)
        )
        x, gathered = halves(out), False

    clock = [ids]

    def pin(state):
        clock[0], state = lax.optimization_barrier((clock[0], state))
        return state

    def absorb(keep, arrived):
        n = keep.shape[0] // 2
        return pin((keep[:n] + arrived[:n], keep[n:] + arrived[n:]))

    def last(keep, arrived):
        x = (keep + arrived)[0]
        bit = 1
        while bit < fine:
            x = x + flip_dp(x, bit)
            bit *= 2
        return pin(x)

    def hop(state, bit):
        return state[0], flip_dp(state[1], fine << bit)

    def all_sides(x):
        far = flip(x, 2)
        return [x, far, flip(x, 1), flip(far, 1)]

    def feed_back(l, grad, gathered):
        k = kept[l]
        g_mixed, g_attn, g_ctx, vec, pre_sum, keep, send = feed_bwd(
            clock[0], grad, gathered, k["norms"], k["slope"], k["act"], k["mixed"], k["ctx_own"],
            k["ctx_shared"], weights, l,
        )
        k["g_mixed"] = g_mixed
        return g_attn, g_ctx, vec, pre_sum, (keep, flip(send, 1))

    def attention_back(l, shared, g_ctx):
        k = kept[l]
        return attention_bwd(
            clock[0], shared, tables, k["joint"], k["turned"], k["kv_far"] if shared else None,
            k["lse_shared" if shared else "lse_own"], g_ctx, rel_pairs, l, l == 0,
        )

    def joint_back(l, own_grads, shared_keep, arrived, g_attn, rel_own, rel_shared, vec, pre_sum):
        k = kept[l]
        g_h, keep, send = joint_bwd(
            clock[0], k["x"], k["gathered"], own_grads, shared_keep, arrived, w_qkv, g_attn, rel_own,
            rel_shared, vec, pre_sum, l, l == 0,
        )
        k["g_h"] = g_h
        return g_h, (keep, flip(send, 1))

    g_attn, g_ctx, vec, pre_sum, f1 = feed_back(1, halves(cotangent), True)
    shared_keep, shared_send, rel_shared = attention_back(1, True, g_ctx)
    arrived = flip(shared_send, 1)
    f1 = hop(absorb(*f1), 0)
    own_grads, rel_own = attention_back(1, False, g_ctx)
    g_h, a1 = joint_back(1, own_grads, shared_keep, arrived, g_attn, rel_own, rel_shared, vec, pre_sum)

    f1 = hop(absorb(*f1), 1)
    g_attn, g_ctx, vec, pre_sum, f0 = feed_back(0, halves(g_h), False)
    f1 = hop(absorb(*f1), 2)
    a1 = hop(absorb(*a1), 0)
    shared_keep, shared_send, rel_shared = attention_back(0, True, g_ctx)
    arrived = flip(shared_send, 1)
    f0 = hop(absorb(*f0), 0)
    own_grads, rel_own = attention_back(0, False, g_ctx)
    f1 = last(*f1)
    a1 = hop(absorb(*a1), 1)
    f1 = all_sides(f1)
    g_h, a0 = joint_back(0, own_grads, shared_keep, arrived, g_attn, rel_own, rel_shared, vec, pre_sum)
    a1 = hop(absorb(*a1), 2)
    a0 = hop(absorb(*a0), 0)
    f0 = hop(absorb(*f0), 1)
    a1 = all_sides(last(*a1))
    a0 = hop(absorb(*a0), 1)
    f0 = hop(absorb(*f0), 2)
    a0 = hop(absorb(*a0), 2)
    f0 = all_sides(last(*f0))
    a0 = all_sides(last(*a0))
    kept[0]["g_h"] = g_h + flip(g_h, 2)

    def of_layer(name):
        return jnp.where(side == 0, kept[0][name], kept[1][name])

    def to_section(first, second, dtype):
        a, b = of_layer(first), of_layer(second)
        own, away = jnp.where(core == 0, a, b), jnp.where(core == 0, b, a)
        return place_rows(ids, own, flip(away, 1), dtype).reshape(1, rows, length, width)

    section_outs = to_section("mixed", "out", bf16)
    in_grads = to_section("g_h", "g_mixed", f32)

    squares_mine = jnp.sum(of_layer("squares"), 1).reshape(2, 2, 2)
    squares_far = flip(squares_mine, 1)
    sub = lambda v: lax.dynamic_index_in_dim(v, core, 0, keepdims=False)
    near, far = sub(squares_mine), sub(squares_far)
    first = jnp.where(core == 0, near[:, 0], far[:, 0])
    second = jnp.where(core == 0, far[:, 0], near[:, 0])
    square_rows = jnp.stack([first, second, near[:, 1] + far[:, 1]])
    row_counts = jnp.sum(valid_mask.astype(f32), 1)
    root_mean_squares = jnp.sqrt(square_rows / (width * jnp.maximum(row_counts, 1.0))[:, None])[None]

    slab = width // SUPER
    d_ffn_in, d_ffn_out, d_out = unpack(
        unpack_feed_kernel, "unpack_feed", ids, f0 + f1,
        [(2, slab, ff), (2, ff // SUPER, width), (2, slab, width)],
    )
    rel_rows = 128 // SUPER
    d_qkv, d_rel, d_qv, d_out_bias, d_scale, d_shift, d_in_bias, d_ffn_bias = unpack(
        unpack_attention_kernel, "unpack_attention", ids, a0 + a1,
        [(2, slab, 3 * width), (2, width, rel_rows), (2, 2, slab), (2, slab),
         (2, 2, slab), (2, 2, slab), (2, LANES), (2, slab)],
    )

    def own_part(x, axis):
        n = x.shape[axis] // fine
        return x if fine == 1 else lax.dynamic_slice_in_dim(x, (dp_index % fine) * n, n, axis)

    d_rel = d_rel.reshape((2,) + rel_proj.shape[1:3] + (rel_rows,))
    return (
        section_outs,
        in_grads,
        own_part(d_qkv, 1),
        own_part(d_qv, 2),
        own_part(d_out, 1),
        own_part(d_out_bias, 1),
        own_part(d_rel, 3),
        own_part(d_scale, 2),
        own_part(d_shift, 2),
        own_part(d_ffn_in, 1),
        own_part(d_in_bias, 1),
        own_part(d_ffn_out, 1),
        own_part(d_ffn_bias, 1),
        root_mean_squares,
    )


def solution(mesh):
    return jax.shard_map(
        body,
        mesh=mesh,
        in_specs=(
            P("dp", None, None),
            P("dp", None, None),
            P("dp", None),
            P(None, "dp", None),
            P("dp", None),
        )
        + (P(),) * 11,
        out_specs=(
            P("section", "dp", None, None),
            P("section", "dp", None, None),
            P(None, "dp", None),
            P(None, None, "dp"),
            P(None, "dp", None),
            P(None, "dp"),
            P(None, None, None, "dp"),
            P(None, None, "dp"),
            P(None, None, "dp"),
            P(None, "dp", None),
            P(None, "dp"),
            P(None, "dp", None),
            P(None, "dp"),
            P("section", "dp", None),
        ),
        check_vma=False,
    )
```

```python
import functools

import jax
import jax.numpy as jnp
from jax import lax
from jax.experimental import pallas as pl
from jax.experimental.pallas import tpu as pltpu
from jax.sharding import PartitionSpec as P

ln_eps = 1e-05
masked_score = -1e30
bf16 = jnp.bfloat16
f32 = jnp.float32
MB = 1 << 20
SUPER = 8
LANES = 384
NORM_ROWS = 64

ERF_COEFS = (
    0.7978849414899046, 0.0363330844086688, -3.259474462099993e-05, -5.5306316685416947e-05,
    3.964773125473232e-06, -1.322662757755248e-07, 1.7562773256476674e-09,
)


def dot(a, b):
    return lax.dot_general(a, b, (((1,), (0,)), ((), ())), preferred_element_type=f32)


def dot_nt(a, b):
    return lax.dot_general(a, b, (((1,), (1,)), ((), ())), preferred_element_type=f32)


def gelu_and_slope(x):
    square = x * x
    g = ERF_COEFS[-1]
    for c in ERF_COEFS[-2::-1]:
        g = g * square + c
    phi = 0.5 * jnp.tanh(x * g) + 0.5
    density = jnp.exp2(square * (-0.5 * 1.4426950408889634)) * 0.3989422804014327
    return x * phi, phi + x * density


def norm_parts(residual):
    average = jnp.mean(residual, -1, keepdims=True)
    centered = residual - average
    inverse = lax.rsqrt(jnp.mean(centered * centered, -1, keepdims=True) + ln_eps)
    return centered * inverse, inverse


def norm_back(gradient, gain, normed, inverse):
    dnormed = gradient * gain
    return inverse * (
        dnormed
        - jnp.mean(dnormed, -1, keepdims=True)
        - normed * jnp.mean(dnormed * normed, -1, keepdims=True)
    )


def row_loop(count, chunk, sums):
    for i in range(count):
        sums = chunk(i, sums)
    return sums


def fold(x):
    return jnp.sum(x.reshape(-1, 8, x.shape[1]), 0)


def col_sum(x):
    return jnp.sum(x, 0, keepdims=True)


COST_US = dict(
    tables=4, projections=8, attention_forward=7, feed_forward=24, feed_backward=30, attention_backward=12,
    projections_backward=3, place_rows=4,
    unpack_feed=4, unpack_attention=3,
)


def call(kernel, name, grid, ids, in_specs, inputs, out_specs, out_shape, scratch=(), micros=None):
    micros = COST_US[name] if micros is None else micros
    cost = pl.CostEstimate(flops=micros * 1100000000, bytes_accessed=micros * 1000000, transcendentals=0)
    return pl.pallas_call(
        kernel,
        grid_spec=pltpu.PrefetchScalarGridSpec(
            num_scalar_prefetch=1,
            grid=grid,
            in_specs=in_specs,
            out_specs=out_specs,
            scratch_shapes=list(scratch),
        ),
        out_shape=out_shape,
        compiler_params=pltpu.CompilerParams(vmem_limit_bytes=62 * MB),
        cost_estimate=cost,
        name=name,
    )(ids, *inputs)


def spec(shape, *index):
    def index_map(i, ids):
        return tuple(x(i, ids) if callable(x) else x for x in index)

    return pl.BlockSpec(shape, index_map)


def shape_of(shape, dtype):
    return jax.ShapeDtypeStruct(shape, dtype)


step = lambda i, ids: i


def row_tiles(half, width, gathered):
    if not gathered:
        return [spec((1, half, width), t, 0, 0) for t in range(3)]
    core = lambda ids: ids[0]
    return [
        spec((1, half, width), lambda i, ids: 2 * core(ids), 0, 0),
        spec((1, half, width), lambda i, ids: 2 * core(ids) + 1, 0, 0),
        spec((1, half, width), lambda i, ids: 4 + core(ids), 0, 0),
    ]


def tables_kernel(
    ids, boxes_ref, seg_ref, valid_ref,
    cos_ref, sin_ref, kf_ref, ctab_ref, stab_ref, code_ref, segrow_ref, valid_col_ref,
):
    core = ids[0]
    length = seg_ref.shape[1]
    half = length // 2

    def ordered(read):
        near = pl.multiple_of(core * half, half)
        far = pl.multiple_of((1 - core) * half, half)
        return jnp.concatenate(
            [read(pl.ds(core, 1), slice(None)), read(2, pl.ds(near, half)), read(2, pl.ds(far, half))], 1
        )

    def row_of(ref):
        def read(r, c):
            r = pl.ds(2, 1) if isinstance(r, int) else r
            return ref[r, c]
        return ordered(read)

    count = length * 2
    at = lax.broadcasted_iota(jnp.int32, (1, count), 1)
    shared = jnp.where(
        at < length + half, at - length + core * half, at - length - half + (1 - core) * half
    )
    position = jnp.where(at < length, at, shared).astype(f32)
    rate_at = lax.broadcasted_iota(jnp.int32, (32, 1), 0).astype(f32)
    text = position * jnp.exp(rate_at * (-9.210340371976184 / 32))
    box_rate = jnp.exp2(-lax.broadcasted_iota(jnp.int32, (8, 1), 0).astype(f32))
    angles = [text]
    for c in range(4):
        coords = row_of(boxes_ref.at[c]).astype(f32)
        angles.append(coords * box_rate)
    angles = jnp.concatenate(angles, 0)
    cosines, sines = jnp.cos(angles), jnp.sin(angles)
    cos_ref[...], sin_ref[...] = cosines, sines
    kf_ref[...] = jnp.concatenate([cosines, sines], 0).T.astype(bf16)
    ctab_ref[...] = jnp.concatenate([cosines, -cosines], 0).T
    stab_ref[...] = jnp.concatenate([sines, sines], 0).T
    seg = row_of(seg_ref).astype(f32)
    valid = row_of(valid_ref).astype(f32)
    segrow_ref[...] = jnp.broadcast_to(seg, segrow_ref.shape)
    code_ref[...] = jnp.broadcast_to(jnp.where(valid > 0, seg, -1.0), (128, count)).T
    valid_col_ref[...] = jnp.broadcast_to(valid, (128, count)).T


def make_tables(ids, word_boxes, segments, valid_mask):
    length = segments.shape[1]
    count = 2 * length
    full = lambda *shape: spec(shape, *([0] * len(shape)))
    outs = [
        ((64, count), f32), ((64, count), f32), ((count, 128), bf16), ((count, 128), f32),
        ((count, 128), f32), ((count, 128), f32), ((8, count), f32), ((count, 128), f32),
    ]
    return call(
        tables_kernel, "tables", (1,), ids,
        [full(*word_boxes.shape), full(*segments.shape), full(*valid_mask.shape)],
        [word_boxes, segments, valid_mask],
        [full(*s) for s, _ in outs], [shape_of(s, d) for s, d in outs],
    )


def qkv_kernel(
    ids, x0, x1, x2, w_ref, bias_ref, rel_ref, ctab_ref, stab_ref, joint_ref, turned_ref, kv_ref, x_ref,
    *, layer,
):
    j = pl.program_id(0)
    half = x0.shape[1]

    @pl.when(j == 0)
    def _():
        x_ref[0:half], x_ref[half : 2 * half], x_ref[2 * half :] = x0[0], x1[0], x2[0]

    flags = [(j == 0).astype(f32), (j == 2).astype(f32)]
    bias = bias_ref[layer, 0:1, :].astype(f32) * flags[0] + bias_ref[layer, 1:2, :].astype(f32) * flags[1]
    joint = (dot(x_ref[...], w_ref[0]) + bias).astype(bf16)
    joint_ref[...] = joint
    kv_ref[...] = joint[2 * half :]

    @pl.when(j == 0)
    def _():
        ctab, stab = ctab_ref[...], stab_ref[...]
        row = lax.broadcasted_iota(jnp.int32, (128, 128), 0)
        for p in range(rel_ref.shape[1]):
            rel = rel_ref[0, p]
            zero = jnp.zeros_like(rel)
            block = jnp.concatenate([jnp.where(row < 64, rel, zero), jnp.where(row < 64, zero, rel)], 1)
            coef = dot(joint[:, 128 * p : 128 * p + 128], block)
            for e in range(2):
                c = coef[:, 128 * e : 128 * e + 128]
                at = 256 * p + 128 * e
                turned_ref[:, at : at + 128] = (c * ctab + pltpu.roll(c, 64, 1) * stab).astype(bf16)


def project(ids, x, gathered, w_qkv, qv_bias, rel_pairs, ctab, stab, layer):
    half, width = x.shape[1], x.shape[2]
    tokens = 3 * half
    pairs = rel_pairs.shape[1]
    return call(
        functools.partial(qkv_kernel, layer=layer), "projections", (3,), ids,
        row_tiles(half, width, gathered)
        + [
            spec((1, width, width), layer, 0, step), spec(qv_bias.shape, 0, 0, 0),
            spec((1, pairs, 128, 128), layer, 0, 0, 0), spec((tokens, 128), 0, 0),
            spec((tokens, 128), 0, 0),
        ],
        [x, x, x, w_qkv, qv_bias, rel_pairs, ctab, stab],
        [
            spec((tokens, width), 0, step), spec((tokens, 2 * width), 0, 0),
            spec((half, width), 0, lambda i, ids: jnp.maximum(i - 1, 0)),
        ],
        [
            shape_of((tokens, 3 * width), bf16), shape_of((tokens, 2 * width), bf16),
            shape_of((half, 2 * width), bf16),
        ],
        [pltpu.VMEM((tokens, width), bf16)],
    )


def lane_half(shape, half):
    lane = lax.broadcasted_iota(jnp.int32, shape, 1)
    return (lane < 64) if half == 0 else (lane >= 64)


def only_half(x, half):
    return jnp.where(lane_half(x.shape, half), x, jnp.zeros_like(x))


def fill_bias(code_ref, seg_ref, bias_ref):
    shape = bias_ref.shape
    code = jnp.concatenate([code_ref[...]] * (shape[1] // 128), 1)
    same = code == seg_ref[0:1, :]
    key_at = lax.broadcasted_iota(jnp.int32, shape, 0)
    query_at = lax.broadcasted_iota(jnp.int32, shape, 1)
    bias_ref[...] = jnp.where(same | (key_at == query_at), 0.0, masked_score)


def attention_fwd_kernel(
    ids, code_ref, seg_ref, kf_ref, q_ref, turned_ref, k_ref, v_ref, *rest, per_step, shared,
):
    if shared:
        k_far, v_far, ctx_ref, lse_ref, bias_ref, k_all, v_all = rest
        half = k_ref.shape[0]
        k_all[0:half], k_all[half:] = k_ref[...], k_far[...]
        v_all[0:half], v_all[half:] = v_ref[...], v_far[...]
        k_ref, v_ref = k_all, v_all
    else:
        ctx_ref, lse_ref, bias_ref = rest

    @pl.when(pl.program_id(0) == 0)
    def _():
        fill_bias(code_ref, seg_ref, bias_ref)

    scale = jnp.asarray(0.125, bf16)
    units = [(pair, e) for pair in range(per_step) for e in range(2)]
    values_t = {}

    def scores_of(unit):
        pair, e = unit
        at = slice(128 * pair, 128 * pair + 128)
        turned = turned_ref[:, 256 * pair + 128 * e : 256 * pair + 128 * e + 128]
        qside = jnp.concatenate([turned, only_half(q_ref[:, at], e)], 1) * scale
        kside = jnp.concatenate([kf_ref[...], k_ref[:, at]], 1)
        return dot_nt(kside, qside) + bias_ref[...]

    def finish(unit, scores):
        pair, e = unit
        top = jnp.max(scores, 0, keepdims=True)
        expo = jnp.exp(scores - top)
        total = jnp.sum(expo, 0, keepdims=True)
        if pair not in values_t:
            values_t[pair] = v_ref[:, 128 * pair : 128 * pair + 128].T
        ctx = dot(values_t[pair][64 * e : 64 * e + 64], expo.astype(bf16))
        at = 128 * pair + 64 * e
        ctx_ref[at : at + 64, :] = (ctx * (1.0 / total)).astype(bf16)
        lse_ref[pair, e : e + 1, :] = top + jnp.log(total)

    scores = scores_of(units[0])
    for i, unit in enumerate(units):
        upcoming = scores_of(units[i + 1]) if i + 1 < len(units) else None
        finish(unit, scores)
        scores = upcoming


def attention_fwd(ids, shared, tables, joint, turned, kv_far, per_step=2):
    cos_t, sin_t, kf, ctab, stab, code, seg, valid = tables
    tokens, width = joint.shape[0], joint.shape[1] // 3
    half = tokens // 3
    nk = 2 * half
    nq = half if shared else nk
    key_rows = half if shared else nk
    lanes = 128 * per_step
    steps = width // lanes
    q_row = 2 if shared else 0
    at = lambda off: (lambda i, ids: i + off)
    in_specs = [
        spec((nk, 128), int(shared), 0), spec((8, nq), 0, q_row), spec((nk, 128), int(shared), 0),
        spec((nq, lanes), q_row, step), spec((nq, 2 * lanes), q_row, step),
        spec((key_rows, lanes), q_row, at(steps)), spec((key_rows, lanes), q_row, at(2 * steps)),
    ]
    inputs = [code, seg, kf, joint, turned, joint, joint]
    scratch = [pltpu.VMEM((nk, nq), f32)]
    if shared:
        in_specs += [spec((half, lanes), 0, step), spec((half, lanes), 0, at(steps))]
        inputs += [kv_far, kv_far]
        scratch += [pltpu.VMEM((nk, lanes), bf16)] * 2
    return call(
        functools.partial(attention_fwd_kernel, per_step=per_step, shared=shared),
        "attention_forward", (steps,), ids, in_specs, inputs,
        [spec((lanes, nq), step, 0), spec((per_step, 2, nq), step, 0, 0)],
        [shape_of((width, nq), bf16), shape_of((width // 128, 2, nq), f32)],
        scratch,
    )


def attention_bwd_kernel(
    ids, code_ref, seg_ref, kf_ref, cos_ref, sin_ref, rel_ref, lse_ref, gc_ref, q_ref, turned_ref,
    k_ref, v_ref, *rest, per_step, shared,
):
    if shared:
        k_far, v_far, keep_ref, send_ref, drel_ref, bias_ref, kft_ref, k_all, v_all = rest
        half = k_ref.shape[0]
        k_all[0:half], k_all[half:] = k_ref[...], k_far[...]
        v_all[0:half], v_all[half:] = v_ref[...], v_far[...]
        k_ref, v_ref = k_all, v_all
    else:
        keep_ref, drel_ref, bias_ref, kft_ref = rest

    @pl.when(pl.program_id(0) == 0)
    def _():
        fill_bias(code_ref, seg_ref, bias_ref)
        kft_ref[...] = kf_ref[...].T

    scale = jnp.asarray(0.125, bf16)
    cosines, sines = cos_ref[...], sin_ref[...]
    units = [(pair, e) for pair in range(per_step) for e in range(2)]
    store = {}

    def scores_of(unit):
        pair, e = unit
        at = slice(128 * pair, 128 * pair + 128)
        q_mine = only_half(q_ref[:, at], e)
        gc_mine = only_half(gc_ref[:, at], e)
        q_scaled = q_mine * scale
        turned = turned_ref[:, 256 * pair + 128 * e : 256 * pair + 128 * e + 128]
        qside = jnp.concatenate([turned * scale, q_scaled], 1)
        kside = jnp.concatenate([kf_ref[...], k_ref[:, at]], 1)
        scores = dot_nt(kside, qside) + bias_ref[...]
        gp = dot_nt(v_ref[:, at], gc_mine)
        return scores, gp, q_mine, gc_mine, q_scaled

    def finish(unit, parts):
        pair, e = unit
        scores, gp, q_mine, gc_mine, q_scaled = parts
        at = slice(128 * pair, 128 * pair + 128)
        shares = jnp.exp(scores - lse_ref[pair, e : e + 1, :])
        dv = dot(shares.astype(bf16), gc_mine)
        weighted = shares * gp
        delta = jnp.sum(weighted, 0, keepdims=True)
        gs = (weighted - shares * delta).astype(bf16)
        dk = dot(gs, q_scaled)
        if pair not in store:
            store[pair] = k_ref[:, at].T
        side_t = jnp.concatenate([kft_ref[...], store[pair][64 * e : 64 * e + 64]], 0)
        dside = dot(side_t, gs) * 0.125
        g_cos, g_sin = dside[0:64], dside[64:128]
        gcoef = jnp.concatenate(
            [g_cos * cosines + g_sin * sines, g_cos * sines - g_sin * cosines], 0
        ).astype(bf16)
        dq = dside[128:192] + dot(rel_ref[0, pair, 64 * e : 64 * e + 64], gcoef)
        drel = dot(gcoef, q_mine)
        if e == 0:
            store["even"] = (dq, dk, dv, drel)
            return
        dq0, dk0, dv0, drel0 = store["even"]
        dq = jnp.concatenate([dq0, dq], 0).T.astype(bf16)
        dk, dv = (dk0 + dk).astype(bf16), (dv0 + dv).astype(bf16)
        drel_ref[:, at] = drel0 + drel
        n = keep_ref.shape[1]
        keep_ref[0, :, at] = dq
        keep_ref[1, :, at], keep_ref[2, :, at] = dk[0:n], dv[0:n]
        if shared:
            send_ref[0, :, at], send_ref[1, :, at] = dk[n:], dv[n:]

    parts = scores_of(units[0])
    for i, unit in enumerate(units):
        upcoming = scores_of(units[i + 1]) if i + 1 < len(units) else None
        finish(unit, parts)
        parts = upcoming


def attention_bwd(ids, shared, tables, joint, turned, kv_far, lse, g_ctx, rel_pairs, layer, split, per_step=2):
    per_step = 1 if split else per_step
    cos_t, sin_t, kf, ctab, stab, code, seg, valid = tables
    tokens, width = joint.shape[0], joint.shape[1] // 3
    half = tokens // 3
    nk = 2 * half
    nq = half if shared else nk
    key_rows = half if shared else nk
    lanes = 128 * per_step
    all_steps = width // lanes
    steps = all_steps // 2 if split else all_steps
    out_width = lanes * steps
    first = lambda ids: ids[1] * steps if split else 0
    q_row = 2 if shared else 0
    at = lambda off: (lambda i, ids: first(ids) + i + off)
    here = at(0)
    in_specs = [
        spec((nk, 128), int(shared), 0), spec((8, nq), 0, q_row), spec((nk, 128), int(shared), 0),
        spec((64, nq), 0, q_row), spec((64, nq), 0, q_row),
        spec((1, per_step, 128, 128), layer, here, 0, 0),
        spec((per_step, 2, nq), here, 0, 0), spec((nq, lanes), q_row, here),
        spec((nq, lanes), q_row, here), spec((nq, 2 * lanes), q_row, here),
        spec((key_rows, lanes), q_row, at(all_steps)), spec((key_rows, lanes), q_row, at(2 * all_steps)),
    ]
    inputs = [code, seg, kf, cos_t, sin_t, rel_pairs, lse, g_ctx, joint, turned, joint, joint]
    scratch = [pltpu.VMEM((nk, nq), f32), pltpu.VMEM((128, nk), bf16)]
    out_specs = [spec((3, key_rows, lanes), 0, 0, step)]
    out_shape = [shape_of((3, key_rows, out_width), bf16)]
    if shared:
        in_specs += [spec((half, lanes), 0, here), spec((half, lanes), 0, at(all_steps))]
        inputs += [kv_far, kv_far]
        scratch += [pltpu.VMEM((nk, lanes), bf16)] * 2
        out_specs.append(spec((2, half, lanes), 0, 0, step))
        out_shape.append(shape_of((2, half, out_width), bf16))
    out_specs.append(spec((128, lanes), 0, step))
    out_shape.append(shape_of((128, out_width), f32))
    return call(
        functools.partial(attention_bwd_kernel, per_step=per_step, shared=shared),
        "attention_backward", (steps,), ids, in_specs, inputs, out_specs, out_shape, scratch,
        40 if shared else 12,
    )


def feed_fwd_kernel(
    ids, x0, x1, x2, own_ref, shared_ref, valid_ref, w_out_ref, out_bias_ref, scale_ref, shift_ref,
    in_ref, in_bias_ref, out_ref, ffn_bias_ref,
    n1_ref, r1_ref, n2_ref, r2_ref, mixed_ref, act_ref, slope_ref, h_ref, squares_ref,
    feed_ref,
    *, layer, parts,
):
    j = pl.program_id(0)
    half = x0.shape[1]
    row = lambda ref, *at: ref[at[:-1] + (slice(at[-1], at[-1] + 1),)].astype(f32)

    rows = NORM_ROWS
    zero = jnp.zeros((8, x0.shape[2]), f32)

    def add_squares(sums, k, tile):
        for i, x in enumerate(sums):
            at = k + 2 * i + tile // 2
            squares_ref[at : at + 1, :] += col_sum(x)

    @pl.when(j == 0)
    def _():
        ctx = jnp.concatenate([own_ref[...].T, shared_ref[...].T], 0)
        feed_ref[...] = dot(ctx, w_out_ref[0])
        bias, gain, shift = row(out_bias_ref, layer), row(scale_ref, layer, 0), row(shift_ref, layer, 0)
        squares_ref[...] = jnp.zeros_like(squares_ref)
        for t, x_ref in enumerate((x0, x1, x2)):

            def chunk(i, sums):
                at = i * rows
                to = pl.ds(t * half + at, rows)
                valid = valid_ref[to, 0:1]
                attention = feed_ref[to, :] + bias
                normed, inverse = norm_parts(x_ref[0, pl.ds(at, rows), :].astype(f32) + attention)
                mixed = (normed * gain + shift).astype(bf16)
                n1_ref[to, :] = normed.astype(bf16)
                r1_ref[to, :] = jnp.broadcast_to(inverse, (rows, 128))
                mixed_ref[to, :] = mixed
                mixed = mixed.astype(f32)
                return (sums[0] + fold(attention * attention * valid), sums[1] + fold(mixed * mixed * valid))

            sums = row_loop(half // rows, chunk, (zero, zero))
            add_squares(sums, 0, t)

    cols = in_ref.shape[2] // parts
    at = lambda k: slice(cols * k, cols * k + cols)
    bias = in_bias_ref[layer : layer + 1, :].astype(f32)
    pre = dot(mixed_ref[...], in_ref[0, :, at(0)]) + bias[:, at(0)]
    feed = None
    for k in range(parts):
        coming = None
        if k + 1 < parts:
            coming = dot(mixed_ref[...], in_ref[0, :, at(k + 1)]) + bias[:, at(k + 1)]
        act, slope = gelu_and_slope(pre)
        act = act.astype(bf16)
        act_ref[:, at(k)] = act
        slope_ref[:, at(k)] = slope.astype(bf16)
        part = dot(act, out_ref[0, at(k)])
        feed = part if feed is None else feed + part
        pre = coming

    @pl.when(j == 0)
    def _():
        feed_ref[...] = feed

    @pl.when(j > 0)
    def _():
        feed_ref[...] += feed

    @pl.when(j == pl.num_programs(0) - 1)
    def _():
        bias, gain, shift = row(ffn_bias_ref, layer), row(scale_ref, layer, 1), row(shift_ref, layer, 1)
        for t in range(3):

            def chunk(i, sums):
                to = pl.ds(t * half + i * rows, rows)
                valid = valid_ref[to, 0:1]
                branch = feed_ref[to, :] + bias
                normed, inverse = norm_parts(mixed_ref[to, :].astype(f32) + branch)
                out = normed * gain + shift
                n2_ref[to, :] = normed.astype(bf16)
                r2_ref[to, :] = jnp.broadcast_to(inverse, (rows, 128))
                h_ref[to, :] = out.astype(bf16)
                return (sums[0] + fold(branch * branch * valid), sums[1] + fold(out * out * valid))

            sums = row_loop(half // rows, chunk, (zero, zero))
            add_squares(sums, 4, t)


def feed_fwd(ids, x, gathered, ctx_own, ctx_shared, valid, weights, layer, chunk=768, parts=1):
    w_out, out_bias, ln_scale, ln_shift, ffn_in, ffn_in_bias, ffn_out, ffn_out_bias = weights
    half, width = x.shape[1], x.shape[2]
    tokens, ff = 3 * half, ffn_in.shape[2]
    full = lambda *shape: spec(shape, *([0] * len(shape)))
    dense = ((tokens, width), bf16)
    column = ((tokens, 128), f32)
    outs = [dense, column, dense, column, dense, ((tokens, ff), bf16), ((tokens, ff), bf16), dense,
            ((8, width), f32)]
    out_specs = [full(*s) for s, _ in outs]
    out_specs[5] = out_specs[6] = spec((tokens, chunk), 0, step)
    return call(
        functools.partial(feed_fwd_kernel, layer=layer, parts=parts), "feed_forward", (ff // chunk,), ids,
        row_tiles(half, width, gathered)
        + [
            full(*ctx_own.shape), full(*ctx_shared.shape), spec((tokens, 128), 0, 0),
            spec((1, width, width), layer, 0, 0), full(*out_bias.shape), full(*ln_scale.shape),
            full(*ln_shift.shape), spec((1, width, chunk), layer, 0, step),
            spec((ffn_in_bias.shape[0], chunk), 0, step), spec((1, chunk, width), layer, step, 0),
            full(*ffn_out_bias.shape),
        ],
        [x, x, x, ctx_own, ctx_shared, valid, w_out, out_bias, ln_scale, ln_shift, ffn_in, ffn_in_bias,
         ffn_out, ffn_out_bias],
        out_specs, [shape_of(s, d) for s, d in outs], [pltpu.VMEM((tokens, width), f32)],
    )


def slab_place(ids, slab):
    relative = jnp.bitwise_xor(ids[2], slab)
    return (
        jnp.bitwise_or(
            jnp.left_shift(jnp.bitwise_and(relative, 1), 2),
            jnp.bitwise_or(jnp.bitwise_and(relative, 2), jnp.right_shift(relative, 2)),
        )
    )


def store_piece(ids, keep_ref, send_ref, slab, core_rows, row, value):
    place = slab_place(ids, slab)
    core = ids[0]
    low, high = value[0:core_rows], value[core_rows:]
    at = slice(row, row + core_rows)

    @pl.when(core == 0)
    def _():
        keep_ref[place, at, :], send_ref[place, at, :] = low, high

    @pl.when(core != 0)
    def _():
        keep_ref[place, at, :], send_ref[place, at, :] = high, low


def feed_bwd_kernel(
    ids, g0, g1, g2, n2_ref, r2_ref, n1_ref, r1_ref, scale_ref, out_ref, slope_ref, in_ref, w_out_ref,
    act_ref, mixed_in_ref, own_ref, shared_ref,
    mixed_ref, attn_ref, ctx_ref, sums_ref, pre_sum_ref, keep_ref, send_ref,
    res_ref, acc_ref, feed_ref, pre_ref, feed_t, mixed_t,
    *, layer, parts,
):
    j = pl.program_id(0)
    tokens = n2_ref.shape[0]
    gain = lambda k: scale_ref[layer, k : k + 1, :].astype(f32)
    rows = NORM_ROWS

    @pl.when(j == 0)
    def _():
        sums_ref[...] = jnp.zeros_like(sums_ref)
        for t, g_ref in enumerate((g0, g1, g2)):
            count = g_ref.shape[1]

            def chunk(i, sums):
                at = i * rows
                to = pl.ds(t * count + at, rows)
                grad = g_ref[0, pl.ds(at, rows), :].astype(f32)
                normed = n2_ref[to, :].astype(f32)
                back = norm_back(grad, gain(1), normed, r2_ref[to, 0:1])
                res_ref[to, :] = back
                feed = back.astype(bf16)
                feed_ref[to, :] = feed
                return (sums[0] + fold(grad * normed), sums[1] + fold(grad), sums[2] + fold(feed.astype(f32)))

            zero = jnp.zeros((8, n2_ref.shape[1]), f32)
            sums = row_loop(count // rows, chunk, (zero, zero, zero))
            for k, x in zip((1, 3, 5), sums):
                sums_ref[k : k + 1, :] += col_sum(x)
        for side in range(2):

            @pl.when(ids[1] == side)
            def _():
                feed_t[...] = feed_ref[:, LANES * side : LANES * side + LANES].T

        mixed_t[...] = mixed_in_ref[...].T

    cols = slope_ref.shape[1] // parts
    at = lambda k: slice(cols * k, cols * k + cols)
    g_act = dot_nt(feed_ref[...], out_ref[0, at(0)])
    for k in range(parts):
        coming = dot_nt(feed_ref[...], out_ref[0, at(k + 1)]) if k + 1 < parts else None
        g_pre = (g_act * slope_ref[:, at(k)].astype(f32)).astype(bf16)
        pre_ref[:, at(k)] = g_pre
        pre_sum_ref[:, at(k)] = jnp.broadcast_to(col_sum(g_pre.astype(f32)), (8, cols))
        g_act = coming
    total = dot_nt(pre_ref[...], in_ref[0])

    @pl.when(j == 0)
    def _():
        acc_ref[...] = total

    @pl.when(j > 0)
    def _():
        acc_ref[...] += total

    high = LANES // 2
    slabs = act_ref.shape[1] // LANES
    result = dot(feed_t[...], act_ref[...]).astype(bf16)
    for k in range(slabs):
        store_piece(ids, keep_ref, send_ref, j * slabs + k, high, 0, result[:, LANES * k : LANES * k + LANES])
    width = mixed_t.shape[0]
    slab_rows = width // SUPER
    half = slab_rows // 2
    steps = 4 // slabs
    for s in range(2 * steps):

        @pl.when((j == s) & (ids[1] == s // steps))
        def _():
            result = dot(mixed_t[...], pre_ref[...]).astype(bf16)
            for slab in range(SUPER):
                for k in range(slabs):
                    store_piece(
                        ids, keep_ref, send_ref, slab, half, high + ((s % steps) * slabs + k) * half,
                        result[slab_rows * slab : slab_rows * slab + slab_rows, LANES * k : LANES * k + LANES],
                    )

    @pl.when(j == pl.num_programs(0) - 1)
    def _():
        def chunk(i, sums):
            to = pl.ds(i * rows, rows)
            g_mixed = acc_ref[to, :] + res_ref[to, :]
            mixed_ref[to, :] = g_mixed.astype(bf16)
            normed = n1_ref[to, :].astype(f32)
            attn = norm_back(g_mixed, gain(0), normed, r1_ref[to, 0:1]).astype(bf16)
            attn_ref[to, :] = attn
            return (sums[0] + fold(g_mixed * normed), sums[1] + fold(g_mixed), sums[2] + fold(attn.astype(f32)))

        zero = jnp.zeros((8, width), f32)
        sums = row_loop(tokens // rows, chunk, (zero, zero, zero))
        for k, x in zip((0, 2, 4), sums):
            sums_ref[k : k + 1, :] = col_sum(x)
        ctx_ref[...] = dot_nt(attn_ref[...], w_out_ref[0]).astype(bf16)
        long = own_ref.shape[1]
        for side in range(2):

            @pl.when(ids[1] == side)
            def _():
                lanes = slice(LANES * side, LANES * side + LANES)
                result = dot(own_ref[...], attn_ref[0:long, lanes]) + dot(shared_ref[...], attn_ref[long:, lanes])
                result = result.astype(bf16)
                for slab in range(SUPER):
                    store_piece(ids, keep_ref, send_ref, slab, half, high + 4 * half,
                                result[slab_rows * slab : slab_rows * slab + slab_rows])


def feed_bwd(ids, grad, gathered, kept, slope, act, mixed, ctx_own, ctx_shared, weights, layer, chunk=768, parts=3):
    w_out, out_bias, ln_scale, ln_shift, ffn_in, ffn_in_bias, ffn_out, ffn_out_bias = weights
    n1, r1, n2, r2 = kept
    half, width = grad.shape[1], grad.shape[2]
    tokens, ff = 3 * half, ffn_in.shape[2]
    once = lambda *shape: pl.BlockSpec(shape, lambda i, ids: (0,) * len(shape), pipeline_mode=pl.Buffered(1))
    full = lambda *shape: spec(shape, *([0] * len(shape)))
    dense = ((tokens, width), bf16)
    piece = ((SUPER, LANES + width // SUPER // 2, LANES), bf16)
    outs = [dense, dense, dense, ((8, width), f32), ((8, ff), f32), piece, piece]
    out_specs = [full(*s) for s, _ in outs]
    out_specs[4] = spec((8, chunk), 0, step)
    return call(
        functools.partial(feed_bwd_kernel, layer=layer, parts=parts), "feed_backward", (ff // chunk,), ids,
        row_tiles(half, width, gathered)
        + [
            once(tokens, width), once(tokens, 128), once(tokens, width), once(tokens, 128),
            full(*ln_scale.shape), spec((1, chunk, width), layer, step, 0), spec((tokens, chunk), 0, step),
            spec((1, width, chunk), layer, 0, step), spec((1, width, width), layer, 0, 0),
            spec((tokens, chunk), 0, step), once(tokens, width), once(*ctx_own.shape), once(*ctx_shared.shape),
        ],
        [grad, grad, grad, n2, r2, n1, r1, ln_scale, ffn_out, slope, ffn_in, w_out, act, mixed, ctx_own,
         ctx_shared],
        out_specs, [shape_of(s, d) for s, d in outs],
        [
            pltpu.VMEM((tokens, width), f32), pltpu.VMEM((tokens, width), f32),
            pltpu.VMEM((tokens, width), bf16), pltpu.VMEM((tokens, chunk), bf16),
            pltpu.VMEM((LANES, tokens), bf16), pltpu.VMEM((width, tokens), bf16),
        ],
    )


def joint_bwd_kernel(
    ids, x0, x1, x2, own_ref, shared_ref, arrived_ref, w_ref, attn_ref, rel0_ref, rel1_ref, vec_ref, pre_sum_ref,
    h_ref, keep_ref, send_ref, acc_ref, x_t, sums_ref, mine_ref,
    *, split,
):
    j = pl.program_id(0)
    width = x_t.shape[0]
    rows = width // SUPER
    half = rows // 2

    @pl.when(j == 0)
    def _():
        x_t[...] = jnp.concatenate([x0[0].T, x1[0].T, x2[0].T], 1)
        sums_ref[...] = jnp.zeros_like(sums_ref)

    far = arrived_ref[0].astype(f32) * (j > 0).astype(f32)
    near = (shared_ref[0].astype(f32) + far).astype(bf16)
    joint = jnp.concatenate([own_ref[0], near], 0)
    part = dot_nt(joint, w_ref[0])
    if split:
        mine_ref[...] = joint

    @pl.when(j == 0)
    def _():
        flag = (ids[1] == 0).astype(f32) if split else 1.0
        acc_ref[...] = part + attn_ref[...].astype(f32) * flag

    @pl.when(j > 0)
    def _():
        acc_ref[...] += part

    for side in range(2):
        lanes = slice(LANES * side, LANES * side + LANES)

        @pl.when(ids[1] == side)
        def _():
            if not split:
                mine_ref[...] = joint[:, lanes]
            sums_ref[j, :, lanes] = jnp.broadcast_to(col_sum(mine_ref[...].astype(f32)), (8, LANES))

    result = dot(x_t[...], mine_ref[...]).astype(bf16)
    for group in range(3):

        @pl.when(j == group)
        def _():
            for slab in range(SUPER):
                store_piece(ids, keep_ref, send_ref, slab, half, group * half,
                            result[rows * slab : rows * slab + rows])

    @pl.when(j == pl.num_programs(0) - 1)
    def _():
        h_ref[...] = acc_ref[...].astype(bf16)
        rel = (rel0_ref[...] + rel1_ref[...]).astype(bf16)
        count = rel.shape[0] // SUPER
        lines = jnp.concatenate([vec_ref[0:6, :], sums_ref[0, 0:1], sums_ref[2, 0:1]], 0)
        blank = jnp.zeros((8, LANES - rows), f32)
        for slab in range(SUPER):
            narrow = jnp.concatenate([lines[:, rows * slab : rows * slab + rows], blank], 1)
            wide = pre_sum_ref[0:1, LANES * slab : LANES * slab + LANES]
            small = jnp.concatenate([narrow, wide, jnp.zeros((count - 9, LANES), f32)], 0).astype(bf16)
            both = jnp.concatenate([rel[count * slab : count * slab + count], small], 0)
            store_piece(ids, keep_ref, send_ref, slab, count, 3 * half, both)


def joint_bwd(ids, x, gathered, own, shared, arrived, w_qkv, g_attn, rel0, rel1, vec, pre_sum, layer, split):
    _, length, cols = own.shape
    width = g_attn.shape[1]
    half = shared.shape[1]
    tokens = length + half
    full = lambda *shape: spec(shape, *([0] * len(shape)))
    side = lambda i, ids: 0 if split else ids[1]
    piece = (SUPER, (width // SUPER // 2) * 3 + rel0.shape[0] // SUPER, LANES)
    return call(
        functools.partial(joint_bwd_kernel, split=split), "projections_backward", (3,), ids,
        row_tiles(half, width, gathered)
        + [
            spec((1, length, cols), step, 0, 0), spec((1, half, cols), step, 0, 0),
            spec((1, half, cols), lambda i, ids: jnp.maximum(i - 1, 0), 0, 0),
            spec((1, width, cols), layer, 0, lambda i, ids: 2 * i + ids[1] if split else i),
            full(tokens, width), spec((rel0.shape[0], LANES), 0, side), spec((rel0.shape[0], LANES), 0, side),
            full(*vec.shape), full(*pre_sum.shape),
        ],
        [x, x, x, own, shared, arrived, w_qkv, g_attn, rel0, rel1, vec, pre_sum],
        [full(tokens, width), full(*piece), full(*piece)],
        [shape_of((tokens, width), bf16), shape_of(piece, bf16), shape_of(piece, bf16)],
        [
            pltpu.VMEM((tokens, width), f32), pltpu.VMEM((width, tokens), bf16),
            pltpu.VMEM((3, 8, width), f32), pltpu.VMEM((tokens, LANES), bf16),
        ],
    )


def place_rows_kernel(ids, own_ref, other_ref, out_ref):
    i = pl.program_id(0)
    core = ids[0]
    row = i // 2
    mine = jnp.where(row == 2, (i - 4) == core, row == core)

    @pl.when(mine)
    def _():
        out_ref[0] = own_ref[0].astype(out_ref.dtype)

    @pl.when(jnp.logical_not(mine))
    def _():
        out_ref[0] = other_ref[0].astype(out_ref.dtype)


def place_rows(ids, own, other, dtype):
    tokens, width = own.shape
    half = tokens // 3
    tile = lambda i, ids: jnp.where(i < 4, i % 2, 2)
    tiles = lambda x: x.reshape(3, half, width)
    return call(
        place_rows_kernel, "place_rows", (6,), ids,
        [spec((1, half, width), tile, 0, 0)] * 2, [tiles(own), tiles(other)],
        spec((1, half, width), step, 0, 0), shape_of((6, half, width), dtype),
    )


def collect(ids, refs, scratch):
    for core in range(2):
        for side in range(2):

            @pl.when((ids[0] == core) & (ids[1] == side))
            def _():
                scratch[core, side] = refs[0][...]
                scratch[core, 1 - side] = refs[1][...]
                scratch[1 - core, side] = refs[2][...]
                scratch[1 - core, 1 - side] = refs[3][...]


def spread_columns(scratch, out_ref, layer, at, groups, rows, inner=False):
    for core in range(2):
        for side in range(2):
            for g in range(groups):
                piece = scratch[core, side, at + g * rows : at + g * rows + rows, :]
                lane = ((g * 2 + side) if inner else (side * groups + g)) * LANES
                out_ref[layer, core * rows : core * rows + rows, lane : lane + LANES] = piece.astype(f32)


def unpack_feed_kernel(ids, *refs):
    inputs, (in_ref, out_ref, w_out_ref, scratch) = refs[:8], refs[8:]
    high = LANES // 2
    for layer in range(2):
        collect(ids, inputs[4 * layer : 4 * layer + 4], scratch)
        columns = [scratch[core, side, 0:high, :] for side in range(2) for core in range(2)]
        out_ref[layer] = jnp.concatenate(columns, 0).astype(f32).T
        rows = in_ref.shape[1] // 2
        spread_columns(scratch, in_ref, layer, high, 4, rows)
        spread_columns(scratch, w_out_ref, layer, high + 4 * rows, 1, rows)


def unpack_attention_kernel(ids, *refs):
    inputs = refs[:8]
    qkv_ref, rel_ref, qv_ref, out_bias_ref, scale_ref, shift_ref, in_bias_ref, ffn_bias_ref = refs[8:16]
    scratch = refs[16]
    rows = qkv_ref.shape[1] // 2
    wide = 2 * rows
    for layer in range(2):
        collect(ids, inputs[4 * layer : 4 * layer + 4], scratch)
        spread_columns(scratch, qkv_ref, layer, 0, 3, rows, True)
        at = 3 * rows
        count = rel_ref.shape[2]
        rel = jnp.concatenate([scratch[0, side, at : at + count, :] for side in range(2)], 1).astype(f32)
        size = rel_ref.shape[3]
        for head in range(rel_ref.shape[1]):
            rel_ref[layer, head] = rel[:, size * head : size * head + size]
        small = scratch[1, 0, at : at + count, :].astype(f32)
        scale_ref[layer] = small[0:2, 0:wide]
        shift_ref[layer] = small[2:4, 0:wide]
        out_bias_ref[layer : layer + 1] = small[4:5, 0:wide]
        ffn_bias_ref[layer : layer + 1] = small[5:6, 0:wide]
        other = scratch[1, 1, at : at + count, :].astype(f32)
        qv_ref[layer] = small[6:8, 0:wide] + other[6:8, 0:wide]
        in_bias_ref[layer : layer + 1] = small[8:9]


def unpack(kernel, name, ids, pieces, shapes):
    full = lambda *shape: spec(shape, *([0] * len(shape)))
    return call(
        kernel, name, (1,), ids, [full(*p.shape) for p in pieces], pieces,
        [full(*s) for s in shapes], [shape_of(s, f32) for s in shapes],
        [pltpu.VMEM((2, 2) + pieces[0].shape, bf16)],
    )


def body(
    stream, cotangent, segments, word_boxes, valid_mask, w_qkv, qv_bias, w_out, out_bias, rel_proj,
    ln_scale, ln_shift, ffn_in, ffn_in_bias, ffn_out, ffn_out_bias,
):
    sections = lax.axis_size("section")
    dp = lax.axis_size("dp")
    section = lax.axis_index("section")
    dp_index = lax.axis_index("dp")
    core, side = section % 2, section // 2
    rows, length, width = stream.shape
    layers = w_qkv.shape[0]
    ff = ffn_in.shape[2]
    half = length // 2
    assert rows == 3 and sections == 4 and layers == 2 and dp % SUPER == 0 and width == 2 * LANES
    fine = dp // SUPER
    ids = jnp.stack([core, side, dp_index // fine]).astype(jnp.int32)
    weights = (w_out, out_bias, ln_scale, ln_shift, ffn_in, ffn_in_bias, ffn_out, ffn_out_bias)
    rel_pairs = rel_proj.reshape(layers, width // 128, 128, 128)

    def flip(x, bit):
        return lax.ppermute(x, "section", [(i, i ^ bit) for i in range(sections)])

    def flip_dp(x, bit):
        return lax.ppermute(x, "dp", [(i, i ^ bit) for i in range(dp)])

    tables = make_tables(ids, word_boxes, segments, valid_mask)
    ctab, stab, valid_col = tables[3], tables[4], tables[7]

    halves = lambda x: x.reshape(-1, half, width)
    x, gathered = halves(stream), True
    kept = []
    for l in range(layers):
        joint, turned, kv = project(ids, x, gathered, w_qkv, qv_bias, rel_pairs, ctab, stab, l)
        kv_far = flip(kv, 1)
        ctx_own, lse_own = attention_fwd(ids, False, tables, joint, turned, None)
        ctx_shared, lse_shared = attention_fwd(ids, True, tables, joint, turned, kv_far)
        n1, r1, n2, r2, mixed, act, slope, out, squares = feed_fwd(
            ids, x, gathered, ctx_own, ctx_shared, valid_col, weights, l
        )
        kept.append(
            dict(x=x, gathered=gathered, joint=joint, turned=turned, kv_far=kv_far, ctx_own=ctx_own,
                 ctx_shared=ctx_shared, lse_own=lse_own, lse_shared=lse_shared, norms=(n1, r1, n2, r2),
                 mixed=mixed, act=act, slope=slope, out=out, squares=squares)
        )
        x, gathered = halves(out), False

    clock = [ids]

    def pin(state):
        clock[0], state = lax.optimization_barrier((clock[0], state))
        return state

    def absorb(keep, arrived):
        keep, arrived = pin((keep, arrived))
        n = keep.shape[0] // 2
        return pin((keep[:n] + arrived[:n], keep[n:] + arrived[n:]))

    def last(keep, arrived):
        keep, arrived = pin((keep, arrived))
        x = (keep + arrived)[0]
        bit = 1
        while bit < fine:
            x = x + flip_dp(x, bit)
            bit *= 2
        return pin(x)

    def hop(state, bit):
        return state[0], flip_dp(state[1], fine << bit)

    def all_sides(x):
        far = flip(x, 2)
        return [x, far, flip(x, 1), flip(far, 1)]

    def feed_back(l, grad, gathered):
        k = kept[l]
        g_mixed, g_attn, g_ctx, vec, pre_sum, keep, send = feed_bwd(
            clock[0], grad, gathered, k["norms"], k["slope"], k["act"], k["mixed"], k["ctx_own"],
            k["ctx_shared"], weights, l,
        )
        k["g_mixed"] = g_mixed
        return g_attn, g_ctx, vec, pre_sum, (keep, flip(send, 1))

    def attention_back(l, shared, g_ctx):
        k = kept[l]
        return attention_bwd(
            clock[0], shared, tables, k["joint"], k["turned"], k["kv_far"] if shared else None,
            k["lse_shared" if shared else "lse_own"], g_ctx, rel_pairs, l, l == 0,
        )

    def joint_back(l, own_grads, shared_keep, arrived, g_attn, rel_own, rel_shared, vec, pre_sum):
        k = kept[l]
        g_h, keep, send = joint_bwd(
            clock[0], k["x"], k["gathered"], own_grads, shared_keep, arrived, w_qkv, g_attn, rel_own,
            rel_shared, vec, pre_sum, l, l == 0,
        )
        k["g_h"] = g_h
        return g_h, (keep, flip(send, 1))

    g_attn, g_ctx, vec, pre_sum, f1 = feed_back(1, halves(cotangent), True)
    shared_keep, shared_send, rel_shared = attention_back(1, True, g_ctx)
    arrived = flip(shared_send, 1)
    f1 = hop(absorb(*f1), 0)
    own_grads, rel_own = attention_back(1, False, g_ctx)
    g_h, a1 = joint_back(1, own_grads, shared_keep, arrived, g_attn, rel_own, rel_shared, vec, pre_sum)

    f1 = hop(absorb(*f1), 1)
    a1 = hop(absorb(*a1), 0)
    g_attn, g_ctx, vec, pre_sum, f0 = feed_back(0, halves(g_h), False)
    f1 = hop(absorb(*f1), 2)
    a1 = hop(absorb(*a1), 1)
    shared_keep, shared_send, rel_shared = attention_back(0, True, g_ctx)
    arrived = flip(shared_send, 1)
    f0 = hop(absorb(*f0), 0)
    own_grads, rel_own = attention_back(0, False, g_ctx)
    f1 = last(*f1)
    a1 = hop(absorb(*a1), 2)
    g_h, a0 = joint_back(0, own_grads, shared_keep, arrived, g_attn, rel_own, rel_shared, vec, pre_sum)
    g_h_far = flip(g_h, 2)
    f1 = all_sides(f1)
    f0 = hop(absorb(*f0), 1)
    a0 = hop(absorb(*a0), 0)
    a1 = all_sides(last(*a1))

    def of_layer(name):
        return jnp.where(side == 0, kept[0][name], kept[1][name])

    def to_section(first, second, dtype):
        a, b = of_layer(first), of_layer(second)
        own, away = jnp.where(core == 0, a, b), jnp.where(core == 0, b, a)
        return place_rows(ids, own, flip(away, 1), dtype).reshape(1, rows, length, width)

    section_outs = pin(to_section("mixed", "out", bf16))
    a0 = hop(absorb(*a0), 1)
    f0 = hop(absorb(*f0), 2)
    kept[0]["g_h"] = pin(g_h + g_h_far)
    in_grads = pin(to_section("g_h", "g_mixed", f32))
    a0 = hop(absorb(*a0), 2)
    f0 = all_sides(last(*f0))
    a0 = all_sides(last(*a0))

    squares_mine = jnp.sum(of_layer("squares"), 1).reshape(2, 2, 2)
    squares_far = flip(squares_mine, 1)
    sub = lambda v: lax.dynamic_index_in_dim(v, core, 0, keepdims=False)
    near, far = sub(squares_mine), sub(squares_far)
    first = jnp.where(core == 0, near[:, 0], far[:, 0])
    second = jnp.where(core == 0, far[:, 0], near[:, 0])
    square_rows = jnp.stack([first, second, near[:, 1] + far[:, 1]])
    row_counts = jnp.sum(valid_mask.astype(f32), 1)
    root_mean_squares = jnp.sqrt(square_rows / (width * jnp.maximum(row_counts, 1.0))[:, None])[None]

    slab = width // SUPER
    d_ffn_in, d_ffn_out, d_out = unpack(
        unpack_feed_kernel, "unpack_feed", clock[0], f0 + f1,
        [(2, slab, ff), (2, ff // SUPER, width), (2, slab, width)],
    )
    d_ffn_in, d_ffn_out, d_out = pin((d_ffn_in, d_ffn_out, d_out))
    rel_rows = 128 // SUPER
    d_qkv, d_rel, d_qv, d_out_bias, d_scale, d_shift, d_in_bias, d_ffn_bias = unpack(
        unpack_attention_kernel, "unpack_attention", clock[0], a0 + a1,
        [(2, slab, 3 * width), (2, rel_proj.shape[1], rel_rows, rel_proj.shape[2]), (2, 2, slab), (2, slab),
         (2, 2, slab), (2, 2, slab), (2, LANES), (2, slab)],
    )

    def own_part(x, axis):
        n = x.shape[axis] // fine
        return x if fine == 1 else lax.dynamic_slice_in_dim(x, (dp_index % fine) * n, n, axis)

    return (
        section_outs,
        in_grads,
        own_part(d_qkv, 1),
        own_part(d_qv, 2),
        own_part(d_out, 1),
        own_part(d_out_bias, 1),
        own_part(jnp.swapaxes(d_rel, 2, 3), 3),
        own_part(d_scale, 2),
        own_part(d_shift, 2),
        own_part(d_ffn_in, 1),
        own_part(d_in_bias, 1),
        own_part(d_ffn_out, 1),
        own_part(d_ffn_bias, 1),
        root_mean_squares,
    )


def solution(mesh):
    return jax.shard_map(
        body,
        mesh=mesh,
        in_specs=(
            P("dp", None, None),
            P("dp", None, None),
            P("dp", None),
            P(None, "dp", None),
            P("dp", None),
        )
        + (P(),) * 11,
        out_specs=(
            P("section", "dp", None, None),
            P("section", "dp", None, None),
            P(None, "dp", None),
            P(None, None, "dp"),
            P(None, "dp", None),
            P(None, "dp"),
            P(None, None, None, "dp"),
            P(None, None, "dp"),
            P(None, None, "dp"),
            P(None, "dp", None),
            P(None, "dp"),
            P(None, "dp", None),
            P(None, "dp"),
            P("section", "dp", None),
        ),
        check_vma=False,
    )
```

```python
import functools

import jax
import jax.numpy as jnp
from jax import lax
from jax.experimental import pallas as pl
from jax.experimental.pallas import tpu as pltpu
from jax.sharding import PartitionSpec as P

ln_eps = 1e-05
masked_score = -1e30
bf16 = jnp.bfloat16
f32 = jnp.float32
MB = 1 << 20
SUPER = 8
LANES = 384
NORM_ROWS = 64

ERF_COEFS = (
    0.7978849414899046, 0.0363330844086688, -3.259474462099993e-05, -5.5306316685416947e-05,
    3.964773125473232e-06, -1.322662757755248e-07, 1.7562773256476674e-09,
)


def dot(a, b):
    return lax.dot_general(a, b, (((1,), (0,)), ((), ())), preferred_element_type=f32)


def dot_nt(a, b):
    return lax.dot_general(a, b, (((1,), (1,)), ((), ())), preferred_element_type=f32)


def gelu_and_slope(x):
    square = x * x
    g = ERF_COEFS[-1]
    for c in ERF_COEFS[-2::-1]:
        g = g * square + c
    phi = 0.5 * jnp.tanh(x * g) + 0.5
    density = jnp.exp2(square * (-0.5 * 1.4426950408889634)) * 0.3989422804014327
    return x * phi, phi + x * density


def norm_parts(residual):
    average = jnp.mean(residual, -1, keepdims=True)
    centered = residual - average
    inverse = lax.rsqrt(jnp.mean(centered * centered, -1, keepdims=True) + ln_eps)
    return centered * inverse, inverse


def norm_back(gradient, gain, normed, inverse):
    dnormed = gradient * gain
    return inverse * (
        dnormed
        - jnp.mean(dnormed, -1, keepdims=True)
        - normed * jnp.mean(dnormed * normed, -1, keepdims=True)
    )


def row_loop(count, chunk, sums):
    for i in range(count):
        sums = chunk(i, sums)
    return sums


def fold(x):
    return jnp.sum(x.reshape(-1, 8, x.shape[1]), 0)


def col_sum(x):
    return jnp.sum(x, 0, keepdims=True)


COST_US = dict(
    tables=4, projections=8, attention_forward=7, feed_forward=24, feed_backward=30, attention_backward=12,
    projections_backward=3, place_rows=4,
    unpack_feed=4, unpack_attention=3,
)


def call(kernel, name, grid, ids, in_specs, inputs, out_specs, out_shape, scratch=(), micros=None):
    micros = COST_US[name] if micros is None else micros
    cost = pl.CostEstimate(flops=micros * 1100000000, bytes_accessed=micros * 1000000, transcendentals=0)
    return pl.pallas_call(
        kernel,
        grid_spec=pltpu.PrefetchScalarGridSpec(
            num_scalar_prefetch=1,
            grid=grid,
            in_specs=in_specs,
            out_specs=out_specs,
            scratch_shapes=list(scratch),
        ),
        out_shape=out_shape,
        compiler_params=pltpu.CompilerParams(vmem_limit_bytes=62 * MB),
        cost_estimate=cost,
        name=name,
    )(ids, *inputs)


def spec(shape, *index):
    def index_map(i, ids):
        return tuple(x(i, ids) if callable(x) else x for x in index)

    return pl.BlockSpec(shape, index_map)


def shape_of(shape, dtype):
    return jax.ShapeDtypeStruct(shape, dtype)


step = lambda i, ids: i


def row_tiles(half, width, gathered):
    if not gathered:
        return [spec((1, half, width), t, 0, 0) for t in range(3)]
    core = lambda ids: ids[0]
    return [
        spec((1, half, width), lambda i, ids: 2 * core(ids), 0, 0),
        spec((1, half, width), lambda i, ids: 2 * core(ids) + 1, 0, 0),
        spec((1, half, width), lambda i, ids: 4 + core(ids), 0, 0),
    ]


def tables_kernel(
    ids, boxes_ref, seg_ref, valid_ref,
    cos_ref, sin_ref, kf_ref, ctab_ref, stab_ref, code_ref, segrow_ref, valid_col_ref,
):
    core = ids[0]
    length = seg_ref.shape[1]
    half = length // 2

    def ordered(read):
        near = pl.multiple_of(core * half, half)
        far = pl.multiple_of((1 - core) * half, half)
        return jnp.concatenate(
            [read(pl.ds(core, 1), slice(None)), read(2, pl.ds(near, half)), read(2, pl.ds(far, half))], 1
        )

    def row_of(ref):
        def read(r, c):
            r = pl.ds(2, 1) if isinstance(r, int) else r
            return ref[r, c]
        return ordered(read)

    count = length * 2
    at = lax.broadcasted_iota(jnp.int32, (1, count), 1)
    shared = jnp.where(
        at < length + half, at - length + core * half, at - length - half + (1 - core) * half
    )
    position = jnp.where(at < length, at, shared).astype(f32)
    rate_at = lax.broadcasted_iota(jnp.int32, (32, 1), 0).astype(f32)
    text = position * jnp.exp(rate_at * (-9.210340371976184 / 32))
    box_rate = jnp.exp2(-lax.broadcasted_iota(jnp.int32, (8, 1), 0).astype(f32))
    angles = [text]
    for c in range(4):
        coords = row_of(boxes_ref.at[:, c]).astype(f32)
        angles.append(coords * box_rate)
    angles = jnp.concatenate(angles, 0)
    cosines, sines = jnp.cos(angles), jnp.sin(angles)
    cos_ref[...], sin_ref[...] = cosines, sines
    kf_ref[...] = jnp.concatenate([cosines, sines], 0).T.astype(bf16)
    ctab_ref[...] = jnp.concatenate([cosines, -cosines], 0).T
    stab_ref[...] = jnp.concatenate([sines, sines], 0).T
    seg = row_of(seg_ref).astype(f32)
    valid = row_of(valid_ref).astype(f32)
    segrow_ref[...] = jnp.broadcast_to(seg, segrow_ref.shape)
    code_ref[...] = jnp.broadcast_to(jnp.where(valid > 0, seg, -1.0), (128, count)).T
    valid_col_ref[...] = jnp.broadcast_to(valid, (128, count)).T


def make_tables(ids, word_boxes, segments, valid_mask):
    length = segments.shape[1]
    count = 2 * length
    full = lambda *shape: spec(shape, *([0] * len(shape)))
    outs = [
        ((64, count), f32), ((64, count), f32), ((count, 128), bf16), ((count, 128), f32),
        ((count, 128), f32), ((count, 128), f32), ((8, count), f32), ((count, 128), f32),
    ]
    return call(
        tables_kernel, "tables", (1,), ids,
        [full(*word_boxes.shape), full(*segments.shape), full(*valid_mask.shape)],
        [word_boxes, segments, valid_mask],
        [full(*s) for s, _ in outs], [shape_of(s, d) for s, d in outs],
    )


def qkv_kernel(
    ids, x0, x1, x2, w_ref, bias_ref, rel_ref, ctab_ref, stab_ref, joint_ref, turned_ref, kv_ref, x_ref,
    *, layer,
):
    j = pl.program_id(0)
    half = x0.shape[1]

    @pl.when(j == 0)
    def _():
        x_ref[0:half], x_ref[half : 2 * half], x_ref[2 * half :] = x0[0], x1[0], x2[0]

    flags = [(j == 0).astype(f32), (j == 2).astype(f32)]
    bias = bias_ref[layer, 0:1, :].astype(f32) * flags[0] + bias_ref[layer, 1:2, :].astype(f32) * flags[1]
    joint = (dot(x_ref[...], w_ref[0]) + bias).astype(bf16)
    joint_ref[...] = joint
    kv_ref[...] = joint[2 * half :]

    @pl.when(j == 0)
    def _():
        ctab, stab = ctab_ref[...], stab_ref[...]
        row = lax.broadcasted_iota(jnp.int32, (128, 128), 0)
        for p in range(rel_ref.shape[1]):
            rel = rel_ref[0, p]
            zero = jnp.zeros_like(rel)
            block = jnp.concatenate([jnp.where(row < 64, rel, zero), jnp.where(row < 64, zero, rel)], 1)
            coef = dot(joint[:, 128 * p : 128 * p + 128], block)
            for e in range(2):
                c = coef[:, 128 * e : 128 * e + 128]
                at = 256 * p + 128 * e
                turned_ref[:, at : at + 128] = (c * ctab + pltpu.roll(c, 64, 1) * stab).astype(bf16)


def project(ids, x, gathered, w_qkv, qv_bias, rel_pairs, ctab, stab, layer):
    half, width = x.shape[1], x.shape[2]
    tokens = 3 * half
    pairs = rel_pairs.shape[1]
    return call(
        functools.partial(qkv_kernel, layer=layer), "projections", (3,), ids,
        row_tiles(half, width, gathered)
        + [
            spec((1, width, width), layer, 0, step), spec(qv_bias.shape, 0, 0, 0),
            spec((1, pairs, 128, 128), layer, 0, 0, 0), spec((tokens, 128), 0, 0),
            spec((tokens, 128), 0, 0),
        ],
        [x, x, x, w_qkv, qv_bias, rel_pairs, ctab, stab],
        [
            spec((tokens, width), 0, step), spec((tokens, 2 * width), 0, 0),
            spec((half, width), 0, lambda i, ids: jnp.maximum(i - 1, 0)),
        ],
        [
            shape_of((tokens, 3 * width), bf16), shape_of((tokens, 2 * width), bf16),
            shape_of((half, 2 * width), bf16),
        ],
        [pltpu.VMEM((tokens, width), bf16)],
    )


def lane_half(shape, half):
    lane = lax.broadcasted_iota(jnp.int32, shape, 1)
    return (lane < 64) if half == 0 else (lane >= 64)


def only_half(x, half):
    return jnp.where(lane_half(x.shape, half), x, jnp.zeros_like(x))


def fill_bias(code_ref, seg_ref, bias_ref):
    shape = bias_ref.shape
    code = jnp.concatenate([code_ref[...]] * (shape[1] // 128), 1)
    same = code == seg_ref[0:1, :]
    key_at = lax.broadcasted_iota(jnp.int32, shape, 0)
    query_at = lax.broadcasted_iota(jnp.int32, shape, 1)
    bias_ref[...] = jnp.where(same | (key_at == query_at), 0.0, masked_score)


def attention_fwd_kernel(
    ids, code_ref, seg_ref, kf_ref, q_ref, turned_ref, k_ref, v_ref, *rest, per_step, shared,
):
    if shared:
        k_far, v_far, ctx_ref, lse_ref, bias_ref, k_all, v_all = rest
        half = k_ref.shape[0]
        k_all[0:half], k_all[half:] = k_ref[...], k_far[...]
        v_all[0:half], v_all[half:] = v_ref[...], v_far[...]
        k_ref, v_ref = k_all, v_all
    else:
        ctx_ref, lse_ref, bias_ref = rest

    @pl.when(pl.program_id(0) == 0)
    def _():
        fill_bias(code_ref, seg_ref, bias_ref)

    scale = jnp.asarray(0.125, bf16)
    units = [(pair, e) for pair in range(per_step) for e in range(2)]
    values_t = {}

    def scores_of(unit):
        pair, e = unit
        at = slice(128 * pair, 128 * pair + 128)
        turned = turned_ref[:, 256 * pair + 128 * e : 256 * pair + 128 * e + 128]
        qside = jnp.concatenate([turned, only_half(q_ref[:, at], e)], 1) * scale
        kside = jnp.concatenate([kf_ref[...], k_ref[:, at]], 1)
        return dot_nt(kside, qside) + bias_ref[...]

    def finish(unit, scores):
        pair, e = unit
        top = jnp.max(scores, 0, keepdims=True)
        expo = jnp.exp(scores - top)
        total = jnp.sum(expo, 0, keepdims=True)
        if pair not in values_t:
            values_t[pair] = v_ref[:, 128 * pair : 128 * pair + 128].T
        ctx = dot(values_t[pair][64 * e : 64 * e + 64], expo.astype(bf16))
        at = 128 * pair + 64 * e
        ctx_ref[at : at + 64, :] = (ctx * (1.0 / total)).astype(bf16)
        lse_ref[pair, e : e + 1, :] = top + jnp.log(total)

    scores = scores_of(units[0])
    for i, unit in enumerate(units):
        upcoming = scores_of(units[i + 1]) if i + 1 < len(units) else None
        finish(unit, scores)
        scores = upcoming


def attention_fwd(ids, shared, tables, joint, turned, kv_far, per_step=2):
    cos_t, sin_t, kf, ctab, stab, code, seg, valid = tables
    tokens, width = joint.shape[0], joint.shape[1] // 3
    half = tokens // 3
    nk = 2 * half
    nq = half if shared else nk
    key_rows = half if shared else nk
    lanes = 128 * per_step
    steps = width // lanes
    q_row = 2 if shared else 0
    at = lambda off: (lambda i, ids: i + off)
    in_specs = [
        spec((nk, 128), int(shared), 0), spec((8, nq), 0, q_row), spec((nk, 128), int(shared), 0),
        spec((nq, lanes), q_row, step), spec((nq, 2 * lanes), q_row, step),
        spec((key_rows, lanes), q_row, at(steps)), spec((key_rows, lanes), q_row, at(2 * steps)),
    ]
    inputs = [code, seg, kf, joint, turned, joint, joint]
    scratch = [pltpu.VMEM((nk, nq), f32)]
    if shared:
        in_specs += [spec((half, lanes), 0, step), spec((half, lanes), 0, at(steps))]
        inputs += [kv_far, kv_far]
        scratch += [pltpu.VMEM((nk, lanes), bf16)] * 2
    return call(
        functools.partial(attention_fwd_kernel, per_step=per_step, shared=shared),
        "attention_forward", (steps,), ids, in_specs, inputs,
        [spec((lanes, nq), step, 0), spec((per_step, 2, nq), step, 0, 0)],
        [shape_of((width, nq), bf16), shape_of((width // 128, 2, nq), f32)],
        scratch,
    )


def attention_bwd_kernel(
    ids, code_ref, seg_ref, kf_ref, cos_ref, sin_ref, rel_ref, lse_ref, gc_ref, q_ref, turned_ref,
    k_ref, v_ref, *rest, per_step, shared,
):
    if shared:
        k_far, v_far, keep_ref, send_ref, drel_ref, bias_ref, kft_ref, k_all, v_all = rest
        half = k_ref.shape[0]
        k_all[0:half], k_all[half:] = k_ref[...], k_far[...]
        v_all[0:half], v_all[half:] = v_ref[...], v_far[...]
        k_ref, v_ref = k_all, v_all
    else:
        keep_ref, drel_ref, bias_ref, kft_ref = rest

    @pl.when(pl.program_id(0) == 0)
    def _():
        fill_bias(code_ref, seg_ref, bias_ref)
        kft_ref[...] = kf_ref[...].T

    scale = jnp.asarray(0.125, bf16)
    cosines, sines = cos_ref[...], sin_ref[...]
    units = [(pair, e) for pair in range(per_step) for e in range(2)]
    store = {}

    def scores_of(unit):
        pair, e = unit
        at = slice(128 * pair, 128 * pair + 128)
        q_mine = only_half(q_ref[:, at], e)
        gc_mine = only_half(gc_ref[:, at], e)
        q_scaled = q_mine * scale
        turned = turned_ref[:, 256 * pair + 128 * e : 256 * pair + 128 * e + 128]
        qside = jnp.concatenate([turned * scale, q_scaled], 1)
        kside = jnp.concatenate([kf_ref[...], k_ref[:, at]], 1)
        scores = dot_nt(kside, qside) + bias_ref[...]
        gp = dot_nt(v_ref[:, at], gc_mine)
        return scores, gp, q_mine, gc_mine, q_scaled

    def finish(unit, parts):
        pair, e = unit
        scores, gp, q_mine, gc_mine, q_scaled = parts
        at = slice(128 * pair, 128 * pair + 128)
        shares = jnp.exp(scores - lse_ref[pair, e : e + 1, :])
        dv = dot(shares.astype(bf16), gc_mine)
        weighted = shares * gp
        delta = jnp.sum(weighted, 0, keepdims=True)
        gs = (weighted - shares * delta).astype(bf16)
        dk = dot(gs, q_scaled)
        if pair not in store:
            store[pair] = k_ref[:, at].T
        side_t = jnp.concatenate([kft_ref[...], store[pair][64 * e : 64 * e + 64]], 0)
        dside = dot(side_t, gs) * 0.125
        g_cos, g_sin = dside[0:64], dside[64:128]
        gcoef = jnp.concatenate(
            [g_cos * cosines + g_sin * sines, g_cos * sines - g_sin * cosines], 0
        ).astype(bf16)
        dq = dside[128:192] + dot(rel_ref[0, pair, 64 * e : 64 * e + 64], gcoef)
        drel = dot(gcoef, q_mine)
        if e == 0:
            store["even"] = (dq, dk, dv, drel)
            return
        dq0, dk0, dv0, drel0 = store["even"]
        dq = jnp.concatenate([dq0, dq], 0).T.astype(bf16)
        dk, dv = (dk0 + dk).astype(bf16), (dv0 + dv).astype(bf16)
        drel_ref[:, at] = drel0 + drel
        n = keep_ref.shape[1]
        keep_ref[0, :, at] = dq
        keep_ref[1, :, at], keep_ref[2, :, at] = dk[0:n], dv[0:n]
        if shared:
            send_ref[0, :, at], send_ref[1, :, at] = dk[n:], dv[n:]

    parts = scores_of(units[0])
    for i, unit in enumerate(units):
        upcoming = scores_of(units[i + 1]) if i + 1 < len(units) else None
        finish(unit, parts)
        parts = upcoming


def attention_bwd(ids, shared, tables, joint, turned, kv_far, lse, g_ctx, rel_pairs, layer, split, per_step=3):
    per_step = 3 if split else per_step
    cos_t, sin_t, kf, ctab, stab, code, seg, valid = tables
    tokens, width = joint.shape[0], joint.shape[1] // 3
    half = tokens // 3
    nk = 2 * half
    nq = half if shared else nk
    key_rows = half if shared else nk
    lanes = 128 * per_step
    all_steps = width // lanes
    steps = all_steps // 2 if split else all_steps
    out_width = lanes * steps
    first = lambda ids: ids[1] * steps if split else 0
    q_row = 2 if shared else 0
    at = lambda off: (lambda i, ids: first(ids) + i + off)
    here = at(0)
    in_specs = [
        spec((nk, 128), int(shared), 0), spec((8, nq), 0, q_row), spec((nk, 128), int(shared), 0),
        spec((64, nq), 0, q_row), spec((64, nq), 0, q_row),
        spec((1, per_step, 128, 128), layer, here, 0, 0),
        spec((per_step, 2, nq), here, 0, 0), spec((nq, lanes), q_row, here),
        spec((nq, lanes), q_row, here), spec((nq, 2 * lanes), q_row, here),
        spec((key_rows, lanes), q_row, at(all_steps)), spec((key_rows, lanes), q_row, at(2 * all_steps)),
    ]
    inputs = [code, seg, kf, cos_t, sin_t, rel_pairs, lse, g_ctx, joint, turned, joint, joint]
    scratch = [pltpu.VMEM((nk, nq), f32), pltpu.VMEM((128, nk), bf16)]
    out_specs = [spec((3, key_rows, lanes), 0, 0, step)]
    out_shape = [shape_of((3, key_rows, out_width), bf16)]
    if shared:
        in_specs += [spec((half, lanes), 0, here), spec((half, lanes), 0, at(all_steps))]
        inputs += [kv_far, kv_far]
        scratch += [pltpu.VMEM((nk, lanes), bf16)] * 2
        out_specs.append(spec((2, half, lanes), 0, 0, step))
        out_shape.append(shape_of((2, half, out_width), bf16))
    out_specs.append(spec((128, lanes), 0, step))
    out_shape.append(shape_of((128, out_width), f32))
    return call(
        functools.partial(attention_bwd_kernel, per_step=per_step, shared=shared),
        "attention_backward", (steps,), ids, in_specs, inputs, out_specs, out_shape, scratch,
        40 if shared else 12,
    )


def feed_fwd_kernel(
    ids, x0, x1, x2, own_ref, shared_ref, valid_ref, w_out_ref, out_bias_ref, scale_ref, shift_ref,
    in_ref, in_bias_ref, out_ref, ffn_bias_ref,
    n1_ref, r1_ref, n2_ref, r2_ref, mixed_ref, act_ref, slope_ref, h_ref, squares_ref,
    feed_ref,
    *, layer, parts,
):
    j = pl.program_id(0)
    half = x0.shape[1]
    row = lambda ref, *at: ref[at[:-1] + (slice(at[-1], at[-1] + 1),)].astype(f32)

    rows = NORM_ROWS
    zero = jnp.zeros((8, x0.shape[2]), f32)

    def add_squares(sums, k, tile):
        for i, x in enumerate(sums):
            at = k + 2 * i + tile // 2
            squares_ref[at : at + 1, :] += col_sum(x)

    @pl.when(j == 0)
    def _():
        ctx = jnp.concatenate([own_ref[...].T, shared_ref[...].T], 0)
        feed_ref[...] = dot(ctx, w_out_ref[0])
        bias, gain, shift = row(out_bias_ref, layer), row(scale_ref, layer, 0), row(shift_ref, layer, 0)
        squares_ref[...] = jnp.zeros_like(squares_ref)
        for t, x_ref in enumerate((x0, x1, x2)):

            def chunk(i, sums):
                at = i * rows
                to = pl.ds(t * half + at, rows)
                valid = valid_ref[to, 0:1]
                attention = feed_ref[to, :] + bias
                normed, inverse = norm_parts(x_ref[0, pl.ds(at, rows), :].astype(f32) + attention)
                mixed = (normed * gain + shift).astype(bf16)
                n1_ref[to, :] = normed.astype(bf16)
                r1_ref[to, :] = jnp.broadcast_to(inverse, (rows, 128))
                mixed_ref[to, :] = mixed
                mixed = mixed.astype(f32)
                return (sums[0] + fold(attention * attention * valid), sums[1] + fold(mixed * mixed * valid))

            sums = row_loop(half // rows, chunk, (zero, zero))
            add_squares(sums, 0, t)

    cols = in_ref.shape[2] // parts
    at = lambda k: slice(cols * k, cols * k + cols)
    bias = in_bias_ref[layer : layer + 1, :].astype(f32)
    pre = dot(mixed_ref[...], in_ref[0, :, at(0)]) + bias[:, at(0)]
    feed = None
    for k in range(parts):
        coming = None
        if k + 1 < parts:
            coming = dot(mixed_ref[...], in_ref[0, :, at(k + 1)]) + bias[:, at(k + 1)]
        act, slope = gelu_and_slope(pre)
        act = act.astype(bf16)
        act_ref[:, at(k)] = act
        slope_ref[:, at(k)] = slope.astype(bf16)
        part = dot(act, out_ref[0, at(k)])
        feed = part if feed is None else feed + part
        pre = coming

    @pl.when(j == 0)
    def _():
        feed_ref[...] = feed

    @pl.when(j > 0)
    def _():
        feed_ref[...] += feed

    @pl.when(j == pl.num_programs(0) - 1)
    def _():
        bias, gain, shift = row(ffn_bias_ref, layer), row(scale_ref, layer, 1), row(shift_ref, layer, 1)
        for t in range(3):

            def chunk(i, sums):
                to = pl.ds(t * half + i * rows, rows)
                valid = valid_ref[to, 0:1]
                branch = feed_ref[to, :] + bias
                normed, inverse = norm_parts(mixed_ref[to, :].astype(f32) + branch)
                out = normed * gain + shift
                n2_ref[to, :] = normed.astype(bf16)
                r2_ref[to, :] = jnp.broadcast_to(inverse, (rows, 128))
                h_ref[to, :] = out.astype(bf16)
                return (sums[0] + fold(branch * branch * valid), sums[1] + fold(out * out * valid))

            sums = row_loop(half // rows, chunk, (zero, zero))
            add_squares(sums, 4, t)


def feed_fwd(ids, x, gathered, ctx_own, ctx_shared, valid, weights, layer, chunk=768, parts=1):
    w_out, out_bias, ln_scale, ln_shift, ffn_in, ffn_in_bias, ffn_out, ffn_out_bias = weights
    half, width = x.shape[1], x.shape[2]
    tokens, ff = 3 * half, ffn_in.shape[2]
    full = lambda *shape: spec(shape, *([0] * len(shape)))
    dense = ((tokens, width), bf16)
    column = ((tokens, 128), f32)
    outs = [dense, column, dense, column, dense, ((tokens, ff), bf16), ((tokens, ff), bf16), dense,
            ((8, width), f32)]
    out_specs = [full(*s) for s, _ in outs]
    out_specs[5] = out_specs[6] = spec((tokens, chunk), 0, step)
    return call(
        functools.partial(feed_fwd_kernel, layer=layer, parts=parts), "feed_forward", (ff // chunk,), ids,
        row_tiles(half, width, gathered)
        + [
            full(*ctx_own.shape), full(*ctx_shared.shape), spec((tokens, 128), 0, 0),
            spec((1, width, width), layer, 0, 0), full(*out_bias.shape), full(*ln_scale.shape),
            full(*ln_shift.shape), spec((1, width, chunk), layer, 0, step),
            spec((ffn_in_bias.shape[0], chunk), 0, step), spec((1, chunk, width), layer, step, 0),
            full(*ffn_out_bias.shape),
        ],
        [x, x, x, ctx_own, ctx_shared, valid, w_out, out_bias, ln_scale, ln_shift, ffn_in, ffn_in_bias,
         ffn_out, ffn_out_bias],
        out_specs, [shape_of(s, d) for s, d in outs], [pltpu.VMEM((tokens, width), f32)],
    )


def slab_place(ids, slab):
    relative = jnp.bitwise_xor(ids[2], slab)
    return (
        jnp.bitwise_or(
            jnp.left_shift(jnp.bitwise_and(relative, 1), 2),
            jnp.bitwise_or(jnp.bitwise_and(relative, 2), jnp.right_shift(relative, 2)),
        )
    )


def store_piece(ids, keep_ref, send_ref, slab, core_rows, row, value):
    place = slab_place(ids, slab)
    core = ids[0]
    low, high = value[0:core_rows], value[core_rows:]
    at = slice(row, row + core_rows)

    @pl.when(core == 0)
    def _():
        keep_ref[place, at, :], send_ref[place, at, :] = low, high

    @pl.when(core != 0)
    def _():
        keep_ref[place, at, :], send_ref[place, at, :] = high, low


def feed_bwd_kernel(
    ids, g0, g1, g2, n2_ref, r2_ref, n1_ref, r1_ref, scale_ref, out_ref, slope_ref, in_ref, w_out_ref,
    act_ref, mixed_in_ref, own_ref, shared_ref,
    mixed_ref, attn_ref, ctx_ref, sums_ref, pre_sum_ref, keep_ref, send_ref,
    res_ref, acc_ref, feed_ref, pre_ref, feed_t, mixed_t, *late,
    layer, parts,
):
    j = pl.program_id(0)
    buffers, sems = late[:-1], late[-1]
    sources = (n1_ref, r1_ref, w_out_ref.at[layer], own_ref, shared_ref)
    copies = [pltpu.make_async_copy(a, b, sems.at[k]) for k, (a, b) in enumerate(zip(sources, buffers))]
    n1_ref, r1_ref, w_out_ref, own_ref, shared_ref = buffers

    @pl.when(j == 0)
    def _():
        for copy in copies:
            copy.start()

    tokens = n2_ref.shape[0]
    gain = lambda k: scale_ref[layer, k : k + 1, :].astype(f32)
    rows = NORM_ROWS

    @pl.when(j == 0)
    def _():
        sums_ref[...] = jnp.zeros_like(sums_ref)
        for t, g_ref in enumerate((g0, g1, g2)):
            count = g_ref.shape[1]

            def chunk(i, sums):
                at = i * rows
                to = pl.ds(t * count + at, rows)
                grad = g_ref[0, pl.ds(at, rows), :].astype(f32)
                normed = n2_ref[to, :].astype(f32)
                back = norm_back(grad, gain(1), normed, r2_ref[to, 0:1])
                res_ref[to, :] = back
                feed = back.astype(bf16)
                feed_ref[to, :] = feed
                return (sums[0] + fold(grad * normed), sums[1] + fold(grad), sums[2] + fold(feed.astype(f32)))

            zero = jnp.zeros((8, n2_ref.shape[1]), f32)
            sums = row_loop(count // rows, chunk, (zero, zero, zero))
            for k, x in zip((1, 3, 5), sums):
                sums_ref[k : k + 1, :] += col_sum(x)
        for side in range(2):

            @pl.when(ids[1] == side)
            def _():
                feed_t[...] = feed_ref[:, LANES * side : LANES * side + LANES].T

        mixed_t[...] = mixed_in_ref[...].T

    cols = slope_ref.shape[1] // parts
    at = lambda k: slice(cols * k, cols * k + cols)
    g_act = dot_nt(feed_ref[...], out_ref[0, at(0)])
    for k in range(parts):
        coming = dot_nt(feed_ref[...], out_ref[0, at(k + 1)]) if k + 1 < parts else None
        g_pre = (g_act * slope_ref[:, at(k)].astype(f32)).astype(bf16)
        pre_ref[:, at(k)] = g_pre
        pre_sum_ref[:, at(k)] = jnp.broadcast_to(col_sum(g_pre.astype(f32)), (8, cols))
        g_act = coming
    total = dot_nt(pre_ref[...], in_ref[0])

    @pl.when(j == 0)
    def _():
        acc_ref[...] = total

    @pl.when(j > 0)
    def _():
        acc_ref[...] += total

    high = LANES // 2
    slabs = act_ref.shape[1] // LANES
    result = dot(feed_t[...], act_ref[...]).astype(bf16)
    for k in range(slabs):
        store_piece(ids, keep_ref, send_ref, j * slabs + k, high, 0, result[:, LANES * k : LANES * k + LANES])
    width = mixed_t.shape[0]
    slab_rows = width // SUPER
    half = slab_rows // 2
    steps = 4 // slabs
    for s in range(2 * steps):

        @pl.when((j == s) & (ids[1] == s // steps))
        def _():
            result = dot(mixed_t[...], pre_ref[...]).astype(bf16)
            for slab in range(SUPER):
                for k in range(slabs):
                    store_piece(
                        ids, keep_ref, send_ref, slab, half, high + ((s % steps) * slabs + k) * half,
                        result[slab_rows * slab : slab_rows * slab + slab_rows, LANES * k : LANES * k + LANES],
                    )

    @pl.when(j == pl.num_programs(0) - 1)
    def _():
        for copy in copies:
            copy.wait()

        def chunk(i, sums):
            to = pl.ds(i * rows, rows)
            g_mixed = acc_ref[to, :] + res_ref[to, :]
            mixed_ref[to, :] = g_mixed.astype(bf16)
            normed = n1_ref[to, :].astype(f32)
            attn = norm_back(g_mixed, gain(0), normed, r1_ref[to, 0:1]).astype(bf16)
            attn_ref[to, :] = attn
            return (sums[0] + fold(g_mixed * normed), sums[1] + fold(g_mixed), sums[2] + fold(attn.astype(f32)))

        zero = jnp.zeros((8, width), f32)
        sums = row_loop(tokens // rows, chunk, (zero, zero, zero))
        for k, x in zip((0, 2, 4), sums):
            sums_ref[k : k + 1, :] = col_sum(x)
        ctx_ref[...] = dot_nt(attn_ref[...], w_out_ref[...]).astype(bf16)
        long = own_ref.shape[1]
        for side in range(2):

            @pl.when(ids[1] == side)
            def _():
                lanes = slice(LANES * side, LANES * side + LANES)
                result = dot(own_ref[...], attn_ref[0:long, lanes]) + dot(shared_ref[...], attn_ref[long:, lanes])
                result = result.astype(bf16)
                for slab in range(SUPER):
                    store_piece(ids, keep_ref, send_ref, slab, half, high + 4 * half,
                                result[slab_rows * slab : slab_rows * slab + slab_rows])


def feed_bwd(ids, grad, gathered, kept, slope, act, mixed, ctx_own, ctx_shared, weights, layer, chunk=768, parts=3):
    w_out, out_bias, ln_scale, ln_shift, ffn_in, ffn_in_bias, ffn_out, ffn_out_bias = weights
    n1, r1, n2, r2 = kept
    half, width = grad.shape[1], grad.shape[2]
    tokens, ff = 3 * half, ffn_in.shape[2]
    once = lambda *shape: pl.BlockSpec(shape, lambda i, ids: (0,) * len(shape), pipeline_mode=pl.Buffered(1))
    full = lambda *shape: spec(shape, *([0] * len(shape)))
    anywhere = pl.BlockSpec(memory_space=pl.ANY)
    dense = ((tokens, width), bf16)
    piece = ((SUPER, LANES + width // SUPER // 2, LANES), bf16)
    outs = [dense, dense, dense, ((8, width), f32), ((8, ff), f32), piece, piece]
    out_specs = [full(*s) for s, _ in outs]
    out_specs[4] = spec((8, chunk), 0, step)
    return call(
        functools.partial(feed_bwd_kernel, layer=layer, parts=parts), "feed_backward", (ff // chunk,), ids,
        row_tiles(half, width, gathered)
        + [
            once(tokens, width), once(tokens, 128), anywhere, anywhere,
            full(*ln_scale.shape), spec((1, chunk, width), layer, step, 0), spec((tokens, chunk), 0, step),
            spec((1, width, chunk), layer, 0, step), anywhere,
            spec((tokens, chunk), 0, step), once(tokens, width), anywhere, anywhere,
        ],
        [grad, grad, grad, n2, r2, n1, r1, ln_scale, ffn_out, slope, ffn_in, w_out, act, mixed, ctx_own,
         ctx_shared],
        out_specs, [shape_of(s, d) for s, d in outs],
        [
            pltpu.VMEM((tokens, width), f32), pltpu.VMEM((tokens, width), f32),
            pltpu.VMEM((tokens, width), bf16), pltpu.VMEM((tokens, chunk), bf16),
            pltpu.VMEM((LANES, tokens), bf16), pltpu.VMEM((width, tokens), bf16),
            pltpu.VMEM((tokens, width), bf16), pltpu.VMEM((tokens, 128), f32),
            pltpu.VMEM((width, width), bf16), pltpu.VMEM(ctx_own.shape, bf16),
            pltpu.VMEM(ctx_shared.shape, bf16), pltpu.SemaphoreType.DMA((5,)),
        ],
    )


def joint_bwd_kernel(
    ids, x0, x1, x2, own_ref, shared_ref, arrived_ref, w_ref, attn_ref, rel0_ref, rel1_ref, vec_ref, pre_sum_ref,
    h_ref, keep_ref, send_ref, acc_ref, x_t, sums_ref, mine_ref,
    *, split,
):
    j = pl.program_id(0)
    width = x_t.shape[0]
    rows = width // SUPER
    half = rows // 2

    @pl.when(j == 0)
    def _():
        x_t[...] = jnp.concatenate([x0[0].T, x1[0].T, x2[0].T], 1)
        sums_ref[...] = jnp.zeros_like(sums_ref)

    far = arrived_ref[0].astype(f32) * (j > 0).astype(f32)
    near = (shared_ref[0].astype(f32) + far).astype(bf16)
    joint = jnp.concatenate([own_ref[0], near], 0)
    part = dot_nt(joint, w_ref[0])
    if split:
        mine_ref[...] = joint

    @pl.when(j == 0)
    def _():
        flag = (ids[1] == 0).astype(f32) if split else 1.0
        acc_ref[...] = part + attn_ref[...].astype(f32) * flag

    @pl.when(j > 0)
    def _():
        acc_ref[...] += part

    for side in range(2):
        lanes = slice(LANES * side, LANES * side + LANES)

        @pl.when(ids[1] == side)
        def _():
            if not split:
                mine_ref[...] = joint[:, lanes]
            sums_ref[j, :, lanes] = jnp.broadcast_to(col_sum(mine_ref[...].astype(f32)), (8, LANES))

    result = dot(x_t[...], mine_ref[...]).astype(bf16)
    for group in range(3):

        @pl.when(j == group)
        def _():
            for slab in range(SUPER):
                store_piece(ids, keep_ref, send_ref, slab, half, group * half,
                            result[rows * slab : rows * slab + rows])

    @pl.when(j == pl.num_programs(0) - 1)
    def _():
        h_ref[...] = acc_ref[...].astype(bf16)
        rel = (rel0_ref[...] + rel1_ref[...]).astype(bf16)
        count = rel.shape[0] // SUPER
        lines = jnp.concatenate([vec_ref[0:6, :], sums_ref[0, 0:1], sums_ref[2, 0:1]], 0)
        blank = jnp.zeros((8, LANES - rows), f32)
        for slab in range(SUPER):
            narrow = jnp.concatenate([lines[:, rows * slab : rows * slab + rows], blank], 1)
            wide = pre_sum_ref[0:1, LANES * slab : LANES * slab + LANES]
            small = jnp.concatenate([narrow, wide, jnp.zeros((count - 9, LANES), f32)], 0).astype(bf16)
            both = jnp.concatenate([rel[count * slab : count * slab + count], small], 0)
            store_piece(ids, keep_ref, send_ref, slab, count, 3 * half, both)


def joint_bwd(ids, x, gathered, own, shared, arrived, w_qkv, g_attn, rel0, rel1, vec, pre_sum, layer, split):
    _, length, cols = own.shape
    width = g_attn.shape[1]
    half = shared.shape[1]
    tokens = length + half
    full = lambda *shape: spec(shape, *([0] * len(shape)))
    side = lambda i, ids: 0 if split else ids[1]
    piece = (SUPER, (width // SUPER // 2) * 3 + rel0.shape[0] // SUPER, LANES)
    return call(
        functools.partial(joint_bwd_kernel, split=split), "projections_backward", (3,), ids,
        row_tiles(half, width, gathered)
        + [
            spec((1, length, cols), step, 0, 0), spec((1, half, cols), step, 0, 0),
            spec((1, half, cols), lambda i, ids: jnp.maximum(i - 1, 0), 0, 0),
            spec((1, width, cols), layer, 0, lambda i, ids: 2 * i + ids[1] if split else i),
            full(tokens, width), spec((rel0.shape[0], LANES), 0, side), spec((rel0.shape[0], LANES), 0, side),
            full(*vec.shape), full(*pre_sum.shape),
        ],
        [x, x, x, own, shared, arrived, w_qkv, g_attn, rel0, rel1, vec, pre_sum],
        [full(tokens, width), full(*piece), full(*piece)],
        [shape_of((tokens, width), bf16), shape_of(piece, bf16), shape_of(piece, bf16)],
        [
            pltpu.VMEM((tokens, width), f32), pltpu.VMEM((width, tokens), bf16),
            pltpu.VMEM((3, 8, width), f32), pltpu.VMEM((tokens, LANES), bf16),
        ],
    )


def place_rows_kernel(ids, own_ref, other_ref, out_ref):
    i = pl.program_id(0)
    core = ids[0]
    row = i // 2
    mine = jnp.where(row == 2, (i - 4) == core, row == core)

    @pl.when(mine)
    def _():
        out_ref[0] = own_ref[0].astype(out_ref.dtype)

    @pl.when(jnp.logical_not(mine))
    def _():
        out_ref[0] = other_ref[0].astype(out_ref.dtype)


def place_rows(ids, own, other, dtype):
    tokens, width = own.shape
    half = tokens // 3
    tile = lambda i, ids: jnp.where(i < 4, i % 2, 2)
    tiles = lambda x: x.reshape(3, half, width)
    return call(
        place_rows_kernel, "place_rows", (6,), ids,
        [spec((1, half, width), tile, 0, 0)] * 2, [tiles(own), tiles(other)],
        spec((1, half, width), step, 0, 0), shape_of((6, half, width), dtype),
    )


def collect(ids, refs, scratch):
    for core in range(2):
        for side in range(2):

            @pl.when((ids[0] == core) & (ids[1] == side))
            def _():
                scratch[core, side] = refs[0][...]
                scratch[core, 1 - side] = refs[1][...]
                scratch[1 - core, side] = refs[2][...]
                scratch[1 - core, 1 - side] = refs[3][...]


def spread_columns(scratch, out_ref, layer, at, groups, rows, inner=False):
    for core in range(2):
        for side in range(2):
            for g in range(groups):
                piece = scratch[core, side, at + g * rows : at + g * rows + rows, :]
                lane = ((g * 2 + side) if inner else (side * groups + g)) * LANES
                out_ref[layer, core * rows : core * rows + rows, lane : lane + LANES] = piece.astype(f32)


def unpack_feed_kernel(ids, *refs):
    inputs, (in_ref, out_ref, w_out_ref, scratch) = refs[:8], refs[8:]
    high = LANES // 2
    for layer in range(2):
        collect(ids, inputs[4 * layer : 4 * layer + 4], scratch)
        columns = [scratch[core, side, 0:high, :] for side in range(2) for core in range(2)]
        out_ref[layer] = jnp.concatenate(columns, 0).astype(f32).T
        rows = in_ref.shape[1] // 2
        spread_columns(scratch, in_ref, layer, high, 4, rows)
        spread_columns(scratch, w_out_ref, layer, high + 4 * rows, 1, rows)


def unpack_attention_kernel(ids, *refs):
    inputs = refs[:8]
    qkv_ref, rel_ref, qv_ref, out_bias_ref, scale_ref, shift_ref, in_bias_ref, ffn_bias_ref = refs[8:16]
    scratch = refs[16]
    rows = qkv_ref.shape[1] // 2
    wide = 2 * rows
    for layer in range(2):
        collect(ids, inputs[4 * layer : 4 * layer + 4], scratch)
        spread_columns(scratch, qkv_ref, layer, 0, 3, rows, True)
        at = 3 * rows
        count = rel_ref.shape[2]
        rel = jnp.concatenate([scratch[0, side, at : at + count, :] for side in range(2)], 1).astype(f32)
        size = rel_ref.shape[3]
        for head in range(rel_ref.shape[1]):
            rel_ref[layer, head] = rel[:, size * head : size * head + size]
        small = scratch[1, 0, at : at + count, :].astype(f32)
        scale_ref[layer] = small[0:2, 0:wide]
        shift_ref[layer] = small[2:4, 0:wide]
        out_bias_ref[layer : layer + 1] = small[4:5, 0:wide]
        ffn_bias_ref[layer : layer + 1] = small[5:6, 0:wide]
        other = scratch[1, 1, at : at + count, :].astype(f32)
        qv_ref[layer] = small[6:8, 0:wide] + other[6:8, 0:wide]
        in_bias_ref[layer : layer + 1] = small[8:9]


def unpack(kernel, name, ids, pieces, shapes):
    full = lambda *shape: spec(shape, *([0] * len(shape)))
    return call(
        kernel, name, (1,), ids, [full(*p.shape) for p in pieces], pieces,
        [full(*s) for s in shapes], [shape_of(s, f32) for s in shapes],
        [pltpu.VMEM((2, 2) + pieces[0].shape, bf16)],
    )


def body(
    stream, cotangent, segments, word_boxes, valid_mask, w_qkv, qv_bias, w_out, out_bias, rel_proj,
    ln_scale, ln_shift, ffn_in, ffn_in_bias, ffn_out, ffn_out_bias,
):
    sections = lax.axis_size("section")
    dp = lax.axis_size("dp")
    section = lax.axis_index("section")
    dp_index = lax.axis_index("dp")
    core, side = section % 2, section // 2
    rows, length, width = stream.shape
    layers = w_qkv.shape[0]
    ff = ffn_in.shape[2]
    half = length // 2
    assert rows == 3 and sections == 4 and layers == 2 and dp % SUPER == 0 and width == 2 * LANES
    fine = dp // SUPER
    ids = jnp.stack([core, side, dp_index // fine]).astype(jnp.int32)
    weights = (w_out, out_bias, ln_scale, ln_shift, ffn_in, ffn_in_bias, ffn_out, ffn_out_bias)
    rel_pairs = rel_proj.reshape(layers, width // 128, 128, 128)

    def flip(x, bit):
        return lax.ppermute(x, "section", [(i, i ^ bit) for i in range(sections)])

    def flip_dp(x, bit):
        return lax.ppermute(x, "dp", [(i, i ^ bit) for i in range(dp)])

    tables = make_tables(ids, jnp.swapaxes(word_boxes, 0, 1), segments, valid_mask)
    ctab, stab, valid_col = tables[3], tables[4], tables[7]

    halves = lambda x: x.reshape(-1, half, width)
    x, gathered = halves(stream), True
    kept = []
    for l in range(layers):
        joint, turned, kv = project(ids, x, gathered, w_qkv, qv_bias, rel_pairs, ctab, stab, l)
        kv_far = flip(kv, 1)
        ctx_own, lse_own = attention_fwd(ids, False, tables, joint, turned, None)
        ctx_shared, lse_shared = attention_fwd(ids, True, tables, joint, turned, kv_far)
        n1, r1, n2, r2, mixed, act, slope, out, squares = feed_fwd(
            ids, x, gathered, ctx_own, ctx_shared, valid_col, weights, l
        )
        kept.append(
            dict(x=x, gathered=gathered, joint=joint, turned=turned, kv_far=kv_far, ctx_own=ctx_own,
                 ctx_shared=ctx_shared, lse_own=lse_own, lse_shared=lse_shared, norms=(n1, r1, n2, r2),
                 mixed=mixed, act=act, slope=slope, out=out, squares=squares)
        )
        x, gathered = halves(out), False

    clock = [ids]

    def pin(state):
        clock[0], state = lax.optimization_barrier((clock[0], state))
        return state

    def absorb(keep, arrived):
        keep, arrived = pin((keep, arrived))
        n = keep.shape[0] // 2
        return pin((keep[:n] + arrived[:n], keep[n:] + arrived[n:]))

    def last(keep, arrived):
        keep, arrived = pin((keep, arrived))
        x = (keep + arrived)[0]
        bit = 1
        while bit < fine:
            x = x + flip_dp(x, bit)
            bit *= 2
        return pin(x)

    def hop(state, bit):
        return state[0], flip_dp(state[1], fine << bit)

    def all_sides(x):
        far = flip(x, 2)
        return [x, far, flip(x, 1), flip(far, 1)]

    def feed_back(l, grad, gathered):
        k = kept[l]
        g_mixed, g_attn, g_ctx, vec, pre_sum, keep, send = feed_bwd(
            clock[0], grad, gathered, k["norms"], k["slope"], k["act"], k["mixed"], k["ctx_own"],
            k["ctx_shared"], weights, l,
        )
        k["g_mixed"] = g_mixed
        return g_attn, g_ctx, vec, pre_sum, (keep, flip(send, 1))

    def attention_back(l, shared, g_ctx):
        k = kept[l]
        return attention_bwd(
            clock[0], shared, tables, k["joint"], k["turned"], k["kv_far"] if shared else None,
            k["lse_shared" if shared else "lse_own"], g_ctx, rel_pairs, l, l == 0,
        )

    def joint_back(l, own_grads, shared_keep, arrived, g_attn, rel_own, rel_shared, vec, pre_sum):
        k = kept[l]
        g_h, keep, send = joint_bwd(
            clock[0], k["x"], k["gathered"], own_grads, shared_keep, arrived, w_qkv, g_attn, rel_own,
            rel_shared, vec, pre_sum, l, l == 0,
        )
        k["g_h"] = g_h
        return g_h, (keep, flip(send, 1))

    g_attn, g_ctx, vec, pre_sum, f1 = feed_back(1, halves(cotangent), True)
    shared_keep, shared_send, rel_shared = attention_back(1, True, g_ctx)
    arrived = flip(shared_send, 1)
    f1 = hop(absorb(*f1), 0)
    own_grads, rel_own = attention_back(1, False, g_ctx)
    g_h, a1 = joint_back(1, own_grads, shared_keep, arrived, g_attn, rel_own, rel_shared, vec, pre_sum)

    f1 = hop(absorb(*f1), 1)
    a1 = hop(absorb(*a1), 0)
    g_attn, g_ctx, vec, pre_sum, f0 = feed_back(0, halves(g_h), False)
    f1 = hop(absorb(*f1), 2)
    a1 = hop(absorb(*a1), 1)
    shared_keep, shared_send, rel_shared = attention_back(0, True, g_ctx)
    arrived = flip(shared_send, 1)
    f0 = hop(absorb(*f0), 0)
    own_grads, rel_own = attention_back(0, False, g_ctx)
    f1 = last(*f1)
    a1 = hop(absorb(*a1), 2)
    g_h, a0 = joint_back(0, own_grads, shared_keep, arrived, g_attn, rel_own, rel_shared, vec, pre_sum)
    g_h_far = flip(g_h, 2)
    f1 = all_sides(f1)
    f0 = hop(absorb(*f0), 1)
    a0 = hop(absorb(*a0), 0)
    a1 = all_sides(last(*a1))

    def of_layer(name):
        return jnp.where(side == 0, kept[0][name], kept[1][name])

    def to_section(first, second, dtype):
        a, b = of_layer(first), of_layer(second)
        own, away = jnp.where(core == 0, a, b), jnp.where(core == 0, b, a)
        return place_rows(ids, own, flip(away, 1), dtype).reshape(1, rows, length, width)

    section_outs = pin(to_section("mixed", "out", bf16))
    a0 = hop(absorb(*a0), 1)
    f0 = hop(absorb(*f0), 2)
    kept[0]["g_h"] = pin(g_h + g_h_far)
    in_grads = pin(to_section("g_h", "g_mixed", f32))
    a0 = hop(absorb(*a0), 2)
    f0 = all_sides(last(*f0))
    a0 = all_sides(last(*a0))

    squares_mine = jnp.sum(of_layer("squares"), 1).reshape(2, 2, 2)
    squares_far = flip(squares_mine, 1)
    sub = lambda v: lax.dynamic_index_in_dim(v, core, 0, keepdims=False)
    near, far = sub(squares_mine), sub(squares_far)
    first = jnp.where(core == 0, near[:, 0], far[:, 0])
    second = jnp.where(core == 0, far[:, 0], near[:, 0])
    square_rows = jnp.stack([first, second, near[:, 1] + far[:, 1]])
    row_counts = jnp.sum(valid_mask.astype(f32), 1)
    root_mean_squares = jnp.sqrt(square_rows / (width * jnp.maximum(row_counts, 1.0))[:, None])[None]

    slab = width // SUPER
    d_ffn_in, d_ffn_out, d_out = unpack(
        unpack_feed_kernel, "unpack_feed", clock[0], f0 + f1,
        [(2, slab, ff), (2, ff // SUPER, width), (2, slab, width)],
    )
    d_ffn_in, d_ffn_out, d_out = pin((d_ffn_in, d_ffn_out, d_out))
    rel_rows = 128 // SUPER
    d_qkv, d_rel, d_qv, d_out_bias, d_scale, d_shift, d_in_bias, d_ffn_bias = unpack(
        unpack_attention_kernel, "unpack_attention", clock[0], a0 + a1,
        [(2, slab, 3 * width), (2, rel_proj.shape[1], rel_rows, rel_proj.shape[2]), (2, 2, slab), (2, slab),
         (2, 2, slab), (2, 2, slab), (2, LANES), (2, slab)],
    )

    def own_part(x, axis):
        n = x.shape[axis] // fine
        return x if fine == 1 else lax.dynamic_slice_in_dim(x, (dp_index % fine) * n, n, axis)

    return (
        section_outs,
        in_grads,
        own_part(d_qkv, 1),
        own_part(d_qv, 2),
        own_part(d_out, 1),
        own_part(d_out_bias, 1),
        own_part(jnp.swapaxes(d_rel, 2, 3), 3),
        own_part(d_scale, 2),
        own_part(d_shift, 2),
        own_part(d_ffn_in, 1),
        own_part(d_in_bias, 1),
        own_part(d_ffn_out, 1),
        own_part(d_ffn_bias, 1),
        root_mean_squares,
    )


def solution(mesh):
    return jax.shard_map(
        body,
        mesh=mesh,
        in_specs=(
            P("dp", None, None),
            P("dp", None, None),
            P("dp", None),
            P(None, "dp", None),
            P("dp", None),
        )
        + (P(),) * 11,
        out_specs=(
            P("section", "dp", None, None),
            P("section", "dp", None, None),
            P(None, "dp", None),
            P(None, None, "dp"),
            P(None, "dp", None),
            P(None, "dp"),
            P(None, None, None, "dp"),
            P(None, None, "dp"),
            P(None, None, "dp"),
            P(None, "dp", None),
            P(None, "dp"),
            P(None, "dp", None),
            P(None, "dp"),
            P("section", "dp", None),
        ),
        check_vma=False,
    )
```

```python
import functools

import jax
import jax.numpy as jnp
from jax import lax
from jax.experimental import pallas as pl
from jax.experimental.pallas import tpu as pltpu
from jax.sharding import PartitionSpec as P

ln_eps = 1e-05
masked_score = -1e30
bf16 = jnp.bfloat16
f32 = jnp.float32
MB = 1 << 20
SUPER = 8
LANES = 384
NORM_ROWS = 64

ERF_COEFS = (
    0.7978849414899046, 0.0363330844086688, -3.259474462099993e-05, -5.5306316685416947e-05,
    3.964773125473232e-06, -1.322662757755248e-07, 1.7562773256476674e-09,
)


def dot(a, b):
    return lax.dot_general(a, b, (((1,), (0,)), ((), ())), preferred_element_type=f32)


def dot_nt(a, b):
    return lax.dot_general(a, b, (((1,), (1,)), ((), ())), preferred_element_type=f32)


def gelu_and_slope(x):
    square = x * x
    g = ERF_COEFS[-1]
    for c in ERF_COEFS[-2::-1]:
        g = g * square + c
    phi = 0.5 * jnp.tanh(x * g) + 0.5
    density = jnp.exp2(square * (-0.5 * 1.4426950408889634)) * 0.3989422804014327
    return x * phi, phi + x * density


def norm_parts(residual):
    average = jnp.mean(residual, -1, keepdims=True)
    centered = residual - average
    inverse = lax.rsqrt(jnp.mean(centered * centered, -1, keepdims=True) + ln_eps)
    return centered * inverse, inverse


def norm_back(gradient, gain, normed, inverse):
    dnormed = gradient * gain
    return inverse * (
        dnormed
        - jnp.mean(dnormed, -1, keepdims=True)
        - normed * jnp.mean(dnormed * normed, -1, keepdims=True)
    )


def row_loop(count, chunk, sums):
    for i in range(count):
        sums = chunk(i, sums)
    return sums


def fold(x):
    return jnp.sum(x.reshape(-1, 8, x.shape[1]), 0)


def col_sum(x):
    return jnp.sum(x, 0, keepdims=True)


COST_US = dict(
    tables=4, projections=8, attention_forward=7, feed_forward=24, feed_backward=30, attention_backward=12,
    projections_backward=3, place_rows=4,
    unpack_feed=4, unpack_attention=3,
)


def call(kernel, name, grid, ids, in_specs, inputs, out_specs, out_shape, scratch=(), micros=None):
    micros = COST_US[name] if micros is None else micros
    cost = pl.CostEstimate(flops=micros * 1100000000, bytes_accessed=micros * 1000000, transcendentals=0)
    return pl.pallas_call(
        kernel,
        grid_spec=pltpu.PrefetchScalarGridSpec(
            num_scalar_prefetch=1,
            grid=grid,
            in_specs=in_specs,
            out_specs=out_specs,
            scratch_shapes=list(scratch),
        ),
        out_shape=out_shape,
        compiler_params=pltpu.CompilerParams(vmem_limit_bytes=62 * MB),
        cost_estimate=cost,
        name=name,
    )(ids, *inputs)


def spec(shape, *index):
    def index_map(i, ids):
        return tuple(x(i, ids) if callable(x) else x for x in index)

    return pl.BlockSpec(shape, index_map)


def shape_of(shape, dtype):
    return jax.ShapeDtypeStruct(shape, dtype)


step = lambda i, ids: i


def row_tiles(half, width, gathered):
    if not gathered:
        return [spec((1, half, width), t, 0, 0) for t in range(3)]
    core = lambda ids: ids[0]
    return [
        spec((1, half, width), lambda i, ids: 2 * core(ids), 0, 0),
        spec((1, half, width), lambda i, ids: 2 * core(ids) + 1, 0, 0),
        spec((1, half, width), lambda i, ids: 4 + core(ids), 0, 0),
    ]


def tables_kernel(
    ids, boxes_ref, seg_ref, valid_ref,
    cos_ref, sin_ref, kf_ref, ctab_ref, stab_ref, code_ref, segrow_ref, valid_col_ref,
):
    core = ids[0]
    length = seg_ref.shape[1]
    half = length // 2

    def ordered(read):
        near = pl.multiple_of(core * half, half)
        far = pl.multiple_of((1 - core) * half, half)
        return jnp.concatenate(
            [read(pl.ds(core, 1), slice(None)), read(2, pl.ds(near, half)), read(2, pl.ds(far, half))], 1
        )

    def row_of(ref):
        def read(r, c):
            r = pl.ds(2, 1) if isinstance(r, int) else r
            return ref[r, c]
        return ordered(read)

    count = length * 2
    at = lax.broadcasted_iota(jnp.int32, (1, count), 1)
    shared = jnp.where(
        at < length + half, at - length + core * half, at - length - half + (1 - core) * half
    )
    position = jnp.where(at < length, at, shared).astype(f32)
    rate_at = lax.broadcasted_iota(jnp.int32, (32, 1), 0).astype(f32)
    text = position * jnp.exp(rate_at * (-9.210340371976184 / 32))
    box_rate = jnp.exp2(-lax.broadcasted_iota(jnp.int32, (8, 1), 0).astype(f32))
    angles = [text]
    for c in range(4):
        coords = row_of(boxes_ref.at[:, c]).astype(f32)
        angles.append(coords * box_rate)
    angles = jnp.concatenate(angles, 0)
    cosines, sines = jnp.cos(angles), jnp.sin(angles)
    cos_ref[...], sin_ref[...] = cosines, sines
    kf_ref[...] = jnp.concatenate([cosines, sines], 0).T.astype(bf16)
    ctab_ref[...] = jnp.concatenate([cosines, -cosines], 0).T
    stab_ref[...] = jnp.concatenate([sines, sines], 0).T
    seg = row_of(seg_ref).astype(f32)
    valid = row_of(valid_ref).astype(f32)
    segrow_ref[...] = jnp.broadcast_to(seg, segrow_ref.shape)
    code_ref[...] = jnp.broadcast_to(jnp.where(valid > 0, seg, -1.0), (128, count)).T
    valid_col_ref[...] = jnp.broadcast_to(valid, (128, count)).T


def make_tables(ids, word_boxes, segments, valid_mask):
    length = segments.shape[1]
    count = 2 * length
    full = lambda *shape: spec(shape, *([0] * len(shape)))
    outs = [
        ((64, count), f32), ((64, count), f32), ((count, 128), bf16), ((count, 128), f32),
        ((count, 128), f32), ((count, 128), f32), ((8, count), f32), ((count, 128), f32),
    ]
    return call(
        tables_kernel, "tables", (1,), ids,
        [full(*word_boxes.shape), full(*segments.shape), full(*valid_mask.shape)],
        [word_boxes, segments, valid_mask],
        [full(*s) for s, _ in outs], [shape_of(s, d) for s, d in outs],
    )


def qkv_kernel(
    ids, x0, x1, x2, w_ref, bias_ref, rel_ref, ctab_ref, stab_ref, joint_ref, turned_ref, kv_ref, x_ref,
    *, layer,
):
    j = pl.program_id(0)
    half = x0.shape[1]

    @pl.when(j == 0)
    def _():
        x_ref[0:half], x_ref[half : 2 * half], x_ref[2 * half :] = x0[0], x1[0], x2[0]

    flags = [(j == 0).astype(f32), (j == 2).astype(f32)]
    bias = bias_ref[layer, 0:1, :].astype(f32) * flags[0] + bias_ref[layer, 1:2, :].astype(f32) * flags[1]
    joint = (dot(x_ref[...], w_ref[0]) + bias).astype(bf16)
    joint_ref[...] = joint
    kv_ref[...] = joint[2 * half :]

    @pl.when(j == 0)
    def _():
        ctab, stab = ctab_ref[...], stab_ref[...]
        row = lax.broadcasted_iota(jnp.int32, (128, 128), 0)
        for p in range(rel_ref.shape[1]):
            rel = rel_ref[0, p]
            zero = jnp.zeros_like(rel)
            block = jnp.concatenate([jnp.where(row < 64, rel, zero), jnp.where(row < 64, zero, rel)], 1)
            coef = dot(joint[:, 128 * p : 128 * p + 128], block)
            for e in range(2):
                c = coef[:, 128 * e : 128 * e + 128]
                at = 256 * p + 128 * e
                turned_ref[:, at : at + 128] = (c * ctab + pltpu.roll(c, 64, 1) * stab).astype(bf16)


def project(ids, x, gathered, w_qkv, qv_bias, rel_pairs, ctab, stab, layer):
    half, width = x.shape[1], x.shape[2]
    tokens = 3 * half
    pairs = rel_pairs.shape[1]
    return call(
        functools.partial(qkv_kernel, layer=layer), "projections", (3,), ids,
        row_tiles(half, width, gathered)
        + [
            spec((1, width, width), layer, 0, step), spec(qv_bias.shape, 0, 0, 0),
            spec((1, pairs, 128, 128), layer, 0, 0, 0), spec((tokens, 128), 0, 0),
            spec((tokens, 128), 0, 0),
        ],
        [x, x, x, w_qkv, qv_bias, rel_pairs, ctab, stab],
        [
            spec((tokens, width), 0, step), spec((tokens, 2 * width), 0, 0),
            spec((half, width), 0, lambda i, ids: jnp.maximum(i - 1, 0)),
        ],
        [
            shape_of((tokens, 3 * width), bf16), shape_of((tokens, 2 * width), bf16),
            shape_of((half, 2 * width), bf16),
        ],
        [pltpu.VMEM((tokens, width), bf16)],
    )


def lane_half(shape, half):
    lane = lax.broadcasted_iota(jnp.int32, shape, 1)
    return (lane < 64) if half == 0 else (lane >= 64)


def only_half(x, half):
    return jnp.where(lane_half(x.shape, half), x, jnp.zeros_like(x))


def fill_bias(code_ref, seg_ref, bias_ref):
    shape = bias_ref.shape
    code = jnp.concatenate([code_ref[...]] * (shape[1] // 128), 1)
    same = code == seg_ref[0:1, :]
    key_at = lax.broadcasted_iota(jnp.int32, shape, 0)
    query_at = lax.broadcasted_iota(jnp.int32, shape, 1)
    bias_ref[...] = jnp.where(same | (key_at == query_at), 0.0, masked_score)


def attention_fwd_kernel(
    ids, code_ref, seg_ref, kf_ref, q_ref, turned_ref, k_ref, v_ref, *rest, per_step, shared,
):
    if shared:
        k_far, v_far, ctx_ref, lse_ref, bias_ref, k_all, v_all = rest
        half = k_ref.shape[0]
        k_all[0:half], k_all[half:] = k_ref[...], k_far[...]
        v_all[0:half], v_all[half:] = v_ref[...], v_far[...]
        k_ref, v_ref = k_all, v_all
    else:
        ctx_ref, lse_ref, bias_ref = rest

    @pl.when(pl.program_id(0) == 0)
    def _():
        fill_bias(code_ref, seg_ref, bias_ref)

    scale = jnp.asarray(0.125, bf16)
    units = [(pair, e) for pair in range(per_step) for e in range(2)]
    values_t = {}

    def scores_of(unit):
        pair, e = unit
        at = slice(128 * pair, 128 * pair + 128)
        turned = turned_ref[:, 256 * pair + 128 * e : 256 * pair + 128 * e + 128]
        qside = jnp.concatenate([turned, only_half(q_ref[:, at], e)], 1) * scale
        kside = jnp.concatenate([kf_ref[...], k_ref[:, at]], 1)
        return dot_nt(kside, qside) + bias_ref[...]

    def finish(unit, scores):
        pair, e = unit
        top = jnp.max(scores, 0, keepdims=True)
        expo = jnp.exp(scores - top)
        total = jnp.sum(expo, 0, keepdims=True)
        if pair not in values_t:
            values_t[pair] = v_ref[:, 128 * pair : 128 * pair + 128].T
        ctx = dot(values_t[pair][64 * e : 64 * e + 64], expo.astype(bf16))
        at = 128 * pair + 64 * e
        ctx_ref[at : at + 64, :] = (ctx * (1.0 / total)).astype(bf16)
        lse_ref[pair, e : e + 1, :] = top + jnp.log(total)

    scores = scores_of(units[0])
    for i, unit in enumerate(units):
        upcoming = scores_of(units[i + 1]) if i + 1 < len(units) else None
        finish(unit, scores)
        scores = upcoming


def attention_fwd(ids, shared, tables, joint, turned, kv_far, per_step=2):
    cos_t, sin_t, kf, ctab, stab, code, seg, valid = tables
    tokens, width = joint.shape[0], joint.shape[1] // 3
    half = tokens // 3
    nk = 2 * half
    nq = half if shared else nk
    key_rows = half if shared else nk
    lanes = 128 * per_step
    steps = width // lanes
    q_row = 2 if shared else 0
    at = lambda off: (lambda i, ids: i + off)
    in_specs = [
        spec((nk, 128), int(shared), 0), spec((8, nq), 0, q_row), spec((nk, 128), int(shared), 0),
        spec((nq, lanes), q_row, step), spec((nq, 2 * lanes), q_row, step),
        spec((key_rows, lanes), q_row, at(steps)), spec((key_rows, lanes), q_row, at(2 * steps)),
    ]
    inputs = [code, seg, kf, joint, turned, joint, joint]
    scratch = [pltpu.VMEM((nk, nq), f32)]
    if shared:
        in_specs += [spec((half, lanes), 0, step), spec((half, lanes), 0, at(steps))]
        inputs += [kv_far, kv_far]
        scratch += [pltpu.VMEM((nk, lanes), bf16)] * 2
    return call(
        functools.partial(attention_fwd_kernel, per_step=per_step, shared=shared),
        "attention_forward", (steps,), ids, in_specs, inputs,
        [spec((lanes, nq), step, 0), spec((per_step, 2, nq), step, 0, 0)],
        [shape_of((width, nq), bf16), shape_of((width // 128, 2, nq), f32)],
        scratch,
    )


def attention_bwd_kernel(
    ids, code_ref, seg_ref, kf_ref, cos_ref, sin_ref, rel_ref, lse_ref, gc_ref, q_ref, turned_ref,
    k_ref, v_ref, *rest, per_step, shared,
):
    if shared:
        k_far, v_far, keep_ref, send_ref, drel_ref, bias_ref, kft_ref, k_all, v_all = rest
        half = k_ref.shape[0]
        k_all[0:half], k_all[half:] = k_ref[...], k_far[...]
        v_all[0:half], v_all[half:] = v_ref[...], v_far[...]
        k_ref, v_ref = k_all, v_all
    else:
        keep_ref, drel_ref, bias_ref, kft_ref = rest

    @pl.when(pl.program_id(0) == 0)
    def _():
        fill_bias(code_ref, seg_ref, bias_ref)
        kft_ref[...] = kf_ref[...].T

    scale = jnp.asarray(0.125, bf16)
    cosines, sines = cos_ref[...], sin_ref[...]
    units = [(pair, e) for pair in range(per_step) for e in range(2)]
    store = {}

    def scores_of(unit):
        pair, e = unit
        at = slice(128 * pair, 128 * pair + 128)
        q_mine = only_half(q_ref[:, at], e)
        gc_mine = only_half(gc_ref[:, at], e)
        q_scaled = q_mine * scale
        turned = turned_ref[:, 256 * pair + 128 * e : 256 * pair + 128 * e + 128]
        qside = jnp.concatenate([turned * scale, q_scaled], 1)
        kside = jnp.concatenate([kf_ref[...], k_ref[:, at]], 1)
        scores = dot_nt(kside, qside) + bias_ref[...]
        gp = dot_nt(v_ref[:, at], gc_mine)
        return scores, gp, q_mine, gc_mine, q_scaled

    def finish(unit, parts):
        pair, e = unit
        scores, gp, q_mine, gc_mine, q_scaled = parts
        at = slice(128 * pair, 128 * pair + 128)
        shares = jnp.exp(scores - lse_ref[pair, e : e + 1, :])
        dv = dot(shares.astype(bf16), gc_mine)
        weighted = shares * gp
        delta = jnp.sum(weighted, 0, keepdims=True)
        gs = (weighted - shares * delta).astype(bf16)
        dk = dot(gs, q_scaled)
        if pair not in store:
            store[pair] = k_ref[:, at].T
        side_t = jnp.concatenate([kft_ref[...], store[pair][64 * e : 64 * e + 64]], 0)
        dside = dot(side_t, gs) * 0.125
        g_cos, g_sin = dside[0:64], dside[64:128]
        gcoef = jnp.concatenate(
            [g_cos * cosines + g_sin * sines, g_cos * sines - g_sin * cosines], 0
        ).astype(bf16)
        dq = dside[128:192] + dot(rel_ref[0, pair, 64 * e : 64 * e + 64], gcoef)
        drel = dot(gcoef, q_mine)
        if e == 0:
            store["even"] = (dq, dk, dv, drel)
            return
        dq0, dk0, dv0, drel0 = store["even"]
        dq = jnp.concatenate([dq0, dq], 0).T.astype(bf16)
        dk, dv = (dk0 + dk).astype(bf16), (dv0 + dv).astype(bf16)
        drel_ref[:, at] = drel0 + drel
        n = keep_ref.shape[1]
        keep_ref[0, :, at] = dq
        keep_ref[1, :, at], keep_ref[2, :, at] = dk[0:n], dv[0:n]
        if shared:
            send_ref[0, :, at], send_ref[1, :, at] = dk[n:], dv[n:]

    parts = scores_of(units[0])
    for i, unit in enumerate(units):
        upcoming = scores_of(units[i + 1]) if i + 1 < len(units) else None
        finish(unit, parts)
        parts = upcoming


def attention_bwd(ids, shared, tables, joint, turned, kv_far, lse, g_ctx, rel_pairs, layer, split, per_step=3):
    per_step = 3 if split else per_step
    cos_t, sin_t, kf, ctab, stab, code, seg, valid = tables
    tokens, width = joint.shape[0], joint.shape[1] // 3
    half = tokens // 3
    nk = 2 * half
    nq = half if shared else nk
    key_rows = half if shared else nk
    lanes = 128 * per_step
    all_steps = width // lanes
    steps = all_steps // 2 if split else all_steps
    out_width = lanes * steps
    first = lambda ids: ids[1] * steps if split else 0
    q_row = 2 if shared else 0
    at = lambda off: (lambda i, ids: first(ids) + i + off)
    here = at(0)
    in_specs = [
        spec((nk, 128), int(shared), 0), spec((8, nq), 0, q_row), spec((nk, 128), int(shared), 0),
        spec((64, nq), 0, q_row), spec((64, nq), 0, q_row),
        spec((1, per_step, 128, 128), layer, here, 0, 0),
        spec((per_step, 2, nq), here, 0, 0), spec((nq, lanes), q_row, here),
        spec((nq, lanes), q_row, here), spec((nq, 2 * lanes), q_row, here),
        spec((key_rows, lanes), q_row, at(all_steps)), spec((key_rows, lanes), q_row, at(2 * all_steps)),
    ]
    inputs = [code, seg, kf, cos_t, sin_t, rel_pairs, lse, g_ctx, joint, turned, joint, joint]
    scratch = [pltpu.VMEM((nk, nq), f32), pltpu.VMEM((128, nk), bf16)]
    out_specs = [spec((3, key_rows, lanes), 0, 0, step)]
    out_shape = [shape_of((3, key_rows, out_width), bf16)]
    if shared:
        in_specs += [spec((half, lanes), 0, here), spec((half, lanes), 0, at(all_steps))]
        inputs += [kv_far, kv_far]
        scratch += [pltpu.VMEM((nk, lanes), bf16)] * 2
        out_specs.append(spec((2, half, lanes), 0, 0, step))
        out_shape.append(shape_of((2, half, out_width), bf16))
    out_specs.append(spec((128, lanes), 0, step))
    out_shape.append(shape_of((128, out_width), f32))
    return call(
        functools.partial(attention_bwd_kernel, per_step=per_step, shared=shared),
        "attention_backward", (steps,), ids, in_specs, inputs, out_specs, out_shape, scratch,
        40 if shared else 12,
    )


def feed_fwd_kernel(
    ids, x0, x1, x2, own_ref, shared_ref, valid_ref, w_out_ref, out_bias_ref, scale_ref, shift_ref,
    in_ref, in_bias_ref, out_ref, ffn_bias_ref,
    n1_out, r1_out, n2_ref, r2_ref, mixed_out, act_ref, slope_ref, h_ref, squares_ref,
    feed_ref, n1_ref, r1_ref, mixed_ref, sems,
    *, layer, parts,
):
    j = pl.program_id(0)
    pairs = ((n1_ref, n1_out), (r1_ref, r1_out), (mixed_ref, mixed_out))
    copies = [pltpu.make_async_copy(a, b, sems.at[k]) for k, (a, b) in enumerate(pairs)]
    half = x0.shape[1]
    row = lambda ref, *at: ref[at[:-1] + (slice(at[-1], at[-1] + 1),)].astype(f32)

    rows = NORM_ROWS
    zero = jnp.zeros((8, x0.shape[2]), f32)

    def add_squares(sums, k, tile):
        for i, x in enumerate(sums):
            at = k + 2 * i + tile // 2
            squares_ref[at : at + 1, :] += col_sum(x)

    @pl.when(j == 0)
    def _():
        ctx = jnp.concatenate([own_ref[...].T, shared_ref[...].T], 0)
        feed_ref[...] = dot(ctx, w_out_ref[0])
        bias, gain, shift = row(out_bias_ref, layer), row(scale_ref, layer, 0), row(shift_ref, layer, 0)
        squares_ref[...] = jnp.zeros_like(squares_ref)
        for t, x_ref in enumerate((x0, x1, x2)):

            def chunk(i, sums):
                at = i * rows
                to = pl.ds(t * half + at, rows)
                valid = valid_ref[to, 0:1]
                attention = feed_ref[to, :] + bias
                normed, inverse = norm_parts(x_ref[0, pl.ds(at, rows), :].astype(f32) + attention)
                mixed = (normed * gain + shift).astype(bf16)
                n1_ref[to, :] = normed.astype(bf16)
                r1_ref[to, :] = jnp.broadcast_to(inverse, (rows, 128))
                mixed_ref[to, :] = mixed
                mixed = mixed.astype(f32)
                return (sums[0] + fold(attention * attention * valid), sums[1] + fold(mixed * mixed * valid))

            sums = row_loop(half // rows, chunk, (zero, zero))
            add_squares(sums, 0, t)
        for copy in copies:
            copy.start()

    cols = in_ref.shape[2] // parts
    at = lambda k: slice(cols * k, cols * k + cols)
    bias = in_bias_ref[layer : layer + 1, :].astype(f32)
    pre = dot(mixed_ref[...], in_ref[0, :, at(0)]) + bias[:, at(0)]
    feed = None
    for k in range(parts):
        coming = None
        if k + 1 < parts:
            coming = dot(mixed_ref[...], in_ref[0, :, at(k + 1)]) + bias[:, at(k + 1)]
        act, slope = gelu_and_slope(pre)
        act = act.astype(bf16)
        act_ref[:, at(k)] = act
        slope_ref[:, at(k)] = slope.astype(bf16)
        part = dot(act, out_ref[0, at(k)])
        feed = part if feed is None else feed + part
        pre = coming

    @pl.when(j == 0)
    def _():
        feed_ref[...] = feed

    @pl.when(j > 0)
    def _():
        feed_ref[...] += feed

    @pl.when(j == pl.num_programs(0) - 1)
    def _():
        bias, gain, shift = row(ffn_bias_ref, layer), row(scale_ref, layer, 1), row(shift_ref, layer, 1)
        for t in range(3):

            def chunk(i, sums):
                to = pl.ds(t * half + i * rows, rows)
                valid = valid_ref[to, 0:1]
                branch = feed_ref[to, :] + bias
                normed, inverse = norm_parts(mixed_ref[to, :].astype(f32) + branch)
                out = normed * gain + shift
                n2_ref[to, :] = normed.astype(bf16)
                r2_ref[to, :] = jnp.broadcast_to(inverse, (rows, 128))
                h_ref[to, :] = out.astype(bf16)
                return (sums[0] + fold(branch * branch * valid), sums[1] + fold(out * out * valid))

            sums = row_loop(half // rows, chunk, (zero, zero))
            add_squares(sums, 4, t)
        for copy in copies:
            copy.wait()


def feed_fwd(ids, x, gathered, ctx_own, ctx_shared, valid, weights, layer, chunk=768, parts=1):
    w_out, out_bias, ln_scale, ln_shift, ffn_in, ffn_in_bias, ffn_out, ffn_out_bias = weights
    half, width = x.shape[1], x.shape[2]
    tokens, ff = 3 * half, ffn_in.shape[2]
    full = lambda *shape: spec(shape, *([0] * len(shape)))
    dense = ((tokens, width), bf16)
    column = ((tokens, 128), f32)
    outs = [dense, column, dense, column, dense, ((tokens, ff), bf16), ((tokens, ff), bf16), dense,
            ((8, width), f32)]
    out_specs = [full(*s) for s, _ in outs]
    out_specs[5] = out_specs[6] = spec((tokens, chunk), 0, step)
    for k in (0, 1, 4):
        out_specs[k] = pl.BlockSpec(memory_space=pl.ANY)
    return call(
        functools.partial(feed_fwd_kernel, layer=layer, parts=parts), "feed_forward", (ff // chunk,), ids,
        row_tiles(half, width, gathered)
        + [
            full(*ctx_own.shape), full(*ctx_shared.shape), spec((tokens, 128), 0, 0),
            spec((1, width, width), layer, 0, 0), full(*out_bias.shape), full(*ln_scale.shape),
            full(*ln_shift.shape), spec((1, width, chunk), layer, 0, step),
            spec((ffn_in_bias.shape[0], chunk), 0, step), spec((1, chunk, width), layer, step, 0),
            full(*ffn_out_bias.shape),
        ],
        [x, x, x, ctx_own, ctx_shared, valid, w_out, out_bias, ln_scale, ln_shift, ffn_in, ffn_in_bias,
         ffn_out, ffn_out_bias],
        out_specs, [shape_of(s, d) for s, d in outs],
        [
            pltpu.VMEM((tokens, width), f32), pltpu.VMEM((tokens, width), bf16), pltpu.VMEM((tokens, 128), f32),
            pltpu.VMEM((tokens, width), bf16), pltpu.SemaphoreType.DMA((3,)),
        ],
    )


def slab_place(ids, slab):
    relative = jnp.bitwise_xor(ids[2], slab)
    return (
        jnp.bitwise_or(
            jnp.left_shift(jnp.bitwise_and(relative, 1), 2),
            jnp.bitwise_or(jnp.bitwise_and(relative, 2), jnp.right_shift(relative, 2)),
        )
    )


def store_piece(ids, keep_ref, send_ref, slab, core_rows, row, value):
    place = slab_place(ids, slab)
    core = ids[0]
    low, high = value[0:core_rows], value[core_rows:]
    at = slice(row, row + core_rows)

    @pl.when(core == 0)
    def _():
        keep_ref[place, at, :], send_ref[place, at, :] = low, high

    @pl.when(core != 0)
    def _():
        keep_ref[place, at, :], send_ref[place, at, :] = high, low


def feed_bwd_kernel(
    ids, g0, g1, g2, n2_ref, r2_ref, n1_ref, r1_ref, scale_ref, out_ref, slope_ref, in_ref, w_out_ref,
    act_ref, mixed_in_ref, own_ref, shared_ref,
    mixed_ref, attn_ref, ctx_ref, sums_ref, pre_sum_ref, keep_ref, send_ref,
    res_ref, acc_ref, feed_ref, pre_ref, feed_t, mixed_t, *late,
    layer, parts,
):
    j = pl.program_id(0)
    outs, late = (mixed_ref, attn_ref, ctx_ref), late[3:] + late[:3]
    mixed_ref, attn_ref, ctx_ref = late[-3:]
    buffers, sems = late[:-4], late[-4]
    sources = (n1_ref, r1_ref, w_out_ref.at[layer], own_ref, shared_ref)
    copies = [pltpu.make_async_copy(a, b, sems.at[k]) for k, (a, b) in enumerate(zip(sources, buffers))]
    n1_ref, r1_ref, w_out_ref, own_ref, shared_ref = buffers
    results = [
        pltpu.make_async_copy(a, b, sems.at[5 + k]) for k, (a, b) in enumerate(zip((mixed_ref, attn_ref, ctx_ref), outs))
    ]

    @pl.when(j == 0)
    def _():
        for copy in copies:
            copy.start()

    tokens = n2_ref.shape[0]
    gain = lambda k: scale_ref[layer, k : k + 1, :].astype(f32)
    rows = NORM_ROWS

    @pl.when(j == 0)
    def _():
        sums_ref[...] = jnp.zeros_like(sums_ref)
        for t, g_ref in enumerate((g0, g1, g2)):
            count = g_ref.shape[1]

            def chunk(i, sums):
                at = i * rows
                to = pl.ds(t * count + at, rows)
                grad = g_ref[0, pl.ds(at, rows), :].astype(f32)
                normed = n2_ref[to, :].astype(f32)
                back = norm_back(grad, gain(1), normed, r2_ref[to, 0:1])
                res_ref[to, :] = back
                feed = back.astype(bf16)
                feed_ref[to, :] = feed
                return (sums[0] + fold(grad * normed), sums[1] + fold(grad), sums[2] + fold(feed.astype(f32)))

            zero = jnp.zeros((8, n2_ref.shape[1]), f32)
            sums = row_loop(count // rows, chunk, (zero, zero, zero))
            for k, x in zip((1, 3, 5), sums):
                sums_ref[k : k + 1, :] += col_sum(x)
        for side in range(2):

            @pl.when(ids[1] == side)
            def _():
                feed_t[...] = feed_ref[:, LANES * side : LANES * side + LANES].T

        mixed_t[...] = mixed_in_ref[...].T

    cols = slope_ref.shape[1] // parts
    at = lambda k: slice(cols * k, cols * k + cols)
    g_act = dot_nt(feed_ref[...], out_ref[0, at(0)])
    for k in range(parts):
        coming = dot_nt(feed_ref[...], out_ref[0, at(k + 1)]) if k + 1 < parts else None
        g_pre = (g_act * slope_ref[:, at(k)].astype(f32)).astype(bf16)
        pre_ref[:, at(k)] = g_pre
        pre_sum_ref[:, at(k)] = jnp.broadcast_to(col_sum(g_pre.astype(f32)), (8, cols))
        g_act = coming
    total = dot_nt(pre_ref[...], in_ref[0])

    @pl.when(j == 0)
    def _():
        acc_ref[...] = total

    @pl.when(j > 0)
    def _():
        acc_ref[...] += total

    width = mixed_t.shape[0]

    @pl.when(j == pl.num_programs(0) - 1)
    def _():
        for copy in copies:
            copy.wait()

        def chunk(i, sums):
            to = pl.ds(i * rows, rows)
            g_mixed = acc_ref[to, :] + res_ref[to, :]
            mixed_ref[to, :] = g_mixed.astype(bf16)
            normed = n1_ref[to, :].astype(f32)
            attn = norm_back(g_mixed, gain(0), normed, r1_ref[to, 0:1]).astype(bf16)
            attn_ref[to, :] = attn
            return (sums[0] + fold(g_mixed * normed), sums[1] + fold(g_mixed), sums[2] + fold(attn.astype(f32)))

        zero = jnp.zeros((8, width), f32)
        sums = row_loop(tokens // rows, chunk, (zero, zero, zero))
        for k, x in zip((0, 2, 4), sums):
            sums_ref[k : k + 1, :] = col_sum(x)
        results[0].start()
        results[1].start()
        ctx_ref[...] = dot_nt(attn_ref[...], w_out_ref[...]).astype(bf16)
        results[2].start()

    high = LANES // 2
    slabs = act_ref.shape[1] // LANES
    result = dot(feed_t[...], act_ref[...]).astype(bf16)
    for k in range(slabs):
        store_piece(ids, keep_ref, send_ref, j * slabs + k, high, 0, result[:, LANES * k : LANES * k + LANES])
    slab_rows = width // SUPER
    half = slab_rows // 2
    steps = 4 // slabs
    for s in range(2 * steps):

        @pl.when((j == s) & (ids[1] == s // steps))
        def _():
            result = dot(mixed_t[...], pre_ref[...]).astype(bf16)
            for slab in range(SUPER):
                for k in range(slabs):
                    store_piece(
                        ids, keep_ref, send_ref, slab, half, high + ((s % steps) * slabs + k) * half,
                        result[slab_rows * slab : slab_rows * slab + slab_rows, LANES * k : LANES * k + LANES],
                    )

    @pl.when(j == pl.num_programs(0) - 1)
    def _():
        long = own_ref.shape[1]
        for side in range(2):

            @pl.when(ids[1] == side)
            def _():
                lanes = slice(LANES * side, LANES * side + LANES)
                result = dot(own_ref[...], attn_ref[0:long, lanes]) + dot(shared_ref[...], attn_ref[long:, lanes])
                result = result.astype(bf16)
                for slab in range(SUPER):
                    store_piece(ids, keep_ref, send_ref, slab, half, high + 4 * half,
                                result[slab_rows * slab : slab_rows * slab + slab_rows])
        for copy in results:
            copy.wait()


def feed_bwd(ids, grad, gathered, kept, slope, act, mixed, ctx_own, ctx_shared, weights, layer, chunk=768, parts=3):
    w_out, out_bias, ln_scale, ln_shift, ffn_in, ffn_in_bias, ffn_out, ffn_out_bias = weights
    n1, r1, n2, r2 = kept
    half, width = grad.shape[1], grad.shape[2]
    tokens, ff = 3 * half, ffn_in.shape[2]
    once = lambda *shape: pl.BlockSpec(shape, lambda i, ids: (0,) * len(shape), pipeline_mode=pl.Buffered(1))
    full = lambda *shape: spec(shape, *([0] * len(shape)))
    anywhere = pl.BlockSpec(memory_space=pl.ANY)
    dense = ((tokens, width), bf16)
    piece = ((SUPER, LANES + width // SUPER // 2, LANES), bf16)
    outs = [dense, dense, dense, ((8, width), f32), ((8, ff), f32), piece, piece]
    out_specs = [full(*s) for s, _ in outs]
    out_specs[4] = spec((8, chunk), 0, step)
    out_specs[0:3] = [anywhere] * 3
    return call(
        functools.partial(feed_bwd_kernel, layer=layer, parts=parts), "feed_backward", (ff // chunk,), ids,
        row_tiles(half, width, gathered)
        + [
            once(tokens, width), once(tokens, 128), anywhere, anywhere,
            full(*ln_scale.shape), spec((1, chunk, width), layer, step, 0), spec((tokens, chunk), 0, step),
            spec((1, width, chunk), layer, 0, step), anywhere,
            spec((tokens, chunk), 0, step), once(tokens, width), anywhere, anywhere,
        ],
        [grad, grad, grad, n2, r2, n1, r1, ln_scale, ffn_out, slope, ffn_in, w_out, act, mixed, ctx_own,
         ctx_shared],
        out_specs, [shape_of(s, d) for s, d in outs],
        [
            pltpu.VMEM((tokens, width), f32), pltpu.VMEM((tokens, width), f32),
            pltpu.VMEM((tokens, width), bf16), pltpu.VMEM((tokens, chunk), bf16),
            pltpu.VMEM((LANES, tokens), bf16), pltpu.VMEM((width, tokens), bf16),
            pltpu.VMEM((tokens, width), bf16), pltpu.VMEM((tokens, width), bf16), pltpu.VMEM((tokens, width), bf16),
            pltpu.VMEM((tokens, width), bf16), pltpu.VMEM((tokens, 128), f32),
            pltpu.VMEM((width, width), bf16), pltpu.VMEM(ctx_own.shape, bf16),
            pltpu.VMEM(ctx_shared.shape, bf16), pltpu.SemaphoreType.DMA((8,)),
        ],
    )


def joint_bwd_kernel(
    ids, x0, x1, x2, own_ref, shared_ref, arrived_ref, w_ref, attn_ref, rel0_ref, rel1_ref, vec_ref, pre_sum_ref,
    h_ref, keep_ref, send_ref, acc_ref, x_t, sums_ref, mine_ref,
    *, split,
):
    j = pl.program_id(0)
    width = x_t.shape[0]
    rows = width // SUPER
    half = rows // 2

    @pl.when(j == 0)
    def _():
        x_t[...] = jnp.concatenate([x0[0].T, x1[0].T, x2[0].T], 1)
        sums_ref[...] = jnp.zeros_like(sums_ref)

    far = arrived_ref[0].astype(f32) * (j > 0).astype(f32)
    near = (shared_ref[0].astype(f32) + far).astype(bf16)
    joint = jnp.concatenate([own_ref[0], near], 0)
    part = dot_nt(joint, w_ref[0])
    if split:
        mine_ref[...] = joint

    @pl.when(j == 0)
    def _():
        flag = (ids[1] == 0).astype(f32) if split else 1.0
        acc_ref[...] = part + attn_ref[...].astype(f32) * flag

    @pl.when(j > 0)
    def _():
        acc_ref[...] += part

    for side in range(2):
        lanes = slice(LANES * side, LANES * side + LANES)

        @pl.when(ids[1] == side)
        def _():
            if not split:
                mine_ref[...] = joint[:, lanes]
            sums_ref[j, :, lanes] = jnp.broadcast_to(col_sum(mine_ref[...].astype(f32)), (8, LANES))

    result = dot(x_t[...], mine_ref[...]).astype(bf16)
    for group in range(3):

        @pl.when(j == group)
        def _():
            for slab in range(SUPER):
                store_piece(ids, keep_ref, send_ref, slab, half, group * half,
                            result[rows * slab : rows * slab + rows])

    @pl.when(j == pl.num_programs(0) - 1)
    def _():
        h_ref[...] = acc_ref[...].astype(bf16)
        rel = (rel0_ref[...] + rel1_ref[...]).astype(bf16)
        count = rel.shape[0] // SUPER
        lines = jnp.concatenate([vec_ref[0:6, :], sums_ref[0, 0:1], sums_ref[2, 0:1]], 0)
        blank = jnp.zeros((8, LANES - rows), f32)
        for slab in range(SUPER):
            narrow = jnp.concatenate([lines[:, rows * slab : rows * slab + rows], blank], 1)
            wide = pre_sum_ref[0:1, LANES * slab : LANES * slab + LANES]
            small = jnp.concatenate([narrow, wide, jnp.zeros((count - 9, LANES), f32)], 0).astype(bf16)
            both = jnp.concatenate([rel[count * slab : count * slab + count], small], 0)
            store_piece(ids, keep_ref, send_ref, slab, count, 3 * half, both)


def joint_bwd(ids, x, gathered, own, shared, arrived, w_qkv, g_attn, rel0, rel1, vec, pre_sum, layer, split):
    _, length, cols = own.shape
    width = g_attn.shape[1]
    half = shared.shape[1]
    tokens = length + half
    full = lambda *shape: spec(shape, *([0] * len(shape)))
    side = lambda i, ids: 0 if split else ids[1]
    piece = (SUPER, (width // SUPER // 2) * 3 + rel0.shape[0] // SUPER, LANES)
    return call(
        functools.partial(joint_bwd_kernel, split=split), "projections_backward", (3,), ids,
        row_tiles(half, width, gathered)
        + [
            spec((1, length, cols), step, 0, 0), spec((1, half, cols), step, 0, 0),
            spec((1, half, cols), lambda i, ids: jnp.maximum(i - 1, 0), 0, 0),
            spec((1, width, cols), layer, 0, lambda i, ids: 2 * i + ids[1] if split else i),
            full(tokens, width), spec((rel0.shape[0], LANES), 0, side), spec((rel0.shape[0], LANES), 0, side),
            full(*vec.shape), full(*pre_sum.shape),
        ],
        [x, x, x, own, shared, arrived, w_qkv, g_attn, rel0, rel1, vec, pre_sum],
        [full(tokens, width), full(*piece), full(*piece)],
        [shape_of((tokens, width), bf16), shape_of(piece, bf16), shape_of(piece, bf16)],
        [
            pltpu.VMEM((tokens, width), f32), pltpu.VMEM((width, tokens), bf16),
            pltpu.VMEM((3, 8, width), f32), pltpu.VMEM((tokens, LANES), bf16),
        ],
    )


def place_rows_kernel(ids, own_ref, other_ref, out_ref):
    i = pl.program_id(0)
    core = ids[0]
    row = i // 2
    mine = jnp.where(row == 2, (i - 4) == core, row == core)

    @pl.when(mine)
    def _():
        out_ref[0] = own_ref[0].astype(out_ref.dtype)

    @pl.when(jnp.logical_not(mine))
    def _():
        out_ref[0] = other_ref[0].astype(out_ref.dtype)


def place_rows(ids, own, other, dtype):
    tokens, width = own.shape
    half = tokens // 3
    tile = lambda i, ids: jnp.where(i < 4, i % 2, 2)
    tiles = lambda x: x.reshape(3, half, width)
    return call(
        place_rows_kernel, "place_rows", (6,), ids,
        [spec((1, half, width), tile, 0, 0)] * 2, [tiles(own), tiles(other)],
        spec((1, half, width), step, 0, 0), shape_of((6, half, width), dtype),
    )


def collect(ids, refs, scratch):
    for core in range(2):
        for side in range(2):

            @pl.when((ids[0] == core) & (ids[1] == side))
            def _():
                scratch[core, side] = refs[0][...]
                scratch[core, 1 - side] = refs[1][...]
                scratch[1 - core, side] = refs[2][...]
                scratch[1 - core, 1 - side] = refs[3][...]


def spread_columns(scratch, out_ref, layer, at, groups, rows, inner=False):
    for core in range(2):
        for side in range(2):
            for g in range(groups):
                piece = scratch[core, side, at + g * rows : at + g * rows + rows, :]
                lane = ((g * 2 + side) if inner else (side * groups + g)) * LANES
                out_ref[layer, core * rows : core * rows + rows, lane : lane + LANES] = piece.astype(f32)


def unpack_feed_kernel(ids, *refs):
    inputs, (in_ref, out_ref, w_out_ref, scratch) = refs[:8], refs[8:]
    high = LANES // 2
    for layer in range(2):
        collect(ids, inputs[4 * layer : 4 * layer + 4], scratch)
        columns = [scratch[core, side, 0:high, :] for side in range(2) for core in range(2)]
        out_ref[layer] = jnp.concatenate(columns, 0).astype(f32).T
        rows = in_ref.shape[1] // 2
        spread_columns(scratch, in_ref, layer, high, 4, rows)
        spread_columns(scratch, w_out_ref, layer, high + 4 * rows, 1, rows)


def unpack_attention_kernel(ids, *refs):
    inputs = refs[:8]
    qkv_ref, rel_ref, qv_ref, out_bias_ref, scale_ref, shift_ref, in_bias_ref, ffn_bias_ref = refs[8:16]
    scratch = refs[16]
    rows = qkv_ref.shape[1] // 2
    wide = 2 * rows
    for layer in range(2):
        collect(ids, inputs[4 * layer : 4 * layer + 4], scratch)
        spread_columns(scratch, qkv_ref, layer, 0, 3, rows, True)
        at = 3 * rows
        count = rel_ref.shape[2]
        rel = jnp.concatenate([scratch[0, side, at : at + count, :] for side in range(2)], 1).astype(f32)
        size = rel_ref.shape[3]
        for head in range(rel_ref.shape[1]):
            rel_ref[layer, head] = rel[:, size * head : size * head + size]
        small = scratch[1, 0, at : at + count, :].astype(f32)
        scale_ref[layer] = small[0:2, 0:wide]
        shift_ref[layer] = small[2:4, 0:wide]
        out_bias_ref[layer : layer + 1] = small[4:5, 0:wide]
        ffn_bias_ref[layer : layer + 1] = small[5:6, 0:wide]
        other = scratch[1, 1, at : at + count, :].astype(f32)
        qv_ref[layer] = small[6:8, 0:wide] + other[6:8, 0:wide]
        in_bias_ref[layer : layer + 1] = small[8:9]


def unpack(kernel, name, ids, pieces, shapes):
    full = lambda *shape: spec(shape, *([0] * len(shape)))
    return call(
        kernel, name, (1,), ids, [full(*p.shape) for p in pieces], pieces,
        [full(*s) for s in shapes], [shape_of(s, f32) for s in shapes],
        [pltpu.VMEM((2, 2) + pieces[0].shape, bf16)],
    )


def body(
    stream, cotangent, segments, word_boxes, valid_mask, w_qkv, qv_bias, w_out, out_bias, rel_proj,
    ln_scale, ln_shift, ffn_in, ffn_in_bias, ffn_out, ffn_out_bias,
):
    sections = lax.axis_size("section")
    dp = lax.axis_size("dp")
    section = lax.axis_index("section")
    dp_index = lax.axis_index("dp")
    core, side = section % 2, section // 2
    rows, length, width = stream.shape
    layers = w_qkv.shape[0]
    ff = ffn_in.shape[2]
    half = length // 2
    assert rows == 3 and sections == 4 and layers == 2 and dp % SUPER == 0 and width == 2 * LANES
    fine = dp // SUPER
    ids = jnp.stack([core, side, dp_index // fine]).astype(jnp.int32)
    weights = (w_out, out_bias, ln_scale, ln_shift, ffn_in, ffn_in_bias, ffn_out, ffn_out_bias)
    rel_pairs = rel_proj.reshape(layers, width // 128, 128, 128)

    def flip(x, bit):
        return lax.ppermute(x, "section", [(i, i ^ bit) for i in range(sections)])

    def flip_dp(x, bit):
        return lax.ppermute(x, "dp", [(i, i ^ bit) for i in range(dp)])

    tables = make_tables(ids, jnp.swapaxes(word_boxes, 0, 1), segments, valid_mask)
    ctab, stab, valid_col = tables[3], tables[4], tables[7]

    halves = lambda x: x.reshape(-1, half, width)
    x, gathered = halves(stream), True
    kept = []
    for l in range(layers):
        joint, turned, kv = project(ids, x, gathered, w_qkv, qv_bias, rel_pairs, ctab, stab, l)
        kv_far = flip(kv, 1)
        ctx_own, lse_own = attention_fwd(ids, False, tables, joint, turned, None)
        ctx_shared, lse_shared = attention_fwd(ids, True, tables, joint, turned, kv_far)
        n1, r1, n2, r2, mixed, act, slope, out, squares = feed_fwd(
            ids, x, gathered, ctx_own, ctx_shared, valid_col, weights, l
        )
        kept.append(
            dict(x=x, gathered=gathered, joint=joint, turned=turned, kv_far=kv_far, ctx_own=ctx_own,
                 ctx_shared=ctx_shared, lse_own=lse_own, lse_shared=lse_shared, norms=(n1, r1, n2, r2),
                 mixed=mixed, act=act, slope=slope, out=out, squares=squares)
        )
        x, gathered = halves(out), False

    clock = [ids]

    def pin(state):
        clock[0], state = lax.optimization_barrier((clock[0], state))
        return state

    def absorb(keep, arrived):
        keep, arrived = pin((keep, arrived))
        n = keep.shape[0] // 2
        return pin((keep[:n] + arrived[:n], keep[n:] + arrived[n:]))

    def last(keep, arrived):
        keep, arrived = pin((keep, arrived))
        x = (keep + arrived)[0]
        bit = 1
        while bit < fine:
            x = x + flip_dp(x, bit)
            bit *= 2
        return pin(x)

    def hop(state, bit):
        return state[0], flip_dp(state[1], fine << bit)

    def all_sides(x):
        far = flip(x, 2)
        return [x, far, flip(x, 1), flip(far, 1)]

    def feed_back(l, grad, gathered):
        k = kept[l]
        g_mixed, g_attn, g_ctx, vec, pre_sum, keep, send = feed_bwd(
            clock[0], grad, gathered, k["norms"], k["slope"], k["act"], k["mixed"], k["ctx_own"],
            k["ctx_shared"], weights, l,
        )
        k["g_mixed"] = g_mixed
        return g_attn, g_ctx, vec, pre_sum, (keep, flip(send, 1))

    def attention_back(l, shared, g_ctx):
        k = kept[l]
        return attention_bwd(
            clock[0], shared, tables, k["joint"], k["turned"], k["kv_far"] if shared else None,
            k["lse_shared" if shared else "lse_own"], g_ctx, rel_pairs, l, l == 0,
        )

    def joint_back(l, own_grads, shared_keep, arrived, g_attn, rel_own, rel_shared, vec, pre_sum):
        k = kept[l]
        g_h, keep, send = joint_bwd(
            clock[0], k["x"], k["gathered"], own_grads, shared_keep, arrived, w_qkv, g_attn, rel_own,
            rel_shared, vec, pre_sum, l, l == 0,
        )
        k["g_h"] = g_h
        return g_h, (keep, flip(send, 1))

    g_attn, g_ctx, vec, pre_sum, f1 = feed_back(1, halves(cotangent), True)
    shared_keep, shared_send, rel_shared = attention_back(1, True, g_ctx)
    arrived = flip(shared_send, 1)
    f1 = hop(absorb(*f1), 0)
    own_grads, rel_own = attention_back(1, False, g_ctx)
    g_h, a1 = joint_back(1, own_grads, shared_keep, arrived, g_attn, rel_own, rel_shared, vec, pre_sum)

    f1 = hop(absorb(*f1), 1)
    a1 = hop(absorb(*a1), 0)
    g_attn, g_ctx, vec, pre_sum, f0 = feed_back(0, halves(g_h), False)
    f1 = hop(absorb(*f1), 2)
    a1 = hop(absorb(*a1), 1)
    shared_keep, shared_send, rel_shared = attention_back(0, True, g_ctx)
    arrived = flip(shared_send, 1)
    f0 = hop(absorb(*f0), 0)
    own_grads, rel_own = attention_back(0, False, g_ctx)
    f1 = last(*f1)
    a1 = hop(absorb(*a1), 2)
    g_h, a0 = joint_back(0, own_grads, shared_keep, arrived, g_attn, rel_own, rel_shared, vec, pre_sum)
    g_h_far = flip(g_h, 2)
    f1 = all_sides(f1)
    f0 = hop(absorb(*f0), 1)
    a0 = hop(absorb(*a0), 0)
    a1 = all_sides(last(*a1))

    def of_layer(name):
        return jnp.where(side == 0, kept[0][name], kept[1][name])

    def to_section(first, second, dtype):
        a, b = of_layer(first), of_layer(second)
        own, away = jnp.where(core == 0, a, b), jnp.where(core == 0, b, a)
        return place_rows(ids, own, flip(away, 1), dtype).reshape(1, rows, length, width)

    section_outs = pin(to_section("mixed", "out", bf16))
    a0 = hop(absorb(*a0), 1)
    f0 = hop(absorb(*f0), 2)
    kept[0]["g_h"] = pin(g_h + g_h_far)
    in_grads = pin(to_section("g_h", "g_mixed", f32))
    a0 = hop(absorb(*a0), 2)
    f0 = all_sides(last(*f0))
    a0 = all_sides(last(*a0))

    squares_mine = jnp.sum(of_layer("squares"), 1).reshape(2, 2, 2)
    squares_far = flip(squares_mine, 1)
    sub = lambda v: lax.dynamic_index_in_dim(v, core, 0, keepdims=False)
    near, far = sub(squares_mine), sub(squares_far)
    first = jnp.where(core == 0, near[:, 0], far[:, 0])
    second = jnp.where(core == 0, far[:, 0], near[:, 0])
    square_rows = jnp.stack([first, second, near[:, 1] + far[:, 1]])
    row_counts = jnp.sum(valid_mask.astype(f32), 1)
    root_mean_squares = jnp.sqrt(square_rows / (width * jnp.maximum(row_counts, 1.0))[:, None])[None]

    slab = width // SUPER
    d_ffn_in, d_ffn_out, d_out = unpack(
        unpack_feed_kernel, "unpack_feed", clock[0], f0 + f1,
        [(2, slab, ff), (2, ff // SUPER, width), (2, slab, width)],
    )
    d_ffn_in, d_ffn_out, d_out = pin((d_ffn_in, d_ffn_out, d_out))
    rel_rows = 128 // SUPER
    d_qkv, d_rel, d_qv, d_out_bias, d_scale, d_shift, d_in_bias, d_ffn_bias = unpack(
        unpack_attention_kernel, "unpack_attention", clock[0], a0 + a1,
        [(2, slab, 3 * width), (2, rel_proj.shape[1], rel_rows, rel_proj.shape[2]), (2, 2, slab), (2, slab),
         (2, 2, slab), (2, 2, slab), (2, LANES), (2, slab)],
    )

    def own_part(x, axis):
        n = x.shape[axis] // fine
        return x if fine == 1 else lax.dynamic_slice_in_dim(x, (dp_index % fine) * n, n, axis)

    return (
        section_outs,
        in_grads,
        own_part(d_qkv, 1),
        own_part(d_qv, 2),
        own_part(d_out, 1),
        own_part(d_out_bias, 1),
        own_part(jnp.swapaxes(d_rel, 2, 3), 3),
        own_part(d_scale, 2),
        own_part(d_shift, 2),
        own_part(d_ffn_in, 1),
        own_part(d_in_bias, 1),
        own_part(d_ffn_out, 1),
        own_part(d_ffn_bias, 1),
        root_mean_squares,
    )


def solution(mesh):
    return jax.shard_map(
        body,
        mesh=mesh,
        in_specs=(
            P("dp", None, None),
            P("dp", None, None),
            P("dp", None),
            P(None, "dp", None),
            P("dp", None),
        )
        + (P(),) * 11,
        out_specs=(
            P("section", "dp", None, None),
            P("section", "dp", None, None),
            P(None, "dp", None),
            P(None, None, "dp"),
            P(None, "dp", None),
            P(None, "dp"),
            P(None, None, None, "dp"),
            P(None, None, "dp"),
            P(None, None, "dp"),
            P(None, "dp", None),
            P(None, "dp"),
            P(None, "dp", None),
            P(None, "dp"),
            P("section", "dp", None),
        ),
        check_vma=False,
    )
```

```python
import functools

import jax
import jax.numpy as jnp
from jax import lax
from jax.experimental import pallas as pl
from jax.experimental.pallas import tpu as pltpu
from jax.sharding import PartitionSpec as P

ln_eps = 1e-05
masked_score = -1e30
bf16 = jnp.bfloat16
f32 = jnp.float32
MB = 1 << 20
SUPER = 8
LANES = 384
NORM_ROWS = 64

ERF_COEFS = (
    0.7978849414899046, 0.0363330844086688, -3.259474462099993e-05, -5.5306316685416947e-05,
    3.964773125473232e-06, -1.322662757755248e-07, 1.7562773256476674e-09,
)


def dot(a, b):
    return lax.dot_general(a, b, (((1,), (0,)), ((), ())), preferred_element_type=f32)


def dot_nt(a, b):
    return lax.dot_general(a, b, (((1,), (1,)), ((), ())), preferred_element_type=f32)


def gelu_and_slope(x):
    square = x * x
    g = ERF_COEFS[-1]
    for c in ERF_COEFS[-2::-1]:
        g = g * square + c
    phi = 0.5 * jnp.tanh(x * g) + 0.5
    density = jnp.exp2(square * (-0.5 * 1.4426950408889634)) * 0.3989422804014327
    return x * phi, phi + x * density


def norm_parts(residual):
    average = jnp.mean(residual, -1, keepdims=True)
    centered = residual - average
    inverse = lax.rsqrt(jnp.mean(centered * centered, -1, keepdims=True) + ln_eps)
    return centered * inverse, inverse


def norm_back(gradient, gain, normed, inverse):
    dnormed = gradient * gain
    return inverse * (
        dnormed
        - jnp.mean(dnormed, -1, keepdims=True)
        - normed * jnp.mean(dnormed * normed, -1, keepdims=True)
    )


def row_loop(count, chunk, sums):
    for i in range(count):
        sums = chunk(i, sums)
    return sums


def fold(x):
    return jnp.sum(x.reshape(-1, 8, x.shape[1]), 0)


def col_sum(x):
    return jnp.sum(x, 0, keepdims=True)


COST_US = dict(
    tables=4, projections=8, attention_forward=7, feed_forward=24, feed_backward=30, attention_backward=12,
    projections_backward=3, place_rows=4,
    unpack_feed=4, unpack_attention=3,
)


def call(kernel, name, grid, ids, in_specs, inputs, out_specs, out_shape, scratch=(), micros=None):
    micros = COST_US[name] if micros is None else micros
    cost = pl.CostEstimate(flops=micros * 1100000000, bytes_accessed=micros * 1000000, transcendentals=0)
    return pl.pallas_call(
        kernel,
        grid_spec=pltpu.PrefetchScalarGridSpec(
            num_scalar_prefetch=1,
            grid=grid,
            in_specs=in_specs,
            out_specs=out_specs,
            scratch_shapes=list(scratch),
        ),
        out_shape=out_shape,
        compiler_params=pltpu.CompilerParams(vmem_limit_bytes=62 * MB),
        cost_estimate=cost,
        name=name,
    )(ids, *inputs)


def spec(shape, *index):
    def index_map(i, ids):
        return tuple(x(i, ids) if callable(x) else x for x in index)

    return pl.BlockSpec(shape, index_map)


def shape_of(shape, dtype):
    return jax.ShapeDtypeStruct(shape, dtype)


step = lambda i, ids: i


def row_tiles(half, width, gathered):
    if not gathered:
        return [spec((1, half, width), t, 0, 0) for t in range(3)]
    core = lambda ids: ids[0]
    return [
        spec((1, half, width), lambda i, ids: 2 * core(ids), 0, 0),
        spec((1, half, width), lambda i, ids: 2 * core(ids) + 1, 0, 0),
        spec((1, half, width), lambda i, ids: 4 + core(ids), 0, 0),
    ]


def tables_kernel(
    ids, boxes_ref, seg_ref, valid_ref,
    cos_ref, sin_ref, kf_ref, ctab_ref, stab_ref, code_ref, segrow_ref, valid_col_ref,
):
    core = ids[0]
    length = seg_ref.shape[1]
    half = length // 2

    def ordered(read):
        near = pl.multiple_of(core * half, half)
        far = pl.multiple_of((1 - core) * half, half)
        return jnp.concatenate(
            [read(pl.ds(core, 1), slice(None)), read(2, pl.ds(near, half)), read(2, pl.ds(far, half))], 1
        )

    def row_of(ref):
        def read(r, c):
            r = pl.ds(2, 1) if isinstance(r, int) else r
            return ref[r, c]
        return ordered(read)

    count = length * 2
    at = lax.broadcasted_iota(jnp.int32, (1, count), 1)
    shared = jnp.where(
        at < length + half, at - length + core * half, at - length - half + (1 - core) * half
    )
    position = jnp.where(at < length, at, shared).astype(f32)
    rate_at = lax.broadcasted_iota(jnp.int32, (32, 1), 0).astype(f32)
    text = position * jnp.exp(rate_at * (-9.210340371976184 / 32))
    box_rate = jnp.exp2(-lax.broadcasted_iota(jnp.int32, (8, 1), 0).astype(f32))
    angles = [text]
    for c in range(4):
        coords = row_of(boxes_ref.at[:, c]).astype(f32)
        angles.append(coords * box_rate)
    angles = jnp.concatenate(angles, 0)
    cosines, sines = jnp.cos(angles), jnp.sin(angles)
    cos_ref[...], sin_ref[...] = cosines, sines
    kf_ref[...] = jnp.concatenate([cosines, sines], 0).T.astype(bf16)
    ctab_ref[...] = jnp.concatenate([cosines, -cosines], 0).T
    stab_ref[...] = jnp.concatenate([sines, sines], 0).T
    seg = row_of(seg_ref).astype(f32)
    valid = row_of(valid_ref).astype(f32)
    segrow_ref[...] = jnp.broadcast_to(seg, segrow_ref.shape)
    code_ref[...] = jnp.broadcast_to(jnp.where(valid > 0, seg, -1.0), (128, count)).T
    valid_col_ref[...] = jnp.broadcast_to(valid, (128, count)).T


def make_tables(ids, word_boxes, segments, valid_mask):
    length = segments.shape[1]
    count = 2 * length
    full = lambda *shape: spec(shape, *([0] * len(shape)))
    outs = [
        ((64, count), f32), ((64, count), f32), ((count, 128), bf16), ((count, 128), f32),
        ((count, 128), f32), ((count, 128), f32), ((8, count), f32), ((count, 128), f32),
    ]
    return call(
        tables_kernel, "tables", (1,), ids,
        [full(*word_boxes.shape), full(*segments.shape), full(*valid_mask.shape)],
        [word_boxes, segments, valid_mask],
        [full(*s) for s, _ in outs], [shape_of(s, d) for s, d in outs],
    )


def qkv_kernel(
    ids, x0, x1, x2, w_ref, bias_ref, rel_ref, ctab_ref, stab_ref, joint_ref, turned_out, kv_ref, x_ref,
    turned_ref, sem, *, layer,
):
    j = pl.program_id(0)
    copy = pltpu.make_async_copy(turned_ref, turned_out, sem)
    half = x0.shape[1]

    @pl.when(j == 0)
    def _():
        x_ref[0:half], x_ref[half : 2 * half], x_ref[2 * half :] = x0[0], x1[0], x2[0]

    flags = [(j == 0).astype(f32), (j == 2).astype(f32)]
    bias = bias_ref[layer, 0:1, :].astype(f32) * flags[0] + bias_ref[layer, 1:2, :].astype(f32) * flags[1]
    joint = (dot(x_ref[...], w_ref[0]) + bias).astype(bf16)
    joint_ref[...] = joint
    kv_ref[...] = joint[2 * half :]

    @pl.when(j == 0)
    def _():
        ctab, stab = ctab_ref[...], stab_ref[...]
        row = lax.broadcasted_iota(jnp.int32, (128, 128), 0)
        for p in range(rel_ref.shape[1]):
            rel = rel_ref[0, p]
            zero = jnp.zeros_like(rel)
            block = jnp.concatenate([jnp.where(row < 64, rel, zero), jnp.where(row < 64, zero, rel)], 1)
            coef = dot(joint[:, 128 * p : 128 * p + 128], block)
            for e in range(2):
                c = coef[:, 128 * e : 128 * e + 128]
                at = 256 * p + 128 * e
                turned_ref[:, at : at + 128] = (c * ctab + pltpu.roll(c, 64, 1) * stab).astype(bf16)
        copy.start()

    @pl.when(j == pl.num_programs(0) - 1)
    def _():
        copy.wait()


def project(ids, x, gathered, w_qkv, qv_bias, rel_pairs, ctab, stab, layer):
    half, width = x.shape[1], x.shape[2]
    tokens = 3 * half
    pairs = rel_pairs.shape[1]
    return call(
        functools.partial(qkv_kernel, layer=layer), "projections", (3,), ids,
        row_tiles(half, width, gathered)
        + [
            spec((1, width, width), layer, 0, step), spec(qv_bias.shape, 0, 0, 0),
            spec((1, pairs, 128, 128), layer, 0, 0, 0), spec((tokens, 128), 0, 0),
            spec((tokens, 128), 0, 0),
        ],
        [x, x, x, w_qkv, qv_bias, rel_pairs, ctab, stab],
        [
            spec((tokens, width), 0, step), pl.BlockSpec(memory_space=pl.ANY),
            spec((half, width), 0, lambda i, ids: jnp.maximum(i - 1, 0)),
        ],
        [
            shape_of((tokens, 3 * width), bf16), shape_of((tokens, 2 * width), bf16),
            shape_of((half, 2 * width), bf16),
        ],
        [
            pltpu.VMEM((tokens, width), bf16), pltpu.VMEM((tokens, 2 * width), bf16),
            pltpu.SemaphoreType.DMA(()),
        ],
    )


def lane_half(shape, half):
    lane = lax.broadcasted_iota(jnp.int32, shape, 1)
    return (lane < 64) if half == 0 else (lane >= 64)


def only_half(x, half):
    return jnp.where(lane_half(x.shape, half), x, jnp.zeros_like(x))


def fill_bias(code_ref, seg_ref, bias_ref):
    shape = bias_ref.shape
    code = jnp.concatenate([code_ref[...]] * (shape[1] // 128), 1)
    same = code == seg_ref[0:1, :]
    key_at = lax.broadcasted_iota(jnp.int32, shape, 0)
    query_at = lax.broadcasted_iota(jnp.int32, shape, 1)
    bias_ref[...] = jnp.where(same | (key_at == query_at), 0.0, masked_score)


def attention_fwd_kernel(
    ids, code_ref, seg_ref, kf_ref, q_ref, turned_ref, k_ref, v_ref, *rest, per_step, shared,
):
    if shared:
        k_far, v_far, ctx_ref, lse_ref, bias_ref, k_all, v_all = rest
        half = k_ref.shape[0]
        k_all[0:half], k_all[half:] = k_ref[...], k_far[...]
        v_all[0:half], v_all[half:] = v_ref[...], v_far[...]
        k_ref, v_ref = k_all, v_all
    else:
        ctx_ref, lse_ref, bias_ref = rest

    @pl.when(pl.program_id(0) == 0)
    def _():
        fill_bias(code_ref, seg_ref, bias_ref)

    scale = jnp.asarray(0.125, bf16)
    units = [(pair, e) for pair in range(per_step) for e in range(2)]
    values_t = {}

    def scores_of(unit):
        pair, e = unit
        at = slice(128 * pair, 128 * pair + 128)
        turned = turned_ref[:, 256 * pair + 128 * e : 256 * pair + 128 * e + 128]
        qside = jnp.concatenate([turned, only_half(q_ref[:, at], e)], 1) * scale
        kside = jnp.concatenate([kf_ref[...], k_ref[:, at]], 1)
        return dot_nt(kside, qside) + bias_ref[...]

    def finish(unit, scores):
        pair, e = unit
        top = jnp.max(scores, 0, keepdims=True)
        expo = jnp.exp(scores - top)
        total = jnp.sum(expo, 0, keepdims=True)
        if pair not in values_t:
            values_t[pair] = v_ref[:, 128 * pair : 128 * pair + 128].T
        ctx = dot(values_t[pair][64 * e : 64 * e + 64], expo.astype(bf16))
        at = 128 * pair + 64 * e
        ctx_ref[at : at + 64, :] = (ctx * (1.0 / total)).astype(bf16)
        lse_ref[pair, e : e + 1, :] = top + jnp.log(total)

    scores = scores_of(units[0])
    for i, unit in enumerate(units):
        upcoming = scores_of(units[i + 1]) if i + 1 < len(units) else None
        finish(unit, scores)
        scores = upcoming


def attention_fwd(ids, shared, tables, joint, turned, kv_far, per_step=2):
    cos_t, sin_t, kf, ctab, stab, code, seg, valid = tables
    tokens, width = joint.shape[0], joint.shape[1] // 3
    half = tokens // 3
    nk = 2 * half
    nq = half if shared else nk
    key_rows = half if shared else nk
    lanes = 128 * per_step
    steps = width // lanes
    q_row = 2 if shared else 0
    at = lambda off: (lambda i, ids: i + off)
    in_specs = [
        spec((nk, 128), int(shared), 0), spec((8, nq), 0, q_row), spec((nk, 128), int(shared), 0),
        spec((nq, lanes), q_row, step), spec((nq, 2 * lanes), q_row, step),
        spec((key_rows, lanes), q_row, at(steps)), spec((key_rows, lanes), q_row, at(2 * steps)),
    ]
    inputs = [code, seg, kf, joint, turned, joint, joint]
    scratch = [pltpu.VMEM((nk, nq), f32)]
    if shared:
        in_specs += [spec((half, lanes), 0, step), spec((half, lanes), 0, at(steps))]
        inputs += [kv_far, kv_far]
        scratch += [pltpu.VMEM((nk, lanes), bf16)] * 2
    return call(
        functools.partial(attention_fwd_kernel, per_step=per_step, shared=shared),
        "attention_forward", (steps,), ids, in_specs, inputs,
        [spec((lanes, nq), step, 0), spec((per_step, 2, nq), step, 0, 0)],
        [shape_of((width, nq), bf16), shape_of((width // 128, 2, nq), f32)],
        scratch,
    )


def attention_bwd_kernel(
    ids, code_ref, seg_ref, kf_ref, cos_ref, sin_ref, rel_ref, lse_ref, gc_ref, q_ref, turned_ref,
    k_ref, v_ref, *rest, per_step, shared,
):
    if shared:
        k_far, v_far, keep_ref, send_ref, drel_ref, bias_ref, kft_ref, k_all, v_all = rest
        half = k_ref.shape[0]
        k_all[0:half], k_all[half:] = k_ref[...], k_far[...]
        v_all[0:half], v_all[half:] = v_ref[...], v_far[...]
        k_ref, v_ref = k_all, v_all
    else:
        keep_ref, drel_ref, bias_ref, kft_ref = rest

    @pl.when(pl.program_id(0) == 0)
    def _():
        fill_bias(code_ref, seg_ref, bias_ref)
        kft_ref[...] = kf_ref[...].T

    scale = jnp.asarray(0.125, bf16)
    cosines, sines = cos_ref[...], sin_ref[...]
    units = [(pair, e) for pair in range(per_step) for e in range(2)]
    store = {}

    def scores_of(unit):
        pair, e = unit
        at = slice(128 * pair, 128 * pair + 128)
        q_mine = only_half(q_ref[:, at], e)
        gc_mine = only_half(gc_ref[:, at], e)
        q_scaled = q_mine * scale
        turned = turned_ref[:, 256 * pair + 128 * e : 256 * pair + 128 * e + 128]
        qside = jnp.concatenate([turned * scale, q_scaled], 1)
        kside = jnp.concatenate([kf_ref[...], k_ref[:, at]], 1)
        scores = dot_nt(kside, qside) + bias_ref[...]
        gp = dot_nt(v_ref[:, at], gc_mine)
        return scores, gp, q_mine, gc_mine, q_scaled

    def finish(unit, parts):
        pair, e = unit
        scores, gp, q_mine, gc_mine, q_scaled = parts
        at = slice(128 * pair, 128 * pair + 128)
        shares = jnp.exp(scores - lse_ref[pair, e : e + 1, :])
        dv = dot(shares.astype(bf16), gc_mine)
        weighted = shares * gp
        delta = jnp.sum(weighted, 0, keepdims=True)
        gs = (weighted - shares * delta).astype(bf16)
        dk = dot(gs, q_scaled)
        if pair not in store:
            store[pair] = k_ref[:, at].T
        side_t = jnp.concatenate([kft_ref[...], store[pair][64 * e : 64 * e + 64]], 0)
        dside = dot(side_t, gs) * 0.125
        g_cos, g_sin = dside[0:64], dside[64:128]
        gcoef = jnp.concatenate(
            [g_cos * cosines + g_sin * sines, g_cos * sines - g_sin * cosines], 0
        ).astype(bf16)
        dq = dside[128:192] + dot(rel_ref[0, pair, 64 * e : 64 * e + 64], gcoef)
        drel = dot(gcoef, q_mine)
        if e == 0:
            store["even"] = (dq, dk, dv, drel)
            return
        dq0, dk0, dv0, drel0 = store["even"]
        dq = jnp.concatenate([dq0, dq], 0).T.astype(bf16)
        dk, dv = (dk0 + dk).astype(bf16), (dv0 + dv).astype(bf16)
        drel_ref[:, at] = drel0 + drel
        n = keep_ref.shape[1]
        keep_ref[0, :, at] = dq
        keep_ref[1, :, at], keep_ref[2, :, at] = dk[0:n], dv[0:n]
        if shared:
            send_ref[0, :, at], send_ref[1, :, at] = dk[n:], dv[n:]

    parts = scores_of(units[0])
    for i, unit in enumerate(units):
        upcoming = scores_of(units[i + 1]) if i + 1 < len(units) else None
        finish(unit, parts)
        parts = upcoming


def attention_bwd(ids, shared, tables, joint, turned, kv_far, lse, g_ctx, rel_pairs, layer, split, per_step=3):
    per_step = 3 if split else per_step
    cos_t, sin_t, kf, ctab, stab, code, seg, valid = tables
    tokens, width = joint.shape[0], joint.shape[1] // 3
    half = tokens // 3
    nk = 2 * half
    nq = half if shared else nk
    key_rows = half if shared else nk
    lanes = 128 * per_step
    all_steps = width // lanes
    steps = all_steps // 2 if split else all_steps
    out_width = lanes * steps
    first = lambda ids: ids[1] * steps if split else 0
    q_row = 2 if shared else 0
    at = lambda off: (lambda i, ids: first(ids) + i + off)
    here = at(0)
    in_specs = [
        spec((nk, 128), int(shared), 0), spec((8, nq), 0, q_row), spec((nk, 128), int(shared), 0),
        spec((64, nq), 0, q_row), spec((64, nq), 0, q_row),
        spec((1, per_step, 128, 128), layer, here, 0, 0),
        spec((per_step, 2, nq), here, 0, 0), spec((nq, lanes), q_row, here),
        spec((nq, lanes), q_row, here), spec((nq, 2 * lanes), q_row, here),
        spec((key_rows, lanes), q_row, at(all_steps)), spec((key_rows, lanes), q_row, at(2 * all_steps)),
    ]
    inputs = [code, seg, kf, cos_t, sin_t, rel_pairs, lse, g_ctx, joint, turned, joint, joint]
    scratch = [pltpu.VMEM((nk, nq), f32), pltpu.VMEM((128, nk), bf16)]
    out_specs = [spec((3, key_rows, lanes), 0, 0, step)]
    out_shape = [shape_of((3, key_rows, out_width), bf16)]
    if shared:
        in_specs += [spec((half, lanes), 0, here), spec((half, lanes), 0, at(all_steps))]
        inputs += [kv_far, kv_far]
        scratch += [pltpu.VMEM((nk, lanes), bf16)] * 2
        out_specs.append(spec((2, half, lanes), 0, 0, step))
        out_shape.append(shape_of((2, half, out_width), bf16))
    out_specs.append(spec((128, lanes), 0, step))
    out_shape.append(shape_of((128, out_width), f32))
    return call(
        functools.partial(attention_bwd_kernel, per_step=per_step, shared=shared),
        "attention_backward", (steps,), ids, in_specs, inputs, out_specs, out_shape, scratch,
        40 if shared else 12,
    )


def feed_fwd_kernel(
    ids, x0, x1, x2, own_ref, shared_ref, valid_ref, w_out_ref, out_bias_ref, scale_ref, shift_ref,
    in_ref, in_bias_ref, out_ref, ffn_bias_ref,
    n1_out, r1_out, n2_ref, r2_ref, mixed_out, act_ref, slope_ref, h_ref, squares_ref,
    feed_ref, n1_ref, r1_ref, mixed_ref, sems,
    *, layer, parts,
):
    j = pl.program_id(0)
    pairs = ((n1_ref, n1_out), (r1_ref, r1_out), (mixed_ref, mixed_out))
    copies = [pltpu.make_async_copy(a, b, sems.at[k]) for k, (a, b) in enumerate(pairs)]
    half = x0.shape[1]
    row = lambda ref, *at: ref[at[:-1] + (slice(at[-1], at[-1] + 1),)].astype(f32)

    rows = NORM_ROWS
    zero = jnp.zeros((8, x0.shape[2]), f32)

    def add_squares(sums, k, tile):
        for i, x in enumerate(sums):
            at = k + 2 * i + tile // 2
            squares_ref[at : at + 1, :] += col_sum(x)

    def squares_of(bias, result_ref, k):
        @pl.when(ids[1] == layer)
        def _():
            for t in range(3):

                def chunk(i, sums):
                    to = pl.ds(t * half + i * rows, rows)
                    valid = valid_ref[to, 0:1]
                    branch, result = feed_ref[to, :] + bias, result_ref[to, :].astype(f32)
                    return (sums[0] + fold(branch * branch * valid), sums[1] + fold(result * result * valid))

                add_squares(row_loop(half // rows, chunk, (zero, zero)), k, t)

    @pl.when(j == 0)
    def _():
        ctx = jnp.concatenate([own_ref[...].T, shared_ref[...].T], 0)
        feed_ref[...] = dot(ctx, w_out_ref[0])
        bias, gain, shift = row(out_bias_ref, layer), row(scale_ref, layer, 0), row(shift_ref, layer, 0)
        squares_ref[...] = jnp.zeros_like(squares_ref)
        for t, x_ref in enumerate((x0, x1, x2)):

            def chunk(i, sums):
                at = i * rows
                to = pl.ds(t * half + at, rows)
                attention = feed_ref[to, :] + bias
                normed, inverse = norm_parts(x_ref[0, pl.ds(at, rows), :].astype(f32) + attention)
                mixed = (normed * gain + shift).astype(bf16)
                n1_ref[to, :] = normed.astype(bf16)
                r1_ref[to, :] = jnp.broadcast_to(inverse, (rows, 128))
                mixed_ref[to, :] = mixed

            row_loop(half // rows, chunk, None)
        squares_of(bias, mixed_ref, 0)
        for copy in copies:
            copy.start()

    cols = in_ref.shape[2] // parts
    at = lambda k: slice(cols * k, cols * k + cols)
    bias = in_bias_ref[layer : layer + 1, :].astype(f32)
    pre = dot(mixed_ref[...], in_ref[0, :, at(0)]) + bias[:, at(0)]
    feed = None
    for k in range(parts):
        coming = None
        if k + 1 < parts:
            coming = dot(mixed_ref[...], in_ref[0, :, at(k + 1)]) + bias[:, at(k + 1)]
        act, slope = gelu_and_slope(pre)
        act = act.astype(bf16)
        act_ref[:, at(k)] = act
        slope_ref[:, at(k)] = slope.astype(bf16)
        part = dot(act, out_ref[0, at(k)])
        feed = part if feed is None else feed + part
        pre = coming

    @pl.when(j == 0)
    def _():
        feed_ref[...] = feed

    @pl.when(j > 0)
    def _():
        feed_ref[...] += feed

    @pl.when(j == pl.num_programs(0) - 1)
    def _():
        bias, gain, shift = row(ffn_bias_ref, layer), row(scale_ref, layer, 1), row(shift_ref, layer, 1)
        for t in range(3):

            def chunk(i, sums):
                to = pl.ds(t * half + i * rows, rows)
                branch = feed_ref[to, :] + bias
                normed, inverse = norm_parts(mixed_ref[to, :].astype(f32) + branch)
                out = normed * gain + shift
                n2_ref[to, :] = normed.astype(bf16)
                r2_ref[to, :] = jnp.broadcast_to(inverse, (rows, 128))
                h_ref[to, :] = out.astype(bf16)

            row_loop(half // rows, chunk, None)
        squares_of(bias, h_ref, 4)
        for copy in copies:
            copy.wait()


def feed_fwd(ids, x, gathered, ctx_own, ctx_shared, valid, weights, layer, chunk=768, parts=1):
    w_out, out_bias, ln_scale, ln_shift, ffn_in, ffn_in_bias, ffn_out, ffn_out_bias = weights
    half, width = x.shape[1], x.shape[2]
    tokens, ff = 3 * half, ffn_in.shape[2]
    full = lambda *shape: spec(shape, *([0] * len(shape)))
    dense = ((tokens, width), bf16)
    column = ((tokens, 128), f32)
    outs = [dense, column, dense, column, dense, ((tokens, ff), bf16), ((tokens, ff), bf16), dense,
            ((8, width), f32)]
    out_specs = [full(*s) for s, _ in outs]
    out_specs[5] = out_specs[6] = spec((tokens, chunk), 0, step)
    for k in (0, 1, 4):
        out_specs[k] = pl.BlockSpec(memory_space=pl.ANY)
    return call(
        functools.partial(feed_fwd_kernel, layer=layer, parts=parts), "feed_forward", (ff // chunk,), ids,
        row_tiles(half, width, gathered)
        + [
            full(*ctx_own.shape), full(*ctx_shared.shape), spec((tokens, 128), 0, 0),
            spec((1, width, width), layer, 0, 0), full(*out_bias.shape), full(*ln_scale.shape),
            full(*ln_shift.shape), spec((1, width, chunk), layer, 0, step),
            spec((ffn_in_bias.shape[0], chunk), 0, step), spec((1, chunk, width), layer, step, 0),
            full(*ffn_out_bias.shape),
        ],
        [x, x, x, ctx_own, ctx_shared, valid, w_out, out_bias, ln_scale, ln_shift, ffn_in, ffn_in_bias,
         ffn_out, ffn_out_bias],
        out_specs, [shape_of(s, d) for s, d in outs],
        [
            pltpu.VMEM((tokens, width), f32), pltpu.VMEM((tokens, width), bf16), pltpu.VMEM((tokens, 128), f32),
            pltpu.VMEM((tokens, width), bf16), pltpu.SemaphoreType.DMA((3,)),
        ],
    )


def slab_place(ids, slab):
    relative = jnp.bitwise_xor(ids[2], slab)
    return (
        jnp.bitwise_or(
            jnp.left_shift(jnp.bitwise_and(relative, 1), 2),
            jnp.bitwise_or(jnp.bitwise_and(relative, 2), jnp.right_shift(relative, 2)),
        )
    )


def store_piece(ids, keep_ref, send_ref, slab, core_rows, row, value):
    place = slab_place(ids, slab)
    core = ids[0]
    low, high = value[0:core_rows], value[core_rows:]
    at = slice(row, row + core_rows)

    @pl.when(core == 0)
    def _():
        keep_ref[place, at, :], send_ref[place, at, :] = low, high

    @pl.when(core != 0)
    def _():
        keep_ref[place, at, :], send_ref[place, at, :] = high, low


def feed_bwd_kernel(
    ids, g0, g1, g2, n2_ref, r2_ref, n1_ref, r1_ref, scale_ref, out_ref, slope_ref, in_ref, w_out_ref,
    act_ref, mixed_in_ref, own_ref, shared_ref,
    mixed_ref, attn_ref, ctx_ref, sums_ref, pre_sum_ref, keep_ref, send_ref,
    res_ref, acc_ref, feed_ref, pre_ref, feed_t, mixed_t, *late,
    layer, parts,
):
    j = pl.program_id(0)
    outs, late = (mixed_ref, attn_ref, ctx_ref), late[3:] + late[:3]
    mixed_ref, attn_ref, ctx_ref = late[-3:]
    buffers, sems = late[:-4], late[-4]
    sources = (n1_ref, r1_ref, w_out_ref.at[layer], own_ref, shared_ref)
    copies = [pltpu.make_async_copy(a, b, sems.at[k]) for k, (a, b) in enumerate(zip(sources, buffers))]
    n1_ref, r1_ref, w_out_ref, own_ref, shared_ref = buffers
    results = [
        pltpu.make_async_copy(a, b, sems.at[5 + k]) for k, (a, b) in enumerate(zip((mixed_ref, attn_ref, ctx_ref), outs))
    ]

    @pl.when(j == 0)
    def _():
        for copy in copies:
            copy.start()

    tokens = n2_ref.shape[0]
    gain = lambda k: scale_ref[layer, k : k + 1, :].astype(f32)
    rows = NORM_ROWS

    @pl.when(j == 0)
    def _():
        sums_ref[...] = jnp.zeros_like(sums_ref)
        for t, g_ref in enumerate((g0, g1, g2)):
            count = g_ref.shape[1]

            def chunk(i, sums):
                at = i * rows
                to = pl.ds(t * count + at, rows)
                grad = g_ref[0, pl.ds(at, rows), :].astype(f32)
                normed = n2_ref[to, :].astype(f32)
                back = norm_back(grad, gain(1), normed, r2_ref[to, 0:1])
                res_ref[to, :] = back
                feed = back.astype(bf16)
                feed_ref[to, :] = feed
                return (sums[0] + fold(grad * normed), sums[1] + fold(grad), sums[2] + fold(feed.astype(f32)))

            zero = jnp.zeros((8, n2_ref.shape[1]), f32)
            sums = row_loop(count // rows, chunk, (zero, zero, zero))
            for k, x in zip((1, 3, 5), sums):
                sums_ref[k : k + 1, :] += col_sum(x)
        for side in range(2):

            @pl.when(ids[1] == side)
            def _():
                feed_t[...] = feed_ref[:, LANES * side : LANES * side + LANES].T

        mixed_t[...] = mixed_in_ref[...].T

    cols = slope_ref.shape[1] // parts
    at = lambda k: slice(cols * k, cols * k + cols)
    g_act = dot_nt(feed_ref[...], out_ref[0, at(0)])
    for k in range(parts):
        coming = dot_nt(feed_ref[...], out_ref[0, at(k + 1)]) if k + 1 < parts else None
        g_pre = (g_act * slope_ref[:, at(k)].astype(f32)).astype(bf16)
        pre_ref[:, at(k)] = g_pre
        pre_sum_ref[:, at(k)] = jnp.broadcast_to(col_sum(g_pre.astype(f32)), (8, cols))
        g_act = coming
    total = dot_nt(pre_ref[...], in_ref[0])

    @pl.when(j == 0)
    def _():
        acc_ref[...] = total

    @pl.when(j > 0)
    def _():
        acc_ref[...] += total

    width = mixed_t.shape[0]

    @pl.when(j == pl.num_programs(0) - 1)
    def _():
        for copy in copies:
            copy.wait()

        def chunk(i, sums):
            to = pl.ds(i * rows, rows)
            g_mixed = acc_ref[to, :] + res_ref[to, :]
            mixed_ref[to, :] = g_mixed.astype(bf16)
            normed = n1_ref[to, :].astype(f32)
            attn = norm_back(g_mixed, gain(0), normed, r1_ref[to, 0:1]).astype(bf16)
            attn_ref[to, :] = attn
            return (sums[0] + fold(g_mixed * normed), sums[1] + fold(g_mixed), sums[2] + fold(attn.astype(f32)))

        zero = jnp.zeros((8, width), f32)
        sums = row_loop(tokens // rows, chunk, (zero, zero, zero))
        for k, x in zip((0, 2, 4), sums):
            sums_ref[k : k + 1, :] = col_sum(x)
        results[0].start()
        results[1].start()
        ctx_ref[...] = dot_nt(attn_ref[...], w_out_ref[...]).astype(bf16)
        results[2].start()

    high = LANES // 2
    slabs = act_ref.shape[1] // LANES
    result = dot(feed_t[...], act_ref[...]).astype(bf16)
    for k in range(slabs):
        store_piece(ids, keep_ref, send_ref, j * slabs + k, high, 0, result[:, LANES * k : LANES * k + LANES])
    slab_rows = width // SUPER
    half = slab_rows // 2
    steps = 4 // slabs
    for s in range(2 * steps):

        @pl.when((j == s) & (ids[1] == s // steps))
        def _():
            result = dot(mixed_t[...], pre_ref[...]).astype(bf16)
            for slab in range(SUPER):
                for k in range(slabs):
                    store_piece(
                        ids, keep_ref, send_ref, slab, half, high + ((s % steps) * slabs + k) * half,
                        result[slab_rows * slab : slab_rows * slab + slab_rows, LANES * k : LANES * k + LANES],
                    )

    @pl.when(j == pl.num_programs(0) - 1)
    def _():
        long = own_ref.shape[1]
        for side in range(2):

            @pl.when(ids[1] == side)
            def _():
                lanes = slice(LANES * side, LANES * side + LANES)
                result = dot(own_ref[...], attn_ref[0:long, lanes]) + dot(shared_ref[...], attn_ref[long:, lanes])
                result = result.astype(bf16)
                for slab in range(SUPER):
                    store_piece(ids, keep_ref, send_ref, slab, half, high + 4 * half,
                                result[slab_rows * slab : slab_rows * slab + slab_rows])
        for copy in results:
            copy.wait()


def feed_bwd(ids, grad, gathered, kept, slope, act, mixed, ctx_own, ctx_shared, weights, layer, chunk=768, parts=3):
    w_out, out_bias, ln_scale, ln_shift, ffn_in, ffn_in_bias, ffn_out, ffn_out_bias = weights
    n1, r1, n2, r2 = kept
    half, width = grad.shape[1], grad.shape[2]
    tokens, ff = 3 * half, ffn_in.shape[2]
    once = lambda *shape: pl.BlockSpec(shape, lambda i, ids: (0,) * len(shape), pipeline_mode=pl.Buffered(1))
    full = lambda *shape: spec(shape, *([0] * len(shape)))
    anywhere = pl.BlockSpec(memory_space=pl.ANY)
    dense = ((tokens, width), bf16)
    piece = ((SUPER, LANES + width // SUPER // 2, LANES), bf16)
    outs = [dense, dense, dense, ((8, width), f32), ((8, ff), f32), piece, piece]
    out_specs = [full(*s) for s, _ in outs]
    out_specs[4] = spec((8, chunk), 0, step)
    out_specs[0:3] = [anywhere] * 3
    return call(
        functools.partial(feed_bwd_kernel, layer=layer, parts=parts), "feed_backward", (ff // chunk,), ids,
        row_tiles(half, width, gathered)
        + [
            once(tokens, width), once(tokens, 128), anywhere, anywhere,
            full(*ln_scale.shape), spec((1, chunk, width), layer, step, 0), spec((tokens, chunk), 0, step),
            spec((1, width, chunk), layer, 0, step), anywhere,
            spec((tokens, chunk), 0, step), once(tokens, width), anywhere, anywhere,
        ],
        [grad, grad, grad, n2, r2, n1, r1, ln_scale, ffn_out, slope, ffn_in, w_out, act, mixed, ctx_own,
         ctx_shared],
        out_specs, [shape_of(s, d) for s, d in outs],
        [
            pltpu.VMEM((tokens, width), f32), pltpu.VMEM((tokens, width), f32),
            pltpu.VMEM((tokens, width), bf16), pltpu.VMEM((tokens, chunk), bf16),
            pltpu.VMEM((LANES, tokens), bf16), pltpu.VMEM((width, tokens), bf16),
            pltpu.VMEM((tokens, width), bf16), pltpu.VMEM((tokens, width), bf16), pltpu.VMEM((tokens, width), bf16),
            pltpu.VMEM((tokens, width), bf16), pltpu.VMEM((tokens, 128), f32),
            pltpu.VMEM((width, width), bf16), pltpu.VMEM(ctx_own.shape, bf16),
            pltpu.VMEM(ctx_shared.shape, bf16), pltpu.SemaphoreType.DMA((8,)),
        ],
    )


def joint_bwd_kernel(
    ids, x0, x1, x2, own_ref, shared_ref, arrived_ref, w_ref, attn_ref, rel0_ref, rel1_ref, vec_ref, pre_sum_ref,
    h_ref, keep_ref, send_ref, acc_ref, x_t, sums_ref, mine_ref, attn, sem,
    *, split,
):
    j = pl.program_id(0)
    copy = pltpu.make_async_copy(attn_ref, attn, sem)
    width = x_t.shape[0]
    rows = width // SUPER
    half = rows // 2

    @pl.when(j == 0)
    def _():
        copy.start()
        x_t[...] = jnp.concatenate([x0[0].T, x1[0].T, x2[0].T], 1)
        sums_ref[...] = jnp.zeros_like(sums_ref)

    far = arrived_ref[0].astype(f32) * (j > 0).astype(f32)
    near = (shared_ref[0].astype(f32) + far).astype(bf16)
    joint = jnp.concatenate([own_ref[0], near], 0)
    part = dot_nt(joint, w_ref[0])
    if split:
        mine_ref[...] = joint

    @pl.when(j == 0)
    def _():
        acc_ref[...] = part

    @pl.when(j > 0)
    def _():
        acc_ref[...] += part

    for side in range(2):
        lanes = slice(LANES * side, LANES * side + LANES)

        @pl.when(ids[1] == side)
        def _():
            if not split:
                mine_ref[...] = joint[:, lanes]
            sums_ref[j, :, lanes] = jnp.broadcast_to(col_sum(mine_ref[...].astype(f32)), (8, LANES))

    result = dot(x_t[...], mine_ref[...]).astype(bf16)
    for group in range(3):

        @pl.when(j == group)
        def _():
            for slab in range(SUPER):
                store_piece(ids, keep_ref, send_ref, slab, half, group * half,
                            result[rows * slab : rows * slab + rows])

    @pl.when(j == pl.num_programs(0) - 1)
    def _():
        copy.wait()
        flag = (ids[1] == 0).astype(f32) if split else 1.0
        h_ref[...] = (acc_ref[...] + attn[...].astype(f32) * flag).astype(bf16)
        rel = (rel0_ref[...] + rel1_ref[...]).astype(bf16)
        count = rel.shape[0] // SUPER
        lines = jnp.concatenate([vec_ref[0:6, :], sums_ref[0, 0:1], sums_ref[2, 0:1]], 0)
        blank = jnp.zeros((8, LANES - rows), f32)
        for slab in range(SUPER):
            narrow = jnp.concatenate([lines[:, rows * slab : rows * slab + rows], blank], 1)
            wide = pre_sum_ref[0:1, LANES * slab : LANES * slab + LANES]
            small = jnp.concatenate([narrow, wide, jnp.zeros((count - 9, LANES), f32)], 0).astype(bf16)
            both = jnp.concatenate([rel[count * slab : count * slab + count], small], 0)
            store_piece(ids, keep_ref, send_ref, slab, count, 3 * half, both)


def joint_bwd(ids, x, gathered, own, shared, arrived, w_qkv, g_attn, rel0, rel1, vec, pre_sum, layer, split):
    _, length, cols = own.shape
    width = g_attn.shape[1]
    half = shared.shape[1]
    tokens = length + half
    full = lambda *shape: spec(shape, *([0] * len(shape)))
    side = lambda i, ids: 0 if split else ids[1]
    piece = (SUPER, (width // SUPER // 2) * 3 + rel0.shape[0] // SUPER, LANES)
    return call(
        functools.partial(joint_bwd_kernel, split=split), "projections_backward", (3,), ids,
        row_tiles(half, width, gathered)
        + [
            spec((1, length, cols), step, 0, 0), spec((1, half, cols), step, 0, 0),
            spec((1, half, cols), lambda i, ids: jnp.maximum(i - 1, 0), 0, 0),
            spec((1, width, cols), layer, 0, lambda i, ids: 2 * i + ids[1] if split else i),
            pl.BlockSpec(memory_space=pl.ANY), spec((rel0.shape[0], LANES), 0, side), spec((rel0.shape[0], LANES), 0, side),
            full(*vec.shape), full(*pre_sum.shape),
        ],
        [x, x, x, own, shared, arrived, w_qkv, g_attn, rel0, rel1, vec, pre_sum],
        [full(tokens, width), full(*piece), full(*piece)],
        [shape_of((tokens, width), bf16), shape_of(piece, bf16), shape_of(piece, bf16)],
        [
            pltpu.VMEM((tokens, width), f32), pltpu.VMEM((width, tokens), bf16),
            pltpu.VMEM((3, 8, width), f32), pltpu.VMEM((tokens, LANES), bf16),
            pltpu.VMEM((tokens, width), bf16), pltpu.SemaphoreType.DMA(()),
        ],
    )


def place_rows_kernel(ids, own_ref, other_ref, out_ref):
    i = pl.program_id(0)
    core = ids[0]
    row = i // 2
    mine = jnp.where(row == 2, (i - 4) == core, row == core)

    @pl.when(mine)
    def _():
        out_ref[0] = own_ref[0].astype(out_ref.dtype)

    @pl.when(jnp.logical_not(mine))
    def _():
        out_ref[0] = other_ref[0].astype(out_ref.dtype)


def place_rows(ids, own, other, dtype):
    tokens, width = own.shape
    half = tokens // 3
    tile = lambda i, ids: jnp.where(i < 4, i % 2, 2)
    tiles = lambda x: x.reshape(3, half, width)
    return call(
        place_rows_kernel, "place_rows", (6,), ids,
        [spec((1, half, width), tile, 0, 0)] * 2, [tiles(own), tiles(other)],
        spec((1, half, width), step, 0, 0), shape_of((6, half, width), dtype),
    )


def collect(ids, refs, scratch):
    for core in range(2):
        for side in range(2):

            @pl.when((ids[0] == core) & (ids[1] == side))
            def _():
                scratch[core, side] = refs[0][...]
                scratch[core, 1 - side] = refs[1][...]
                scratch[1 - core, side] = refs[2][...]
                scratch[1 - core, 1 - side] = refs[3][...]


def spread_columns(scratch, out_ref, layer, at, groups, rows, inner=False):
    for core in range(2):
        for side in range(2):
            for g in range(groups):
                piece = scratch[core, side, at + g * rows : at + g * rows + rows, :]
                lane = ((g * 2 + side) if inner else (side * groups + g)) * LANES
                out_ref[layer, core * rows : core * rows + rows, lane : lane + LANES] = piece.astype(f32)


def unpack_feed_kernel(ids, *refs):
    inputs, (in_ref, out_ref, w_out_ref, scratch) = refs[:8], refs[8:]
    high = LANES // 2
    for layer in range(2):
        collect(ids, inputs[4 * layer : 4 * layer + 4], scratch)
        columns = [scratch[core, side, 0:high, :] for side in range(2) for core in range(2)]
        out_ref[layer] = jnp.concatenate(columns, 0).astype(f32).T
        rows = in_ref.shape[1] // 2
        spread_columns(scratch, in_ref, layer, high, 4, rows)
        spread_columns(scratch, w_out_ref, layer, high + 4 * rows, 1, rows)


def unpack_attention_kernel(ids, *refs):
    inputs = refs[:8]
    qkv_ref, rel_ref, qv_ref, out_bias_ref, scale_ref, shift_ref, in_bias_ref, ffn_bias_ref = refs[8:16]
    scratch = refs[16]
    rows = qkv_ref.shape[1] // 2
    wide = 2 * rows
    for layer in range(2):
        collect(ids, inputs[4 * layer : 4 * layer + 4], scratch)
        spread_columns(scratch, qkv_ref, layer, 0, 3, rows, True)
        at = 3 * rows
        count = rel_ref.shape[2]
        rel = jnp.concatenate([scratch[0, side, at : at + count, :] for side in range(2)], 1).astype(f32)
        size = rel_ref.shape[3]
        for head in range(rel_ref.shape[1]):
            rel_ref[layer, head] = rel[:, size * head : size * head + size]
        small = scratch[1, 0, at : at + count, :].astype(f32)
        scale_ref[layer] = small[0:2, 0:wide]
        shift_ref[layer] = small[2:4, 0:wide]
        out_bias_ref[layer : layer + 1] = small[4:5, 0:wide]
        ffn_bias_ref[layer : layer + 1] = small[5:6, 0:wide]
        other = scratch[1, 1, at : at + count, :].astype(f32)
        qv_ref[layer] = small[6:8, 0:wide] + other[6:8, 0:wide]
        in_bias_ref[layer : layer + 1] = small[8:9]


def unpack(kernel, name, ids, pieces, shapes):
    full = lambda *shape: spec(shape, *([0] * len(shape)))
    return call(
        kernel, name, (1,), ids, [full(*p.shape) for p in pieces], pieces,
        [full(*s) for s in shapes], [shape_of(s, f32) for s in shapes],
        [pltpu.VMEM((2, 2) + pieces[0].shape, bf16)],
    )


def body(
    stream, cotangent, segments, word_boxes, valid_mask, w_qkv, qv_bias, w_out, out_bias, rel_proj,
    ln_scale, ln_shift, ffn_in, ffn_in_bias, ffn_out, ffn_out_bias,
):
    sections = lax.axis_size("section")
    dp = lax.axis_size("dp")
    section = lax.axis_index("section")
    dp_index = lax.axis_index("dp")
    core, side = section % 2, section // 2
    rows, length, width = stream.shape
    layers = w_qkv.shape[0]
    ff = ffn_in.shape[2]
    half = length // 2
    assert rows == 3 and sections == 4 and layers == 2 and dp % SUPER == 0 and width == 2 * LANES
    fine = dp // SUPER
    ids = jnp.stack([core, side, dp_index // fine]).astype(jnp.int32)
    weights = (w_out, out_bias, ln_scale, ln_shift, ffn_in, ffn_in_bias, ffn_out, ffn_out_bias)
    rel_pairs = rel_proj.reshape(layers, width // 128, 128, 128)

    def flip(x, bit):
        return lax.ppermute(x, "section", [(i, i ^ bit) for i in range(sections)])

    def flip_dp(x, bit):
        return lax.ppermute(x, "dp", [(i, i ^ bit) for i in range(dp)])

    tables = make_tables(ids, jnp.swapaxes(word_boxes, 0, 1), segments, valid_mask)
    ctab, stab, valid_col = tables[3], tables[4], tables[7]

    halves = lambda x: x.reshape(-1, half, width)
    x, gathered = halves(stream), True
    kept = []
    for l in range(layers):
        joint, turned, kv = project(ids, x, gathered, w_qkv, qv_bias, rel_pairs, ctab, stab, l)
        kv_far = flip(kv, 1)
        ctx_own, lse_own = attention_fwd(ids, False, tables, joint, turned, None)
        ctx_shared, lse_shared = attention_fwd(ids, True, tables, joint, turned, kv_far)
        n1, r1, n2, r2, mixed, act, slope, out, squares = feed_fwd(
            ids, x, gathered, ctx_own, ctx_shared, valid_col, weights, l
        )
        kept.append(
            dict(x=x, gathered=gathered, joint=joint, turned=turned, kv_far=kv_far, ctx_own=ctx_own,
                 ctx_shared=ctx_shared, lse_own=lse_own, lse_shared=lse_shared, norms=(n1, r1, n2, r2),
                 mixed=mixed, act=act, slope=slope, out=out, squares=squares)
        )
        x, gathered = halves(out), False

    clock = [ids]

    def pin(state):
        clock[0], state = lax.optimization_barrier((clock[0], state))
        return state

    def absorb(keep, arrived):
        keep, arrived = pin((keep, arrived))
        n = keep.shape[0] // 2
        return pin((keep[:n] + arrived[:n], keep[n:] + arrived[n:]))

    def last(keep, arrived):
        keep, arrived = pin((keep, arrived))
        x = (keep + arrived)[0]
        bit = 1
        while bit < fine:
            x = x + flip_dp(x, bit)
            bit *= 2
        return pin(x)

    def hop(state, bit):
        return state[0], flip_dp(state[1], fine << bit)

    def all_sides(x):
        far = flip(x, 2)
        return [x, far, flip(x, 1), flip(far, 1)]

    def feed_back(l, grad, gathered):
        k = kept[l]
        g_mixed, g_attn, g_ctx, vec, pre_sum, keep, send = feed_bwd(
            clock[0], grad, gathered, k["norms"], k["slope"], k["act"], k["mixed"], k["ctx_own"],
            k["ctx_shared"], weights, l,
        )
        k["g_mixed"] = g_mixed
        return g_attn, g_ctx, vec, pre_sum, (keep, flip(send, 1))

    def attention_back(l, shared, g_ctx):
        k = kept[l]
        return attention_bwd(
            clock[0], shared, tables, k["joint"], k["turned"], k["kv_far"] if shared else None,
            k["lse_shared" if shared else "lse_own"], g_ctx, rel_pairs, l, l == 0,
        )

    def joint_back(l, own_grads, shared_keep, arrived, g_attn, rel_own, rel_shared, vec, pre_sum):
        k = kept[l]
        g_h, keep, send = joint_bwd(
            clock[0], k["x"], k["gathered"], own_grads, shared_keep, arrived, w_qkv, g_attn, rel_own,
            rel_shared, vec, pre_sum, l, l == 0,
        )
        k["g_h"] = g_h
        return g_h, (keep, flip(send, 1))

    g_attn, g_ctx, vec, pre_sum, f1 = feed_back(1, halves(cotangent), True)
    shared_keep, shared_send, rel_shared = attention_back(1, True, g_ctx)
    arrived = flip(shared_send, 1)
    f1 = hop(absorb(*f1), 0)
    own_grads, rel_own = attention_back(1, False, g_ctx)
    g_h, a1 = joint_back(1, own_grads, shared_keep, arrived, g_attn, rel_own, rel_shared, vec, pre_sum)

    f1 = hop(absorb(*f1), 1)
    a1 = hop(absorb(*a1), 0)
    g_attn, g_ctx, vec, pre_sum, f0 = feed_back(0, halves(g_h), False)
    f1 = hop(absorb(*f1), 2)
    a1 = hop(absorb(*a1), 1)
    shared_keep, shared_send, rel_shared = attention_back(0, True, g_ctx)
    arrived = flip(shared_send, 1)
    f0 = hop(absorb(*f0), 0)
    own_grads, rel_own = attention_back(0, False, g_ctx)
    f1 = last(*f1)
    a1 = hop(absorb(*a1), 2)
    g_h, a0 = joint_back(0, own_grads, shared_keep, arrived, g_attn, rel_own, rel_shared, vec, pre_sum)
    g_h_far = flip(g_h, 2)
    f1 = all_sides(f1)
    f0 = hop(absorb(*f0), 1)
    a0 = hop(absorb(*a0), 0)
    a1 = all_sides(last(*a1))

    def of_layer(name):
        return jnp.where(side == 0, kept[0][name], kept[1][name])

    def to_section(first, second, dtype):
        a, b = of_layer(first), of_layer(second)
        own, away = jnp.where(core == 0, a, b), jnp.where(core == 0, b, a)
        return place_rows(ids, own, flip(away, 1), dtype).reshape(1, rows, length, width)

    section_outs = pin(to_section("mixed", "out", bf16))
    a0 = hop(absorb(*a0), 1)
    f0 = hop(absorb(*f0), 2)
    kept[0]["g_h"] = pin(g_h + g_h_far)
    in_grads = pin(to_section("g_h", "g_mixed", f32))
    a0 = hop(absorb(*a0), 2)
    f0 = all_sides(last(*f0))
    a0 = all_sides(last(*a0))

    squares_mine = jnp.sum(of_layer("squares"), 1).reshape(2, 2, 2)
    squares_far = flip(squares_mine, 1)
    sub = lambda v: lax.dynamic_index_in_dim(v, core, 0, keepdims=False)
    near, far = sub(squares_mine), sub(squares_far)
    first = jnp.where(core == 0, near[:, 0], far[:, 0])
    second = jnp.where(core == 0, far[:, 0], near[:, 0])
    square_rows = jnp.stack([first, second, near[:, 1] + far[:, 1]])
    row_counts = jnp.sum(valid_mask.astype(f32), 1)
    root_mean_squares = jnp.sqrt(square_rows / (width * jnp.maximum(row_counts, 1.0))[:, None])[None]

    slab = width // SUPER
    d_ffn_in, d_ffn_out, d_out = unpack(
        unpack_feed_kernel, "unpack_feed", clock[0], f0 + f1,
        [(2, slab, ff), (2, ff // SUPER, width), (2, slab, width)],
    )
    d_ffn_in, d_ffn_out, d_out = pin((d_ffn_in, d_ffn_out, d_out))
    rel_rows = 128 // SUPER
    d_qkv, d_rel, d_qv, d_out_bias, d_scale, d_shift, d_in_bias, d_ffn_bias = unpack(
        unpack_attention_kernel, "unpack_attention", clock[0], a0 + a1,
        [(2, slab, 3 * width), (2, rel_proj.shape[1], rel_rows, rel_proj.shape[2]), (2, 2, slab), (2, slab),
         (2, 2, slab), (2, 2, slab), (2, LANES), (2, slab)],
    )

    def own_part(x, axis):
        n = x.shape[axis] // fine
        return x if fine == 1 else lax.dynamic_slice_in_dim(x, (dp_index % fine) * n, n, axis)

    return (
        section_outs,
        in_grads,
        own_part(d_qkv, 1),
        own_part(d_qv, 2),
        own_part(d_out, 1),
        own_part(d_out_bias, 1),
        own_part(jnp.swapaxes(d_rel, 2, 3), 3),
        own_part(d_scale, 2),
        own_part(d_shift, 2),
        own_part(d_ffn_in, 1),
        own_part(d_in_bias, 1),
        own_part(d_ffn_out, 1),
        own_part(d_ffn_bias, 1),
        root_mean_squares,
    )


def solution(mesh):
    return jax.shard_map(
        body,
        mesh=mesh,
        in_specs=(
            P("dp", None, None),
            P("dp", None, None),
            P("dp", None),
            P(None, "dp", None),
            P("dp", None),
        )
        + (P(),) * 11,
        out_specs=(
            P("section", "dp", None, None),
            P("section", "dp", None, None),
            P(None, "dp", None),
            P(None, None, "dp"),
            P(None, "dp", None),
            P(None, "dp"),
            P(None, None, None, "dp"),
            P(None, None, "dp"),
            P(None, None, "dp"),
            P(None, "dp", None),
            P(None, "dp"),
            P(None, "dp", None),
            P(None, "dp"),
            P("section", "dp", None),
        ),
        check_vma=False,
    )
```
